256 devices in a mesh: member: 16 (over y, z_lo), space: 16 (over x, z_hi, core).
Axes of the slice: x: 4, y: 4, z: 8 (z_hi: 2, z_lo: 4; z = z_hi * 4 + z_lo), core: 2. Of those that a mesh axis runs over, the one named last changes fastest.
Arguments:
- background: bfloat16 [64, 4, 6, 16, 8192], P('member', None, None, 'space'), may hold values from -6 to 6
- obs_values: float32 [16, 8, 128], P('space'), may hold values from -6 to 6
- obs_precision: float32 [16, 8, 128], P('space'), may hold values from 0.25 to 4
- obs_cell: int32 [16, 8, 128], P('space'), may hold values from 0 to 24575
- obs_count: int32 [16, 8], P('space'), may hold values from 32 to 128, as said below
- radius: int32 [16, 8], P('space'), may hold values from 32 to 64
Outputs:
- analysis: bfloat16 [64, 4, 6, 16, 8192], P('member', None, None, 'space')
The draws below stay inside these ranges and needn't reach their ends.
Inputs may be any that keep to these rules, and one draw needn't show every extreme that they name: `obs_count`: slots at or past a tile's count are unused; in every draw some tile uses all 128 slots.
All inputs are finite; a program needn't handle non-finite values.
Results may differ from the reference program's by a relative error of at most 0.0049.
Values may be sent and summed in bfloat16 or wider, within the bound.
No kernel may reach another device: no remote copies, remote signals or barrier semaphores. Data moves between devices by JAX's collectives and lax.ppermute only.
A program may use at most 192 MiB of HBM per device.

```python
import math
import jax
import jax.numpy as jnp
from jax import lax

MEMBERS = 64
FIELDS = 6
LEVELS = 4
TILE_SIDE = 32
TILE_CELLS = 1024
TILE_COLS = 8
TILE_ROWS = 16
OBS_SLOTS = 128
SWEEPS = 6


def draw_obs_count(key, part):
    key = jax.random.fold_in(key, 7)
    first_key, second_key = jax.random.split(key)
    counts = jax.random.randint(first_key, (TILE_ROWS * TILE_COLS,), OBS_SLOTS // 4, OBS_SLOTS + 1)
    chosen = jax.random.randint(second_key, (), 0, TILE_ROWS * TILE_COLS)
    counts = counts.at[chosen].set(OBS_SLOTS)
    return counts.reshape(TILE_ROWS, TILE_COLS).astype(jnp.int32)


def place_ends(drawn, stream_key, least, top_value):
    index_at = [jax.random.randint(jax.random.fold_in(stream_key, axis), (), 0, length) for axis, length in enumerate(drawn.shape)]
    main_axis = drawn.shape.index(max(drawn.shape))
    beside = index_at[:main_axis] + [(index_at[main_axis] + 1) % drawn.shape[main_axis]] + index_at[main_axis + 1:]
    return drawn.at[tuple(index_at)].set(least).at[tuple(beside)].set(top_value)


def level_of(stream_key, dims, cuts, least, high):
    loudness = 1.0
    for dim, shards_of in cuts:
        draws = jax.random.uniform(jax.random.fold_in(jax.random.fold_in(stream_key, 6), dim), (shards_of,), jnp.float32, least / len(cuts), high / len(cuts))
        loudness = loudness * jnp.repeat(jnp.exp(draws), dims[dim] // shards_of).reshape((-1,) + (1,) * (len(dims) - 1 - dim))
    return loudness


def bell_draw(key, extent, width, limit, cuts=(), held_as=jnp.bfloat16):
    result = width * jax.random.normal(key, extent, jnp.float32)
    if cuts:
        result = result * level_of(key, extent, cuts, -0.22, 0.18)
    return jnp.clip(result, -limit, limit).astype(held_as)


def setup_inputs(seed: int = 0) -> dict:
    keys = jax.random.split(jax.random.key(seed), 7)
    return {
        "background": bell_draw(keys[0], (MEMBERS, LEVELS, FIELDS, TILE_ROWS, TILE_COLS * TILE_CELLS), 1.0, 6.0, ((0, 16), (3, 16))),
        "obs_values": bell_draw(keys[1], (TILE_ROWS, TILE_COLS, OBS_SLOTS), 1.0, 6.0, ((0, 16),), jnp.float32),
        "obs_precision": jnp.clip(jnp.exp(math.log(4.0) - 2.7725887 * jax.random.uniform(keys[2], (TILE_ROWS, TILE_COLS, OBS_SLOTS), jnp.float32) ** level_of(keys[2], (TILE_ROWS, TILE_COLS, OBS_SLOTS), ((0, 16),), -0.2, 0.2)), 0.25, 4.0),
        "obs_cell": place_ends(jax.random.randint(keys[3], (TILE_ROWS, TILE_COLS, OBS_SLOTS), 0, LEVELS * FIELDS * TILE_CELLS), jax.random.fold_in(keys[3], 1), 0, (LEVELS * FIELDS * TILE_CELLS) - 1).astype(jnp.int32),
        "obs_count": draw_obs_count(jax.random.fold_in(keys[6], 71), 0),
        "radius": place_ends(jax.random.randint(keys[5], (TILE_ROWS, TILE_COLS), TILE_SIDE, 2 * TILE_SIDE + 1), jax.random.fold_in(keys[5], 1), TILE_SIDE, 2 * TILE_SIDE).astype(jnp.int32),
    }


exact_mode = lax.Precision.HIGHEST

def observe(fields, obs_cell, cell_count):
    members = fields.shape[0]
    row_count = fields.shape[3]
    row_width = fields.shape[4]
    level_field = obs_cell // cell_count
    in_tile = obs_cell % cell_count
    row_index = jnp.arange(row_count, dtype=jnp.int32)[:, None, None]
    col_index = jnp.arange(row_width // cell_count, dtype=jnp.int32)[None, :, None]
    flat_index = (level_field * row_count + row_index) * row_width + col_index * cell_count + in_tile
    gathered = jnp.take(fields.reshape(members, -1), flat_index.reshape(-1).astype(jnp.int32), axis=1)
    return gathered.reshape(members, row_count, row_width // cell_count, -1)

def observation_rows(obs_values, obs_precision, obs_cell, obs_count, cell_count, tile_side):
    slot_count = obs_cell.shape[-1]
    slot_index = jnp.arange(slot_count, dtype=jnp.int32)
    active = jnp.where(slot_index[None, None, :] < obs_count[:, :, None], obs_precision, jnp.zeros_like(obs_precision))
    in_tile = obs_cell % cell_count
    row_place = (in_tile // tile_side).astype(obs_values.dtype)
    col_place = (in_tile % tile_side).astype(obs_values.dtype)
    return jnp.stack([obs_values, active, row_place, col_place])

def neighbourhood(obs_rows, tile_side):
    row_count = obs_rows.shape[1] - 2
    col_count = obs_rows.shape[2]
    slot_count = obs_rows.shape[3]
    padded = jnp.pad(obs_rows, ((0, 0), (0, 0), (1, 1), (0, 0)))
    pieces = []
    shift_rows = []
    shift_cols = []
    for row_step in range(3):
        for col_step in range(3):
            pieces.append(padded[:, row_step:row_step + row_count, col_step:col_step + col_count, :])
            shift_rows.append(jnp.full((slot_count,), (row_step - 1) * tile_side, obs_rows.dtype))
            shift_cols.append(jnp.full((slot_count,), (col_step - 1) * tile_side, obs_rows.dtype))
    stacked = jnp.concatenate(pieces, axis=3)
    offset_row = jnp.concatenate(shift_rows)
    offset_col = jnp.concatenate(shift_cols)
    return (stacked, offset_row, offset_col)

def solve_tiles(stacked, offset_row, offset_col, radius, members, tile_side, sweeps):
    ensemble = stacked[:members]
    values = stacked[members]
    active = stacked[members + 1]
    centre = 0.5 * tile_side - 0.5
    dist_row = offset_row + stacked[members + 2] - centre
    dist_col = offset_col + stacked[members + 3] - centre
    reach_cells = radius.astype(stacked.dtype)[:, :, None]
    tapered = jnp.maximum(1.0 - (dist_row * dist_row + dist_col * dist_col) / (reach_cells * reach_cells), 0.0) ** 2
    weight = active * tapered
    mean_obs = lax.optimization_barrier(jnp.mean(ensemble, axis=0))
    anomaly = ensemble - mean_obs
    scaled = anomaly * weight
    innovation = values - mean_obs
    identity = jnp.eye(members, dtype=stacked.dtype)
    system = (members - 1.0) * identity + jnp.einsum('krtm,jrtm->rtkj', scaled, anomaly, precision=exact_mode)
    forcing = jnp.einsum('krtm,rtm->rtk', scaled, innovation, precision=exact_mode)
    scale = jnp.trace(system, axis1=2, axis2=3)[:, :, None, None]
    root_part = system / scale
    inverse = jnp.broadcast_to(identity, system.shape)
    for sweep_index in range(sweeps):
        factor = 0.5 * (3.0 * identity - jnp.einsum('rtij,rtjk->rtik', inverse, root_part, precision=exact_mode))
        root_part = jnp.einsum('rtij,rtjk->rtik', root_part, factor, precision=exact_mode)
        inverse = jnp.einsum('rtij,rtjk->rtik', factor, inverse, precision=exact_mode)
    inv_sqrt = inverse / jnp.sqrt(scale)
    covariance = jnp.einsum('rtij,rtjk->rtik', inv_sqrt, inv_sqrt, precision=exact_mode)
    mean_weight = jnp.einsum('rtkj,rtj->rtk', covariance, forcing, precision=exact_mode)
    total = jnp.sqrt(members - 1.0) * inv_sqrt + mean_weight[:, :, :, None]
    mixing = total - lax.optimization_barrier(jnp.mean(total, axis=2, keepdims=True)) + 1.0 / members
    return mixing.astype(jnp.bfloat16)

def reference(background, obs_values, obs_precision, obs_cell, obs_count, radius):
    members = background.shape[0]
    predicted = observe(background, obs_cell, TILE_CELLS)
    extra = observation_rows(obs_values, obs_precision, obs_cell, obs_count, TILE_CELLS, TILE_SIDE)
    obs_rows = jnp.concatenate([predicted.astype(jnp.float32), extra], axis=0)
    obs_rows = jnp.pad(obs_rows, ((0, 0), (1, 1), (0, 0), (0, 0)))
    stacked, offset_row, offset_col = neighbourhood(obs_rows, TILE_SIDE)
    mixing = solve_tiles(stacked, offset_row, offset_col, radius, members, TILE_SIDE, SWEEPS)

    def one_row(row_number):
        row_fields = lax.dynamic_index_in_dim(background, row_number, 3, keepdims=False)
        row_fields = row_fields.reshape(members, LEVELS, FIELDS, TILE_COLS, TILE_CELLS)
        row_mixing = lax.dynamic_index_in_dim(mixing, row_number, 0, keepdims=False)
        mixed_row = jnp.einsum('jlftc,tjk->klftc', row_fields.astype(jnp.float32), row_mixing.astype(jnp.float32))
        return mixed_row.astype(jnp.bfloat16).reshape(members, LEVELS, FIELDS, TILE_COLS * TILE_CELLS)
    analysed_rows = lax.map(one_row, jnp.arange(TILE_ROWS, dtype=jnp.int32))
    return jnp.moveaxis(analysed_rows, 0, 3)
```

```python
import functools

import jax
import jax.numpy as jnp
from jax import lax
from jax.experimental import pallas as pl
from jax.experimental.pallas import tpu as pltpu
from jax.sharding import PartitionSpec as P

TILE_SIDE = 32
TILE_CELLS = 1024
SWEEPS = 6
EXACT = lax.Precision.HIGHEST


def split_kernel(parts, width, x_ref, out_ref, sems):
    copies = [
        pltpu.make_async_copy(
            x_ref.at[:, :, :, pl.ds(d * width, width)], out_ref.at[d], sems.at[d]
        )
        for d in range(parts)
    ]
    for copy in copies:
        copy.start()
    for copy in copies:
        copy.wait()


def join_kernel(parts, width, x_ref, out_ref, sems):
    copies = [
        pltpu.make_async_copy(
            x_ref.at[d], out_ref.at[:, :, :, pl.ds(d * width, width)], sems.at[d]
        )
        for d in range(parts)
    ]
    for copy in copies:
        copy.start()
    for copy in copies:
        copy.wait()


def observe_kernel(x_ref, cell_ref, out_ref):
    own, fields, levels, cells = x_ref.shape
    slots = out_ref.shape[-1]
    tile = pl.program_id(0)
    cell = cell_ref[pl.ds(tile, 1), :]
    in_tile = cell % cells
    level_field = cell // cells
    wanted = (level_field % fields) * levels + level_field // fields
    onehot = lax.broadcasted_iota(jnp.int32, (cells, slots), 0) == in_tile
    rows = x_ref[...].reshape(own * fields * levels, cells)
    found = jnp.dot(rows, onehot.astype(rows.dtype), preferred_element_type=jnp.float32)
    found = found.reshape(own, fields * levels, slots)
    match = lax.broadcasted_iota(jnp.int32, (fields * levels, slots), 0) == wanted
    picked = jnp.sum(jnp.where(match[None], found, 0.0), axis=1)
    out_ref[...] = picked.astype(out_ref.dtype)[None]


def solve_kernel(levels, where_ref, radius_ref, pred_ref, above_ref, own_ref, below_ref, out_ref):
    tile = where_ref[0]
    tiles = own_ref.shape[1]
    sources, _, own, slots = pred_ref.shape
    members = sources * own
    reach = radius_ref[0, tile].astype(jnp.float32)
    centre = 0.5 * TILE_SIDE - 0.5
    ensemble, values, weights = [], [], []
    for a, rows_ref in enumerate((above_ref, own_ref, below_ref)):
        for b in range(3):
            place = tile + b - 1
            inside = jnp.logical_and(place >= 0, place < tiles)
            held = jnp.clip(place, 0, tiles - 1)
            value, active, row, col = (rows_ref[i, pl.ds(held, 1), :] for i in range(4))
            dist_row = row + ((a - 1) * TILE_SIDE - centre)
            dist_col = col + ((b - 1) * TILE_SIDE - centre)
            taper = jnp.maximum(
                1.0 - (dist_row * dist_row + dist_col * dist_col) / (reach * reach), 0.0
            )
            weights.append(jnp.where(inside, active, 0.0) * (taper * taper))
            values.append(value)
            ensemble.append(
                pred_ref[:, a * 3 + b].astype(jnp.float32).reshape(members, slots)
            )
    ensemble = jnp.concatenate(ensemble, axis=1)
    values = jnp.concatenate(values, axis=1)
    weight = jnp.concatenate(weights, axis=1)
    mean_obs = jnp.mean(ensemble, axis=0, keepdims=True)
    anomaly = ensemble - mean_obs
    innovation = values - mean_obs
    scaled = anomaly * weight
    extended = jnp.concatenate(
        [anomaly, jnp.broadcast_to(innovation, (8, innovation.shape[1]))], axis=0
    )
    product = lax.dot_general(
        extended, scaled, (((1,), (1,)), ((), ())), precision=EXACT,
        preferred_element_type=jnp.float32,
    )
    forcing = product[members : members + 1]
    row_id = lax.broadcasted_iota(jnp.int32, (members, members), 0)
    col_id = lax.broadcasted_iota(jnp.int32, (members, members), 1)
    identity = (row_id == col_id).astype(jnp.float32)
    system = (members - 1.0) * identity + product[:members]
    scale = jnp.sum(
        jnp.sum(system * identity, axis=1, keepdims=True), axis=0, keepdims=True
    )
    root_part = system / scale
    inverse = identity
    mul = functools.partial(jnp.dot, precision=EXACT, preferred_element_type=jnp.float32)
    for sweep in range(SWEEPS):
        factor = 1.5 * identity - 0.5 * (root_part if sweep == 0 else mul(inverse, root_part))
        if sweep < SWEEPS - 1:
            root_part = mul(root_part, factor)
        inverse = factor if sweep == 0 else mul(factor, inverse)
    inv_sqrt = inverse / jnp.sqrt(scale)
    half = jnp.sum(inv_sqrt * forcing, axis=1, keepdims=True)
    mean_weight = jnp.sum(inv_sqrt * half, axis=0, keepdims=True)
    total = jnp.sqrt(jnp.float32(members - 1)) * inv_sqrt + mean_weight
    mixing = total - jnp.mean(total, axis=1, keepdims=True) + 1.0 / members
    mixing = mixing.astype(jnp.bfloat16)
    wide = members * levels
    spread = (
        lax.broadcasted_iota(jnp.int32, (wide, members), 0) // levels
        == lax.broadcasted_iota(jnp.int32, (wide, members), 1)
    ).astype(jnp.bfloat16)
    tall = jnp.dot(spread, mixing, preferred_element_type=jnp.float32).astype(jnp.bfloat16)
    full = lax.dot_general(
        tall, spread, (((1,), (1,)), ((), ())), preferred_element_type=jnp.float32
    )
    same = (
        lax.broadcasted_iota(jnp.int32, (wide, wide), 0) % levels
        == lax.broadcasted_iota(jnp.int32, (wide, wide), 1) % levels
    )
    out_ref[...] = jnp.where(same, full, 0.0).astype(out_ref.dtype)


def apply_kernel(mix_ref, x_ref, out_ref):
    sources, own, _, levels, width = x_ref.shape
    rows = x_ref[...].reshape(sources * own * levels, width)
    mixed = jnp.dot(mix_ref[...], rows, preferred_element_type=jnp.float32)
    out_ref[...] = mixed.astype(out_ref.dtype).reshape(out_ref.shape)


def observe(fields, cells):
    own, count, levels, width = fields.shape
    tiles, slots = cells.shape
    return pl.pallas_call(
        observe_kernel,
        grid=(tiles,),
        in_specs=[
            pl.BlockSpec((own, count, levels, TILE_CELLS), lambda t: (0, 0, 0, t)),
            pl.BlockSpec((tiles, slots), lambda t: (0, 0)),
        ],
        out_specs=pl.BlockSpec((1, own, slots), lambda t: (t, 0, 0)),
        out_shape=jax.ShapeDtypeStruct((tiles, own, slots), fields.dtype),
        name="observe",
    )(fields, cells)


def split(fields, parts):
    own, count, levels, width = fields.shape
    part = width // parts
    return pl.pallas_call(
        functools.partial(split_kernel, parts, part),
        in_specs=[pl.BlockSpec(memory_space=pl.ANY)],
        out_specs=pl.BlockSpec(memory_space=pl.ANY),
        out_shape=jax.ShapeDtypeStruct((parts, own, count, levels, part), fields.dtype),
        scratch_shapes=[pltpu.SemaphoreType.DMA((parts,))],
        name="split",
    )(fields)


def join(pieces):
    parts, own, count, levels, part = pieces.shape
    return pl.pallas_call(
        functools.partial(join_kernel, parts, part),
        in_specs=[pl.BlockSpec(memory_space=pl.ANY)],
        out_specs=pl.BlockSpec(memory_space=pl.ANY),
        out_shape=jax.ShapeDtypeStruct((own, count, levels, parts * part), pieces.dtype),
        scratch_shapes=[pltpu.SemaphoreType.DMA((parts,))],
        name="join",
    )(pieces)


def solve(tile, radius, pred, above, own, below, levels):
    members = pred.shape[0] * pred.shape[2]
    wide = members * levels
    vmem = pl.BlockSpec(memory_space=pltpu.VMEM)
    smem = pl.BlockSpec(memory_space=pltpu.SMEM)
    return pl.pallas_call(
        functools.partial(solve_kernel, levels),
        in_specs=[smem, smem, vmem, vmem, vmem, vmem],
        out_specs=vmem,
        out_shape=jax.ShapeDtypeStruct((wide, wide), jnp.bfloat16),
        name="solve",
    )(tile, radius, pred, above, own, below)


def apply_mixing(mix, pieces):
    parts, own, count, levels, part = pieces.shape
    block = pl.BlockSpec((parts, own, 1, levels, part), lambda f: (0, 0, f, 0, 0))
    return pl.pallas_call(
        apply_kernel,
        grid=(count,),
        in_specs=[pl.BlockSpec(mix.shape, lambda f: (0, 0)), block],
        out_specs=block,
        out_shape=jax.ShapeDtypeStruct(pieces.shape, pieces.dtype),
        name="apply",
    )(mix, pieces)


def observation_rows(obs_values, obs_precision, obs_cell, obs_count):
    slot_index = jnp.arange(obs_cell.shape[-1], dtype=jnp.int32)
    active = jnp.where(slot_index[None, :] < obs_count[:, None], obs_precision, 0.0)
    in_tile = obs_cell % TILE_CELLS
    row_place = (in_tile // TILE_SIDE).astype(jnp.float32)
    col_place = (in_tile % TILE_SIDE).astype(jnp.float32)
    return jnp.stack([obs_values, active, row_place, col_place])


def on_device(background, obs_values, obs_precision, obs_cell, obs_count, radius):
    own, levels, count, _, width = background.shape
    parts = lax.axis_size("member")
    rows = lax.axis_size("space")
    tiles = width // TILE_CELLS
    down = [(i, i + 1) for i in range(rows - 1)]
    up = [(i + 1, i) for i in range(rows - 1)]
    fields = background.transpose(0, 2, 3, 1, 4).reshape(own, count, levels, width)
    sent = lax.all_to_all(split(fields, parts), "member", 0, 0)

    extra = observation_rows(obs_values[0], obs_precision[0], obs_cell[0], obs_count[0])
    extra_above = lax.ppermute(extra, "space", down)
    extra_below = lax.ppermute(extra, "space", up)
    pred = observe(fields, obs_cell[0])
    around = jnp.stack(
        [lax.ppermute(pred, "space", down), pred, lax.ppermute(pred, "space", up)]
    )
    padded = jnp.pad(around, ((0, 0), (1, 1), (0, 0), (0, 0)))
    near = jnp.stack([padded[:, b : b + tiles] for b in range(3)], axis=1)
    near = near.reshape((9,) + pred.shape).transpose(1, 0, 2, 3)
    share = parts // tiles
    near = jnp.repeat(near, share, axis=0)
    near = lax.all_to_all(near, "member", 0, 0)
    tile = (lax.axis_index("member") // share).astype(jnp.int32).reshape(1)
    mix = solve(tile, radius, near, extra_above, extra, extra_below, levels)

    mixed = apply_mixing(mix, sent)
    back = lax.all_to_all(mixed, "member", 0, 0)
    out = join(back)
    return out.reshape(own, count, 1, levels, width).transpose(0, 3, 1, 2, 4)


def solution(mesh):
    return jax.shard_map(
        on_device,
        mesh=mesh,
        in_specs=(
            P("member", None, None, "space", None),
            P("space", None, None),
            P("space", None, None),
            P("space", None, None),
            P("space", None),
            P("space", None),
        ),
        out_specs=P("member", None, None, "space", None),
        check_vma=False,
    )
```

```python
import functools

import jax
import jax.numpy as jnp
from jax import lax
from jax.experimental import pallas as pl
from jax.experimental.pallas import tpu as pltpu
from jax.sharding import PartitionSpec as P

TILE_SIDE = 32
TILE_CELLS = 1024
SWEEPS = 6
EXACT = lax.Precision.HIGHEST


def split_kernel(x_ref, out_ref):
    share, _, _, _, width = out_ref.shape
    for h in range(share):
        out_ref[h] = x_ref[:, :, :, h * width : (h + 1) * width]


def join_kernel(x_ref, out_ref):
    share, _, _, _, width = x_ref.shape
    for h in range(share):
        out_ref[:, :, :, h * width : (h + 1) * width] = x_ref[h]


def observe_kernel(x_ref, value_ref, precision_ref, cell_ref, count_ref, out_ref):
    own, fields, levels, cells = x_ref.shape
    slots = out_ref.shape[-1]
    tile = pl.program_id(0)
    cell = cell_ref[pl.ds(tile, 1), :]
    in_tile = cell % cells
    level_field = cell // cells
    wanted = (level_field % fields) * levels + level_field // fields
    onehot = lax.broadcasted_iota(jnp.int32, (cells, slots), 0) == in_tile
    rows = x_ref[...].reshape(own * fields * levels, cells)
    found = jnp.dot(rows, onehot.astype(rows.dtype), preferred_element_type=jnp.float32)
    found = found.reshape(own, fields * levels, slots)
    match = lax.broadcasted_iota(jnp.int32, (fields * levels, slots), 0) == wanted
    picked = jnp.sum(jnp.where(match[None], found, 0.0), axis=1)
    used = lax.broadcasted_iota(jnp.int32, (1, slots), 1) < count_ref[0, tile]
    active = jnp.where(used, precision_ref[pl.ds(tile, 1), :], 0.0)
    row_place = (in_tile // TILE_SIDE).astype(jnp.float32)
    col_place = (in_tile % TILE_SIDE).astype(jnp.float32)
    out_ref[0, 0:own, :] = picked
    out_ref[0, own : own + 1, :] = value_ref[pl.ds(tile, 1), :]
    out_ref[0, own + 1 : own + 2, :] = active
    out_ref[0, own + 2 : own + 3, :] = row_place
    out_ref[0, own + 3 : own + 4, :] = col_place


def near_kernel(above_ref, own_ref, below_ref, out_ref):
    parts, _, own, _ = out_ref.shape
    tiles = own_ref.shape[0]
    share = parts // tiles
    for a, rows_ref in enumerate((above_ref, own_ref, below_ref)):
        for t in range(tiles):
            rows = rows_ref[t, 0:own, :].astype(out_ref.dtype)
            for b in range(3):
                for h in range(share):
                    place = t + 1 - b
                    if 0 <= place < tiles:
                        out_ref[place * share + h, a * 3 + b] = rows
    for h in range(share):
        for a in range(3):
            blank = jnp.zeros((own, out_ref.shape[-1]), out_ref.dtype)
            out_ref[h, a * 3] = blank
            out_ref[(tiles - 1) * share + h, a * 3 + 2] = blank


def solve_kernel(levels, where_ref, radius_ref, pred_ref, above_ref, own_ref, below_ref, out_ref):
    tile = where_ref[0]
    tiles = own_ref.shape[0]
    sources, _, own, slots = pred_ref.shape
    members = sources * own
    reach = radius_ref[0, tile].astype(jnp.float32)
    centre = 0.5 * TILE_SIDE - 0.5
    ensemble, values, weights = [], [], []
    for a, rows_ref in enumerate((above_ref, own_ref, below_ref)):
        for b in range(3):
            place = tile + b - 1
            inside = jnp.logical_and(place >= 0, place < tiles)
            held = jnp.clip(place, 0, tiles - 1)
            value, active, row, col = (
                rows_ref[held, own + i : own + i + 1, :] for i in range(4)
            )
            dist_row = row + ((a - 1) * TILE_SIDE - centre)
            dist_col = col + ((b - 1) * TILE_SIDE - centre)
            taper = jnp.maximum(
                1.0 - (dist_row * dist_row + dist_col * dist_col) / (reach * reach), 0.0
            )
            weights.append(jnp.where(inside, active, 0.0) * (taper * taper))
            values.append(value)
            ensemble.append(
                pred_ref[:, a * 3 + b].astype(jnp.float32).reshape(members, slots)
            )
    ensemble = jnp.concatenate(ensemble, axis=1)
    values = jnp.concatenate(values, axis=1)
    weight = jnp.concatenate(weights, axis=1)
    mean_obs = jnp.mean(ensemble, axis=0, keepdims=True)
    anomaly = ensemble - mean_obs
    innovation = values - mean_obs
    scaled = anomaly * weight
    extended = jnp.concatenate(
        [anomaly, jnp.broadcast_to(innovation, (8, innovation.shape[1]))], axis=0
    )
    product = lax.dot_general(
        extended, scaled, (((1,), (1,)), ((), ())), precision=EXACT,
        preferred_element_type=jnp.float32,
    )
    forcing = product[members : members + 1]
    row_id = lax.broadcasted_iota(jnp.int32, (members, members), 0)
    col_id = lax.broadcasted_iota(jnp.int32, (members, members), 1)
    identity = (row_id == col_id).astype(jnp.float32)
    system = (members - 1.0) * identity + product[:members]
    scale = jnp.sum(
        jnp.sum(system * identity, axis=1, keepdims=True), axis=0, keepdims=True
    )
    root_part = system / scale
    inverse = identity
    mul = functools.partial(jnp.dot, precision=EXACT, preferred_element_type=jnp.float32)
    for sweep in range(SWEEPS):
        factor = 1.5 * identity - 0.5 * (root_part if sweep == 0 else mul(inverse, root_part))
        if sweep < SWEEPS - 1:
            root_part = mul(root_part, factor)
        inverse = factor if sweep == 0 else mul(factor, inverse)
    inv_sqrt = inverse / jnp.sqrt(scale)
    half = jnp.sum(inv_sqrt * forcing, axis=1, keepdims=True)
    mean_weight = jnp.sum(inv_sqrt * half, axis=0, keepdims=True)
    total = jnp.sqrt(jnp.float32(members - 1)) * inv_sqrt + mean_weight
    mixing = total - jnp.mean(total, axis=1, keepdims=True) + 1.0 / members
    mixing = mixing.astype(jnp.bfloat16)
    wide = members * levels
    spread = (
        lax.broadcasted_iota(jnp.int32, (wide, members), 0) // levels
        == lax.broadcasted_iota(jnp.int32, (wide, members), 1)
    ).astype(jnp.bfloat16)
    tall = jnp.dot(spread, mixing, preferred_element_type=jnp.float32).astype(jnp.bfloat16)
    full = lax.dot_general(
        tall, spread, (((1,), (1,)), ((), ())), preferred_element_type=jnp.float32
    )
    same = (
        lax.broadcasted_iota(jnp.int32, (wide, wide), 0) % levels
        == lax.broadcasted_iota(jnp.int32, (wide, wide), 1) % levels
    )
    out_ref[...] = jnp.where(same, full, 0.0).astype(out_ref.dtype)


def apply_kernel(mix_ref, x_ref, out_ref):
    sources, own, _, levels, width = x_ref.shape
    rows = x_ref[...].reshape(sources * own * levels, width)
    mixed = jnp.dot(mix_ref[...], rows, preferred_element_type=jnp.float32)
    out_ref[...] = mixed.astype(out_ref.dtype).reshape(out_ref.shape)


def observe(fields, values, precision, cells, count):
    own, kinds, levels, width = fields.shape
    tiles, slots = cells.shape
    whole = pl.BlockSpec((tiles, slots), lambda t: (0, 0))
    return pl.pallas_call(
        observe_kernel,
        grid=(tiles,),
        in_specs=[
            pl.BlockSpec((own, kinds, levels, TILE_CELLS), lambda t: (0, 0, 0, t)),
            whole,
            whole,
            whole,
            pl.BlockSpec(memory_space=pltpu.SMEM),
        ],
        out_specs=pl.BlockSpec((1, own + 4, slots), lambda t: (t, 0, 0)),
        out_shape=jax.ShapeDtypeStruct((tiles, own + 4, slots), jnp.float32),
        name="observe",
    )(fields, values, precision, cells, count)


def split(fields, parts):
    own, kinds, levels, width = fields.shape
    part = width // parts
    share = TILE_CELLS // part
    return pl.pallas_call(
        split_kernel,
        grid=(parts // share,),
        in_specs=[pl.BlockSpec((own, kinds, levels, TILE_CELLS), lambda t: (0, 0, 0, t))],
        out_specs=pl.BlockSpec((share, own, kinds, levels, part), lambda t: (t, 0, 0, 0, 0)),
        out_shape=jax.ShapeDtypeStruct((parts, own, kinds, levels, part), fields.dtype),
        name="split",
    )(fields)


def join(pieces):
    parts, own, kinds, levels, part = pieces.shape
    share = TILE_CELLS // part
    return pl.pallas_call(
        join_kernel,
        grid=(parts // share,),
        in_specs=[pl.BlockSpec((share, own, kinds, levels, part), lambda t: (t, 0, 0, 0, 0))],
        out_specs=pl.BlockSpec((own, kinds, levels, TILE_CELLS), lambda t: (0, 0, 0, t)),
        out_shape=jax.ShapeDtypeStruct((own, kinds, levels, parts * part), pieces.dtype),
        name="join",
    )(pieces)


def surround(above, own, below, parts, members):
    tiles, _, slots = own.shape
    vmem = pl.BlockSpec(memory_space=pltpu.VMEM)
    return pl.pallas_call(
        near_kernel,
        in_specs=[vmem, vmem, vmem],
        out_specs=vmem,
        out_shape=jax.ShapeDtypeStruct((parts, 9, members, slots), jnp.bfloat16),
        name="surround",
    )(above, own, below)


def solve(tile, radius, pred, above, own, below, levels):
    members = pred.shape[0] * pred.shape[2]
    wide = members * levels
    vmem = pl.BlockSpec(memory_space=pltpu.VMEM)
    smem = pl.BlockSpec(memory_space=pltpu.SMEM)
    return pl.pallas_call(
        functools.partial(solve_kernel, levels),
        in_specs=[smem, smem, vmem, vmem, vmem, vmem],
        out_specs=vmem,
        out_shape=jax.ShapeDtypeStruct((wide, wide), jnp.bfloat16),
        name="solve",
    )(tile, radius, pred, above, own, below)


def apply_mixing(mix, pieces):
    parts, own, count, levels, part = pieces.shape
    block = pl.BlockSpec((parts, own, 1, levels, part), lambda f: (0, 0, f, 0, 0))
    return pl.pallas_call(
        apply_kernel,
        grid=(count,),
        in_specs=[pl.BlockSpec(mix.shape, lambda f: (0, 0)), block],
        out_specs=block,
        out_shape=jax.ShapeDtypeStruct(pieces.shape, pieces.dtype),
        name="apply",
    )(mix, pieces)


def on_device(background, obs_values, obs_precision, obs_cell, obs_count, radius):
    own, levels, kinds, _, width = background.shape
    parts = lax.axis_size("member")
    rows = lax.axis_size("space")
    share = parts * TILE_CELLS // width
    down = [(i, i + 1) for i in range(rows - 1)]
    up = [(i + 1, i) for i in range(rows - 1)]
    fields = background.transpose(0, 2, 3, 1, 4).reshape(own, kinds, levels, width)
    pieces = split(fields, parts)
    pieces, fields = lax.optimization_barrier((pieces, fields))
    sent = lax.all_to_all(pieces, "member", 0, 0)

    here = observe(fields, obs_values[0], obs_precision[0], obs_cell[0], obs_count)
    above = lax.ppermute(here, "space", down)
    below = lax.ppermute(here, "space", up)
    near = lax.all_to_all(surround(above, here, below, parts, own), "member", 0, 0)
    tile = (lax.axis_index("member") // share).astype(jnp.int32).reshape(1)
    mix = solve(tile, radius, near, above, here, below, levels)

    mixed = apply_mixing(mix, sent)
    back = lax.all_to_all(mixed, "member", 0, 0)
    out = join(back)
    return out.reshape(own, kinds, 1, levels, width).transpose(0, 3, 1, 2, 4)


def solution(mesh):
    return jax.shard_map(
        on_device,
        mesh=mesh,
        in_specs=(
            P("member", None, None, "space", None),
            P("space", None, None),
            P("space", None, None),
            P("space", None, None),
            P("space", None),
            P("space", None),
        ),
        out_specs=P("member", None, None, "space", None),
        check_vma=False,
    )
```

```python
import functools

import jax
import jax.numpy as jnp
from jax import lax
from jax.experimental import pallas as pl
from jax.experimental.pallas import tpu as pltpu
from jax.sharding import PartitionSpec as P

TILE_SIDE = 32
TILE_CELLS = 1024
SWEEPS = 6
EXACT = lax.Precision.HIGHEST


LANES = 128


def split_kernel(x_ref, out_ref):
    own, kinds, levels, width = x_ref.shape
    blocks = width // LANES
    per = blocks // out_ref.shape[0]

    def body(f, carry):
        for c in range(blocks):
            for m in range(own):
                out_ref[c // per, (f * per + c % per) * own + m] = x_ref[
                    m, f, :, c * LANES : (c + 1) * LANES
                ]
        return carry

    lax.fori_loop(0, kinds, body, 0)


def join_kernel(x_ref, out_ref):
    own, kinds, levels, width = out_ref.shape
    blocks = width // LANES
    per = blocks // x_ref.shape[0]

    def body(f, carry):
        for c in range(blocks):
            for m in range(own):
                out_ref[m, f, :, c * LANES : (c + 1) * LANES] = x_ref[
                    c // per, (f * per + c % per) * own + m
                ]
        return carry

    lax.fori_loop(0, kinds, body, 0)


def observe_kernel(x_ref, value_ref, precision_ref, cell_ref, count_ref, out_ref):
    own, fields, levels, cells = x_ref.shape
    slots = out_ref.shape[-1]
    tile = pl.program_id(0)
    cell = cell_ref[pl.ds(tile, 1), :]
    in_tile = cell % cells
    level_field = cell // cells
    wanted = (level_field % fields) * levels + level_field // fields
    onehot = lax.broadcasted_iota(jnp.int32, (cells, slots), 0) == in_tile
    rows = x_ref[...].reshape(own * fields * levels, cells)
    found = jnp.dot(rows, onehot.astype(rows.dtype), preferred_element_type=jnp.float32)
    found = found.reshape(own, fields * levels, slots)
    match = lax.broadcasted_iota(jnp.int32, (fields * levels, slots), 0) == wanted
    picked = jnp.sum(jnp.where(match[None], found, 0.0), axis=1)
    used = lax.broadcasted_iota(jnp.int32, (1, slots), 1) < count_ref[0, tile]
    active = jnp.where(used, precision_ref[pl.ds(tile, 1), :], 0.0)
    row_place = (in_tile // TILE_SIDE).astype(jnp.float32)
    col_place = (in_tile % TILE_SIDE).astype(jnp.float32)
    out_ref[0, 0:own, :] = picked
    out_ref[0, own : own + 1, :] = value_ref[pl.ds(tile, 1), :]
    out_ref[0, own + 1 : own + 2, :] = active
    out_ref[0, own + 2 : own + 3, :] = row_place
    out_ref[0, own + 3 : own + 4, :] = col_place


def near_kernel(first, above_ref, own_ref, below_ref, _, out_ref, held, sem):
    parts, _, own, slots = held.shape
    tiles = own_ref.shape[0]
    share = parts // tiles
    for a, rows_ref in enumerate((above_ref, own_ref, below_ref)):
        for t in range(tiles):
            rows = rows_ref[t, 0:own, :].astype(held.dtype)
            for b in range(3):
                for h in range(share):
                    place = t + 1 - b
                    if 0 <= place < tiles:
                        held[place * share + h, a * 3 + b] = rows
    blank = jnp.zeros((own, slots), held.dtype)
    for h in range(share):
        for a in range(3):
            held[h, a * 3] = blank
            held[(tiles - 1) * share + h, a * 3 + 2] = blank
    copy = pltpu.make_async_copy(held, out_ref.at[:, pl.ds(first, 9)], sem)
    copy.start()
    copy.wait()


def analyse_kernel(
    kinds, where_ref, radius_ref, x_ref, above_ref, own_ref, below_ref, out_ref, mix_ref
):
    tile = where_ref[0]
    tiles = own_ref.shape[0]
    sources, _, levels, slots = x_ref.shape
    own = own_ref.shape[1] - 4
    first = out_ref.shape[1]
    members = sources * own
    reach = radius_ref[0, tile].astype(jnp.float32)
    centre = 0.5 * TILE_SIDE - 0.5
    ensemble, values, weights = [], [], []
    for a, rows_ref in enumerate((above_ref, own_ref, below_ref)):
        for b in range(3):
            place = tile + b - 1
            inside = jnp.logical_and(place >= 0, place < tiles)
            held = jnp.clip(place, 0, tiles - 1)
            value, active, row, col = (
                rows_ref[held, own + i : own + i + 1, :] for i in range(4)
            )
            dist_row = row + ((a - 1) * TILE_SIDE - centre)
            dist_col = col + ((b - 1) * TILE_SIDE - centre)
            taper = jnp.maximum(
                1.0 - (dist_row * dist_row + dist_col * dist_col) / (reach * reach), 0.0
            )
            weights.append(jnp.where(inside, active, 0.0) * (taper * taper))
            values.append(value)
            ensemble.append(
                x_ref[:, first + a * 3 + b].astype(jnp.float32).reshape(members, slots)
            )
    ensemble = jnp.concatenate(ensemble, axis=1)
    values = jnp.concatenate(values, axis=1)
    weight = jnp.concatenate(weights, axis=1)
    mean_obs = jnp.mean(ensemble, axis=0, keepdims=True)
    anomaly = ensemble - mean_obs
    innovation = values - mean_obs
    scaled = anomaly * weight
    extended = jnp.concatenate(
        [anomaly, jnp.broadcast_to(innovation, (8, innovation.shape[1]))], axis=0
    )
    product = lax.dot_general(
        extended, scaled, (((1,), (1,)), ((), ())), precision=EXACT,
        preferred_element_type=jnp.float32,
    )
    forcing = product[members : members + 1]
    row_id = lax.broadcasted_iota(jnp.int32, (members, members), 0)
    col_id = lax.broadcasted_iota(jnp.int32, (members, members), 1)
    identity = (row_id == col_id).astype(jnp.float32)
    system = (members - 1.0) * identity + product[:members]
    scale = jnp.sum(
        jnp.sum(system * identity, axis=1, keepdims=True), axis=0, keepdims=True
    )
    root_part = system / scale
    inverse = identity
    mul = functools.partial(jnp.dot, precision=EXACT, preferred_element_type=jnp.float32)
    for sweep in range(SWEEPS):
        factor = 1.5 * identity - 0.5 * (root_part if sweep == 0 else mul(inverse, root_part))
        if sweep < SWEEPS - 1:
            root_part = mul(root_part, factor)
        inverse = factor if sweep == 0 else mul(factor, inverse)
    inv_sqrt = inverse / jnp.sqrt(scale)
    half = jnp.sum(inv_sqrt * forcing, axis=1, keepdims=True)
    mean_weight = jnp.sum(inv_sqrt * half, axis=0, keepdims=True)
    total = jnp.sqrt(jnp.float32(members - 1)) * inv_sqrt + mean_weight
    mixing = total - jnp.mean(total, axis=1, keepdims=True) + 1.0 / members
    mixing = mixing.astype(jnp.bfloat16)
    wide = members * levels
    spread = (
        lax.broadcasted_iota(jnp.int32, (wide, members), 0) // levels
        == lax.broadcasted_iota(jnp.int32, (wide, members), 1)
    ).astype(jnp.bfloat16)
    tall = jnp.dot(spread, mixing, preferred_element_type=jnp.float32).astype(jnp.bfloat16)
    full = lax.dot_general(
        tall, spread, (((1,), (1,)), ((), ())), preferred_element_type=jnp.float32
    )
    same = (
        lax.broadcasted_iota(jnp.int32, (wide, wide), 0) % levels
        == lax.broadcasted_iota(jnp.int32, (wide, wide), 1) % levels
    )
    mix_ref[...] = jnp.where(same, full, 0.0).astype(mix_ref.dtype)
    per = first // (kinds * own)

    def body(f, carry):
        places = [pl.ds((f * per + c) * own, own) for c in range(per)]
        rows = jnp.concatenate(
            [x_ref[:, place].reshape(wide, LANES) for place in places], axis=1
        )
        mixed = jnp.dot(mix_ref[...], rows, preferred_element_type=jnp.float32)
        mixed = mixed.astype(out_ref.dtype)
        for c, place in enumerate(places):
            out_ref[:, place] = mixed[:, c * LANES : (c + 1) * LANES].reshape(
                sources, own, levels, LANES
            )
        return carry

    lax.fori_loop(0, kinds, body, 0)


def observe(fields, values, precision, cells, count):
    own, kinds, levels, width = fields.shape
    tiles, slots = cells.shape
    whole = pl.BlockSpec((tiles, slots), lambda t: (0, 0))
    return pl.pallas_call(
        observe_kernel,
        grid=(tiles,),
        in_specs=[
            pl.BlockSpec((own, kinds, levels, TILE_CELLS), lambda t: (0, 0, 0, t)),
            whole,
            whole,
            whole,
            pl.BlockSpec(memory_space=pltpu.SMEM),
        ],
        out_specs=pl.BlockSpec((1, own + 4, slots), lambda t: (t, 0, 0)),
        out_shape=jax.ShapeDtypeStruct((tiles, own + 4, slots), jnp.float32),
        name="observe",
    )(fields, values, precision, cells, count)


VMEM = pl.BlockSpec(memory_space=pltpu.VMEM)
SMEM = pl.BlockSpec(memory_space=pltpu.SMEM)
ANY = pl.BlockSpec(memory_space=pl.ANY)


def split(fields, parts):
    own, kinds, levels, width = fields.shape
    blocks = own * kinds * (width // parts // LANES)
    return pl.pallas_call(
        split_kernel,
        in_specs=[VMEM],
        out_specs=VMEM,
        out_shape=jax.ShapeDtypeStruct((parts, blocks + 9, levels, LANES), fields.dtype),
        name="split",
    )(fields)


def join(pieces, shape):
    return pl.pallas_call(
        join_kernel,
        in_specs=[VMEM],
        out_specs=VMEM,
        out_shape=jax.ShapeDtypeStruct(shape, pieces.dtype),
        name="join",
    )(pieces)


def surround(above, own, below, pieces):
    parts, blocks, levels, slots = pieces.shape
    return pl.pallas_call(
        functools.partial(near_kernel, blocks - 9),
        in_specs=[VMEM, VMEM, VMEM, ANY],
        out_specs=ANY,
        out_shape=jax.ShapeDtypeStruct(pieces.shape, pieces.dtype),
        scratch_shapes=[
            pltpu.VMEM((parts, 9, own.shape[1] - 4, slots), pieces.dtype),
            pltpu.SemaphoreType.DMA,
        ],
        input_output_aliases={3: 0},
        name="surround",
    )(above, own, below, pieces)


def analyse(tile, radius, pieces, above, own, below, kinds):
    parts, blocks, levels, lanes = pieces.shape
    wide = parts * (own.shape[1] - 4) * levels
    return pl.pallas_call(
        functools.partial(analyse_kernel, kinds),
        in_specs=[SMEM, SMEM, VMEM, VMEM, VMEM, VMEM],
        out_specs=VMEM,
        out_shape=jax.ShapeDtypeStruct((parts, blocks - 9, levels, lanes), pieces.dtype),
        scratch_shapes=[pltpu.VMEM((wide, wide), jnp.bfloat16)],
        name="analyse",
    )(tile, radius, pieces, above, own, below)


def on_device(background, obs_values, obs_precision, obs_cell, obs_count, radius):
    own, levels, kinds, _, width = background.shape
    parts = lax.axis_size("member")
    rows = lax.axis_size("space")
    share = parts * TILE_CELLS // width
    down = [(i, i + 1) for i in range(rows - 1)]
    up = [(i + 1, i) for i in range(rows - 1)]
    fields = background.transpose(0, 2, 3, 1, 4).reshape(own, kinds, levels, width)
    here = observe(fields, obs_values[0], obs_precision[0], obs_cell[0], obs_count)
    above = lax.ppermute(here, "space", down)
    below = lax.ppermute(here, "space", up)
    pieces = surround(above, here, below, split(fields, parts))
    sent = lax.all_to_all(pieces, "member", 0, 0)
    tile = (lax.axis_index("member") // share).astype(jnp.int32).reshape(1)
    mixed = analyse(tile, radius, sent, above, here, below, kinds)
    out = join(lax.all_to_all(mixed, "member", 0, 0), fields.shape)
    return out.reshape(own, kinds, 1, levels, width).transpose(0, 3, 1, 2, 4)


def solution(mesh):
    return jax.shard_map(
        on_device,
        mesh=mesh,
        in_specs=(
            P("member", None, None, "space", None),
            P("space", None, None),
            P("space", None, None),
            P("space", None, None),
            P("space", None),
            P("space", None),
        ),
        out_specs=P("member", None, None, "space", None),
        check_vma=False,
    )
```

```python
import functools

import jax
import jax.numpy as jnp
from jax import lax
from jax.experimental import pallas as pl
from jax.experimental.pallas import tpu as pltpu
from jax.sharding import PartitionSpec as P

TILE_SIDE = 32
TILE_CELLS = 1024
SWEEPS = 6
EXACT = lax.Precision.HIGHEST


LANES = 128
VMEM = pl.BlockSpec(memory_space=pltpu.VMEM)
SMEM = pl.BlockSpec(memory_space=pltpu.SMEM)
PARAMS = pltpu.CompilerParams(vmem_limit_bytes=16 * 1024 * 1024)
EARLY = 3


def copy_blocks(x_ref, out_ref, begin, end):
    own, _, _, width = x_ref.shape
    blocks = width // LANES
    per = blocks // out_ref.shape[0]

    def body(f, carry):
        for c in range(blocks):
            for m in range(own):
                out_ref[c // per, ((f - begin) * per + c % per) * own + m] = x_ref[
                    m, f, :, c * LANES : (c + 1) * LANES
                ]
        return carry

    lax.fori_loop(begin, end, body, 0)


def split_kernel(end, x_ref, out_ref):
    copy_blocks(x_ref, out_ref, 0, end)


def join_kernel(x_ref, out_ref):
    own, kinds, levels, width = out_ref.shape
    blocks = width // LANES
    per = blocks // x_ref.shape[0]

    def body(f, carry):
        for c in range(blocks):
            for m in range(own):
                out_ref[m, f, :, c * LANES : (c + 1) * LANES] = x_ref[
                    c // per, (f * per + c % per) * own + m
                ]
        return carry

    lax.fori_loop(0, kinds, body, 0)


def observe_kernel(x_ref, value_ref, precision_ref, cell_ref, count_ref, out_ref):
    own, fields, levels, cells = x_ref.shape
    slots = out_ref.shape[-1]
    tile = pl.program_id(0)
    cell = cell_ref[pl.ds(tile, 1), :]
    in_tile = cell % cells
    level_field = cell // cells
    wanted = (level_field % fields) * levels + level_field // fields
    onehot = lax.broadcasted_iota(jnp.int32, (cells, slots), 0) == in_tile
    rows = x_ref[...].reshape(own * fields * levels, cells)
    found = jnp.dot(rows, onehot.astype(rows.dtype), preferred_element_type=jnp.float32)
    found = found.reshape(own, fields * levels, slots)
    match = lax.broadcasted_iota(jnp.int32, (fields * levels, slots), 0) == wanted
    picked = jnp.sum(jnp.where(match[None], found, 0.0), axis=1)
    used = lax.broadcasted_iota(jnp.int32, (1, slots), 1) < count_ref[0, tile]
    active = jnp.where(used, precision_ref[pl.ds(tile, 1), :], 0.0)
    row_place = (in_tile // TILE_SIDE).astype(jnp.float32)
    col_place = (in_tile % TILE_SIDE).astype(jnp.float32)
    out_ref[0, 0:own, :] = picked
    out_ref[0, own : own + 1, :] = value_ref[pl.ds(tile, 1), :]
    out_ref[0, own + 1 : own + 2, :] = active
    out_ref[0, own + 2 : own + 3, :] = row_place
    out_ref[0, own + 3 : own + 4, :] = col_place


def pack_kernel(begin, x_ref, above_ref, own_ref, below_ref, out_ref):
    copy_blocks(x_ref, out_ref, begin, x_ref.shape[1])
    parts, blocks, own, slots = out_ref.shape
    first = blocks - 9
    tiles = own_ref.shape[0]
    share = parts // tiles
    for a, rows_ref in enumerate((above_ref, own_ref, below_ref)):
        for t in range(tiles):
            rows = rows_ref[t, 0:own, :].astype(out_ref.dtype)
            for b in range(3):
                for h in range(share):
                    place = t + 1 - b
                    if 0 <= place < tiles:
                        out_ref[place * share + h, first + a * 3 + b] = rows
    blank = jnp.zeros((own, slots), out_ref.dtype)
    for h in range(share):
        for a in range(3):
            out_ref[h, first + a * 3] = blank
            out_ref[(tiles - 1) * share + h, first + a * 3 + 2] = blank


def analyse_kernel(
    kinds, where_ref, radius_ref, early_ref, x_ref, above_ref, own_ref, below_ref, out_ref, mix_ref
):
    tile = where_ref[0]
    tiles = own_ref.shape[0]
    sources, _, levels, slots = x_ref.shape
    own = own_ref.shape[1] - 4
    ahead = early_ref.shape[1]
    first = x_ref.shape[1] - 9
    members = sources * own
    reach = radius_ref[0, tile].astype(jnp.float32)
    centre = 0.5 * TILE_SIDE - 0.5
    ensemble, values, weights = [], [], []
    for a, rows_ref in enumerate((above_ref, own_ref, below_ref)):
        for b in range(3):
            place = tile + b - 1
            inside = jnp.logical_and(place >= 0, place < tiles)
            held = jnp.clip(place, 0, tiles - 1)
            value, active, row, col = (
                rows_ref[held, own + i : own + i + 1, :] for i in range(4)
            )
            dist_row = row + ((a - 1) * TILE_SIDE - centre)
            dist_col = col + ((b - 1) * TILE_SIDE - centre)
            taper = jnp.maximum(
                1.0 - (dist_row * dist_row + dist_col * dist_col) / (reach * reach), 0.0
            )
            weights.append(jnp.where(inside, active, 0.0) * (taper * taper))
            values.append(value)
            ensemble.append(
                x_ref[:, first + a * 3 + b].astype(jnp.float32).reshape(members, slots)
            )
    ensemble = jnp.concatenate(ensemble, axis=1)
    values = jnp.concatenate(values, axis=1)
    weight = jnp.concatenate(weights, axis=1)
    mean_obs = jnp.mean(ensemble, axis=0, keepdims=True)
    anomaly = ensemble - mean_obs
    innovation = values - mean_obs
    scaled = anomaly * weight
    extended = jnp.concatenate(
        [anomaly, jnp.broadcast_to(innovation, (8, innovation.shape[1]))], axis=0
    )
    product = lax.dot_general(
        extended, scaled, (((1,), (1,)), ((), ())), precision=EXACT,
        preferred_element_type=jnp.float32,
    )
    forcing = product[members : members + 1]
    row_id = lax.broadcasted_iota(jnp.int32, (members, members), 0)
    col_id = lax.broadcasted_iota(jnp.int32, (members, members), 1)
    identity = (row_id == col_id).astype(jnp.float32)
    system = (members - 1.0) * identity + product[:members]
    scale = jnp.sum(
        jnp.sum(system * identity, axis=1, keepdims=True), axis=0, keepdims=True
    )
    root_part = system / scale
    inverse = identity
    mul = functools.partial(jnp.dot, precision=EXACT, preferred_element_type=jnp.float32)
    for sweep in range(SWEEPS):
        factor = 1.5 * identity - 0.5 * (root_part if sweep == 0 else mul(inverse, root_part))
        if sweep < SWEEPS - 1:
            root_part = mul(root_part, factor)
        inverse = factor if sweep == 0 else mul(factor, inverse)
    inv_sqrt = inverse / jnp.sqrt(scale)
    half = jnp.sum(inv_sqrt * forcing, axis=1, keepdims=True)
    mean_weight = jnp.sum(inv_sqrt * half, axis=0, keepdims=True)
    total = jnp.sqrt(jnp.float32(members - 1)) * inv_sqrt + mean_weight
    mixing = total - jnp.mean(total, axis=1, keepdims=True) + 1.0 / members
    mixing = mixing.astype(jnp.bfloat16)
    wide = members * levels
    spread = (
        lax.broadcasted_iota(jnp.int32, (wide, members), 0) // levels
        == lax.broadcasted_iota(jnp.int32, (wide, members), 1)
    ).astype(jnp.bfloat16)
    tall = jnp.dot(spread, mixing, preferred_element_type=jnp.float32).astype(jnp.bfloat16)
    full = lax.dot_general(
        tall, spread, (((1,), (1,)), ((), ())), preferred_element_type=jnp.float32
    )
    same = (
        lax.broadcasted_iota(jnp.int32, (wide, wide), 0) % levels
        == lax.broadcasted_iota(jnp.int32, (wide, wide), 1) % levels
    )
    mix_ref[...] = jnp.where(same, full, 0.0).astype(mix_ref.dtype)
    per = out_ref.shape[1] // (kinds * own)

    def mix_fields(from_ref, offset):
        def body(f, carry):
            begin = f * per * own
            rows = jnp.concatenate(
                [
                    from_ref[:, pl.ds(begin + c * own, own)].reshape(wide, LANES)
                    for c in range(per)
                ],
                axis=1,
            )
            mixed = jnp.dot(mix_ref[...], rows, preferred_element_type=jnp.float32)
            mixed = mixed.astype(out_ref.dtype)
            for c in range(per):
                out_ref[:, pl.ds(offset + begin + c * own, own)] = mixed[
                    :, c * LANES : (c + 1) * LANES
                ].reshape(sources, own, levels, LANES)
            return carry

        return body

    lax.fori_loop(0, ahead // (per * own), mix_fields(early_ref, 0), 0)
    lax.fori_loop(0, first // (per * own), mix_fields(x_ref, ahead), 0)


def observe(fields, values, precision, cells, count):
    own, kinds, levels, width = fields.shape
    tiles, slots = cells.shape
    whole = pl.BlockSpec((tiles, slots), lambda t: (0, 0))
    return pl.pallas_call(
        observe_kernel,
        grid=(tiles,),
        in_specs=[
            pl.BlockSpec((own, kinds, levels, TILE_CELLS), lambda t: (0, 0, 0, t)),
            whole,
            whole,
            whole,
            pl.BlockSpec(memory_space=pltpu.SMEM),
        ],
        out_specs=pl.BlockSpec((1, own + 4, slots), lambda t: (t, 0, 0)),
        out_shape=jax.ShapeDtypeStruct((tiles, own + 4, slots), jnp.float32),
        compiler_params=PARAMS,
        name="observe",
    )(fields, values, precision, cells, count)


def split(fields, parts, end):
    own, kinds, levels, width = fields.shape
    blocks = own * end * (width // parts // LANES)
    return pl.pallas_call(
        functools.partial(split_kernel, end),
        in_specs=[VMEM],
        out_specs=VMEM,
        out_shape=jax.ShapeDtypeStruct((parts, blocks, levels, LANES), fields.dtype),
        compiler_params=PARAMS,
        name="split",
    )(fields)


def join(pieces, shape):
    return pl.pallas_call(
        join_kernel,
        in_specs=[VMEM],
        out_specs=VMEM,
        out_shape=jax.ShapeDtypeStruct(shape, pieces.dtype),
        compiler_params=PARAMS,
        name="join",
    )(pieces)


def pack(fields, parts, begin, above, here, below):
    own, kinds, levels, width = fields.shape
    blocks = own * (kinds - begin) * (width // parts // LANES) + 9
    return pl.pallas_call(
        functools.partial(pack_kernel, begin),
        in_specs=[VMEM] * 4,
        out_specs=VMEM,
        out_shape=jax.ShapeDtypeStruct((parts, blocks, levels, LANES), fields.dtype),
        compiler_params=PARAMS,
        name="pack",
    )(fields, above, here, below)


def analyse(tile, radius, early, late, above, here, below, kinds):
    parts, blocks, levels, lanes = early.shape
    wide = parts * (here.shape[1] - 4) * levels
    blocks += late.shape[1] - 9
    return pl.pallas_call(
        functools.partial(analyse_kernel, kinds),
        in_specs=[SMEM, SMEM] + [VMEM] * 5,
        out_specs=VMEM,
        out_shape=jax.ShapeDtypeStruct((parts, blocks, levels, lanes), early.dtype),
        scratch_shapes=[pltpu.VMEM((wide, wide), jnp.bfloat16)],
        compiler_params=PARAMS,
        name="analyse",
    )(tile, radius, early, late, above, here, below)


def on_device(background, obs_values, obs_precision, obs_cell, obs_count, radius):
    own, levels, kinds, _, width = background.shape
    parts = lax.axis_size("member")
    rows = lax.axis_size("space")
    share = parts * TILE_CELLS // width
    down = [(i, i + 1) for i in range(rows - 1)]
    up = [(i + 1, i) for i in range(rows - 1)]
    fields = background.transpose(0, 2, 3, 1, 4).reshape(own, kinds, levels, width)
    early = split(fields, parts, EARLY)
    early, fields = lax.optimization_barrier((early, fields))
    early = lax.all_to_all(early, "member", 0, 0)
    here = observe(fields, obs_values[0], obs_precision[0], obs_cell[0], obs_count)
    above = lax.ppermute(here, "space", down)
    below = lax.ppermute(here, "space", up)
    late = pack(fields, parts, EARLY, above, here, below)
    late = lax.all_to_all(late, "member", 0, 0)
    tile = (lax.axis_index("member") // share).astype(jnp.int32).reshape(1)
    mixed = analyse(tile, radius, early, late, above, here, below, kinds)
    out = join(lax.all_to_all(mixed, "member", 0, 0), fields.shape)
    return out.reshape(own, kinds, 1, levels, width).transpose(0, 3, 1, 2, 4)


def solution(mesh):
    return jax.shard_map(
        on_device,
        mesh=mesh,
        in_specs=(
            P("member", None, None, "space", None),
            P("space", None, None),
            P("space", None, None),
            P("space", None, None),
            P("space", None),
            P("space", None),
        ),
        out_specs=P("member", None, None, "space", None),
        check_vma=False,
    )
```

```python
import functools

import jax
import jax.numpy as jnp
from jax import lax
from jax.experimental import pallas as pl
from jax.experimental.pallas import tpu as pltpu
from jax.sharding import PartitionSpec as P

TILE_SIDE = 32
TILE_CELLS = 1024
SWEEPS = 6


LANES = 128
VMEM = pl.BlockSpec(memory_space=pltpu.VMEM)
SMEM = pl.BlockSpec(memory_space=pltpu.SMEM)
HBM = pl.BlockSpec(memory_space=pltpu.HBM)
PARAMS = pltpu.CompilerParams(vmem_limit_bytes=16 * 1024 * 1024)
EARLY = 3


def split_kernel(x_ref, out_ref, held, made, in_sems, out_sems):
    kinds, own = held.shape[:2]
    width = held.shape[3]
    blocks = width // LANES
    parts, step = made.shape[1:3]
    per = blocks // parts
    loads = [
        pltpu.make_async_copy(x_ref.at[:, f], held.at[f], in_sems.at[f]) for f in range(kinds)
    ]
    stores = [
        pltpu.make_async_copy(
            made.at[f], out_ref.at[:, pl.ds(f * step, step)], out_sems.at[f]
        )
        for f in range(kinds)
    ]
    for load in loads:
        load.start()
    for f in range(kinds):
        loads[f].wait()
        for c in range(blocks):
            for m in range(own):
                made[f, c // per, c % per * own + m] = held[
                    f, m, :, c * LANES : (c + 1) * LANES
                ]
        stores[f].start()
    for store in stores:
        store.wait()


def join_kernel(x_ref, out_ref, made, out_sems):
    kinds, own = made.shape[:2]
    width = made.shape[3]
    blocks = width // LANES
    per = blocks // x_ref.shape[0]
    stores = [
        pltpu.make_async_copy(made.at[f], out_ref.at[:, f], out_sems.at[f])
        for f in range(kinds)
    ]
    for f in range(kinds):
        for c in range(blocks):
            for m in range(own):
                made[f, m, :, c * LANES : (c + 1) * LANES] = x_ref[
                    c // per, (f * per + c % per) * own + m
                ]
        stores[f].start()
    for store in stores:
        store.wait()


def observe_kernel(x_ref, value_ref, precision_ref, cell_ref, count_ref, out_ref):
    own, fields, levels, cells = x_ref.shape
    slots = out_ref.shape[-1]
    tile = pl.program_id(0)
    cell = cell_ref[pl.ds(tile, 1), :]
    in_tile = cell % cells
    level_field = cell // cells
    wanted = (level_field % fields) * levels + level_field // fields
    onehot = lax.broadcasted_iota(jnp.int32, (cells, slots), 0) == in_tile
    rows = x_ref[...].reshape(own * fields * levels, cells)
    found = jnp.dot(rows, onehot.astype(rows.dtype), preferred_element_type=jnp.float32)
    found = found.reshape(own, fields * levels, slots)
    match = lax.broadcasted_iota(jnp.int32, (fields * levels, slots), 0) == wanted
    picked = jnp.sum(jnp.where(match[None], found, 0.0), axis=1)
    used = lax.broadcasted_iota(jnp.int32, (1, slots), 1) < count_ref[0, tile]
    active = jnp.where(used, precision_ref[pl.ds(tile, 1), :], 0.0)
    row_place = (in_tile // TILE_SIDE).astype(jnp.float32)
    col_place = (in_tile % TILE_SIDE).astype(jnp.float32)
    out_ref[0, 0:own, :] = picked
    out_ref[0, own : own + 1, :] = value_ref[pl.ds(tile, 1), :]
    out_ref[0, own + 1 : own + 2, :] = active
    out_ref[0, own + 2 : own + 3, :] = row_place
    out_ref[0, own + 3 : own + 4, :] = col_place


def pack_kernel(begin, x_ref, above_ref, own_ref, below_ref, out_ref):
    parts, blocks, own, slots = out_ref.shape
    lane_blocks = x_ref.shape[3] // LANES
    per = lane_blocks // parts

    def copy_field(f, carry):
        for c in range(lane_blocks):
            for m in range(own):
                out_ref[c // per, ((f - begin) * per + c % per) * own + m] = x_ref[
                    m, f, :, c * LANES : (c + 1) * LANES
                ]
        return carry

    lax.fori_loop(begin, x_ref.shape[1], copy_field, 0)
    first = blocks - 9
    tiles = own_ref.shape[0]
    share = parts // tiles
    for a, rows_ref in enumerate((above_ref, own_ref, below_ref)):
        for t in range(tiles):
            rows = rows_ref[t, 0:own, :].astype(out_ref.dtype)
            for b in range(3):
                for h in range(share):
                    place = t + 1 - b
                    if 0 <= place < tiles:
                        out_ref[place * share + h, first + a * 3 + b] = rows
    blank = jnp.zeros((own, slots), out_ref.dtype)
    for h in range(share):
        for a in range(3):
            out_ref[h, first + a * 3] = blank
            out_ref[(tiles - 1) * share + h, first + a * 3 + 2] = blank


def two_terms(array):
    high = array.astype(jnp.bfloat16)
    return high, (array - high.astype(jnp.float32)).astype(jnp.bfloat16)


def gram(left, right):
    def product(a, b):
        return lax.dot_general(
            a, b, (((1,), (1,)), ((), ())), preferred_element_type=jnp.float32
        )

    return (
        product(left[0], right[0]) + product(left[0], right[1]) + product(left[1], right[0])
    )


def doubled_product(left, right):
    return jnp.dot(
        jnp.concatenate(left, axis=1),
        jnp.concatenate(right + right, axis=0),
        preferred_element_type=jnp.float32,
    )


def analyse_kernel(
    kinds, where_ref, radius_ref, early_ref, x_ref, above_ref, own_ref, below_ref, out_ref, mix_ref
):
    tile = where_ref[0]
    tiles = own_ref.shape[0]
    sources, _, levels, slots = x_ref.shape
    own = own_ref.shape[1] - 4
    ahead = early_ref.shape[1]
    first = x_ref.shape[1] - 9
    members = sources * own
    reach = radius_ref[0, tile].astype(jnp.float32)
    centre = 0.5 * TILE_SIDE - 0.5
    ensemble, values, weights = [], [], []
    for a, rows_ref in enumerate((above_ref, own_ref, below_ref)):
        for b in range(3):
            place = tile + b - 1
            inside = jnp.logical_and(place >= 0, place < tiles)
            held = jnp.clip(place, 0, tiles - 1)
            value, active, row, col = (
                rows_ref[held, own + i : own + i + 1, :] for i in range(4)
            )
            dist_row = row + ((a - 1) * TILE_SIDE - centre)
            dist_col = col + ((b - 1) * TILE_SIDE - centre)
            taper = jnp.maximum(
                1.0 - (dist_row * dist_row + dist_col * dist_col) / (reach * reach), 0.0
            )
            weights.append(jnp.where(inside, active, 0.0) * (taper * taper))
            values.append(value)
            ensemble.append(
                x_ref[:, first + a * 3 + b].astype(jnp.float32).reshape(members, slots)
            )
    ensemble = jnp.concatenate(ensemble, axis=1)
    values = jnp.concatenate(values, axis=1)
    weight = jnp.concatenate(weights, axis=1)
    mean_obs = jnp.mean(ensemble, axis=0, keepdims=True)
    anomaly = ensemble - mean_obs
    innovation = values - mean_obs
    scaled = anomaly * weight
    extended = jnp.concatenate(
        [anomaly, jnp.broadcast_to(innovation, (8, innovation.shape[1]))], axis=0
    )
    product = gram(two_terms(extended), two_terms(scaled))
    forcing = product[members : members + 1]
    row_id = lax.broadcasted_iota(jnp.int32, (members, 2 * members), 0)
    col_id = lax.broadcasted_iota(jnp.int32, (members, 2 * members), 1)
    identity = (row_id == col_id % members).astype(jnp.float32)
    system = (members - 1.0) * identity + jnp.concatenate([product[:members]] * 2, axis=1)
    scale = 0.5 * jnp.sum(
        jnp.sum(system * identity, axis=1, keepdims=True), axis=0, keepdims=True
    )
    root_part = system / scale
    factor = 1.5 * identity - 0.5 * root_part
    inverse = factor
    for sweep in range(1, SWEEPS):
        factor_terms = two_terms(factor)
        if sweep > 1:
            inverse = doubled_product(factor_terms, two_terms(inverse))
        root_part = doubled_product(two_terms(root_part), factor_terms)
        factor = 1.5 * identity - 0.5 * doubled_product(
            two_terms(inverse), two_terms(root_part)
        )
    inverse = doubled_product(two_terms(factor), two_terms(inverse))
    inv_sqrt = inverse[:, :members] / jnp.sqrt(scale)
    half = jnp.sum(inv_sqrt * forcing, axis=1, keepdims=True)
    mean_weight = jnp.sum(inv_sqrt * half, axis=0, keepdims=True)
    total = jnp.sqrt(jnp.float32(members - 1)) * inv_sqrt + mean_weight
    mixing = total - jnp.mean(total, axis=1, keepdims=True) + 1.0 / members
    mixing = mixing.astype(jnp.bfloat16)
    wide = members * levels
    spread = (
        lax.broadcasted_iota(jnp.int32, (wide, members), 0) // levels
        == lax.broadcasted_iota(jnp.int32, (wide, members), 1)
    ).astype(jnp.bfloat16)
    tall = jnp.dot(spread, mixing, preferred_element_type=jnp.float32).astype(jnp.bfloat16)
    full = lax.dot_general(
        tall, spread, (((1,), (1,)), ((), ())), preferred_element_type=jnp.float32
    )
    same = (
        lax.broadcasted_iota(jnp.int32, (wide, wide), 0) % levels
        == lax.broadcasted_iota(jnp.int32, (wide, wide), 1) % levels
    )
    mix_ref[...] = jnp.where(same, full, 0.0).astype(mix_ref.dtype)
    per = out_ref.shape[1] // (kinds * own)

    def mix_fields(from_ref, offset):
        def body(f, carry):
            begin = f * per * own
            rows = jnp.concatenate(
                [
                    from_ref[:, pl.ds(begin + c * own, own)].reshape(wide, LANES)
                    for c in range(per)
                ],
                axis=1,
            )
            mixed = jnp.dot(mix_ref[...], rows, preferred_element_type=jnp.float32)
            mixed = mixed.astype(out_ref.dtype)
            for c in range(per):
                out_ref[:, pl.ds(offset + begin + c * own, own)] = mixed[
                    :, c * LANES : (c + 1) * LANES
                ].reshape(sources, own, levels, LANES)
            return carry

        return body

    lax.fori_loop(0, ahead // (per * own), mix_fields(early_ref, 0), 0)
    lax.fori_loop(0, first // (per * own), mix_fields(x_ref, ahead), 0)


def observe(fields, values, precision, cells, count):
    own, kinds, levels, width = fields.shape
    tiles, slots = cells.shape
    whole = pl.BlockSpec((tiles, slots), lambda t: (0, 0))
    return pl.pallas_call(
        observe_kernel,
        grid=(tiles,),
        in_specs=[
            pl.BlockSpec((own, kinds, levels, TILE_CELLS), lambda t: (0, 0, 0, t)),
            whole,
            whole,
            whole,
            pl.BlockSpec(memory_space=pltpu.SMEM),
        ],
        out_specs=pl.BlockSpec((1, own + 4, slots), lambda t: (t, 0, 0)),
        out_shape=jax.ShapeDtypeStruct((tiles, own + 4, slots), jnp.float32),
        compiler_params=PARAMS,
        name="observe",
    )(fields, values, precision, cells, count)


def split(fields, parts, end):
    own, kinds, levels, width = fields.shape
    step = own * (width // parts // LANES)
    return pl.pallas_call(
        split_kernel,
        in_specs=[HBM],
        out_specs=HBM,
        out_shape=jax.ShapeDtypeStruct((parts, end * step, levels, LANES), fields.dtype),
        scratch_shapes=[
            pltpu.VMEM((end, own, levels, width), fields.dtype),
            pltpu.VMEM((end, parts, step, levels, LANES), fields.dtype),
            pltpu.SemaphoreType.DMA((end,)),
            pltpu.SemaphoreType.DMA((end,)),
        ],
        name="split",
    )(fields)


def join(pieces, shape):
    own, kinds, levels, width = shape
    return pl.pallas_call(
        join_kernel,
        in_specs=[VMEM],
        out_specs=HBM,
        out_shape=jax.ShapeDtypeStruct(shape, pieces.dtype),
        scratch_shapes=[
            pltpu.VMEM((kinds, own, levels, width), pieces.dtype),
            pltpu.SemaphoreType.DMA((kinds,)),
        ],
        compiler_params=PARAMS,
        name="join",
    )(pieces)


def pack(fields, parts, begin, above, here, below):
    own, kinds, levels, width = fields.shape
    blocks = own * (kinds - begin) * (width // parts // LANES) + 9
    return pl.pallas_call(
        functools.partial(pack_kernel, begin),
        in_specs=[VMEM] * 4,
        out_specs=VMEM,
        out_shape=jax.ShapeDtypeStruct((parts, blocks, levels, LANES), fields.dtype),
        compiler_params=PARAMS,
        name="pack",
    )(fields, above, here, below)


def analyse(tile, radius, early, late, above, here, below, kinds):
    parts, blocks, levels, lanes = early.shape
    wide = parts * (here.shape[1] - 4) * levels
    blocks += late.shape[1] - 9
    return pl.pallas_call(
        functools.partial(analyse_kernel, kinds),
        in_specs=[SMEM, SMEM] + [VMEM] * 5,
        out_specs=VMEM,
        out_shape=jax.ShapeDtypeStruct((parts, blocks, levels, lanes), early.dtype),
        scratch_shapes=[pltpu.VMEM((wide, wide), jnp.bfloat16)],
        compiler_params=PARAMS,
        name="analyse",
    )(tile, radius, early, late, above, here, below)


def on_device(background, obs_values, obs_precision, obs_cell, obs_count, radius):
    own, levels, kinds, _, width = background.shape
    parts = lax.axis_size("member")
    rows = lax.axis_size("space")
    share = parts * TILE_CELLS // width
    down = [(i, i + 1) for i in range(rows - 1)]
    up = [(i + 1, i) for i in range(rows - 1)]
    fields = background.transpose(0, 2, 3, 1, 4).reshape(own, kinds, levels, width)
    early = split(fields, parts, EARLY)
    early, fields = lax.optimization_barrier((early, fields))
    early = lax.all_to_all(early, "member", 0, 0)
    here = observe(fields, obs_values[0], obs_precision[0], obs_cell[0], obs_count)
    above = lax.ppermute(here, "space", down)
    below = lax.ppermute(here, "space", up)
    late = pack(fields, parts, EARLY, above, here, below)
    late = lax.all_to_all(late, "member", 0, 0)
    tile = (lax.axis_index("member") // share).astype(jnp.int32).reshape(1)
    mixed = analyse(tile, radius, early, late, above, here, below, kinds)
    out = join(lax.all_to_all(mixed, "member", 0, 0), fields.shape)
    return out.reshape(own, kinds, 1, levels, width).transpose(0, 3, 1, 2, 4)


def solution(mesh):
    return jax.shard_map(
        on_device,
        mesh=mesh,
        in_specs=(
            P("member", None, None, "space", None),
            P("space", None, None),
            P("space", None, None),
            P("space", None, None),
            P("space", None),
            P("space", None),
        ),
        out_specs=P("member", None, None, "space", None),
        check_vma=False,
    )
```

```python
import functools

import jax
import jax.numpy as jnp
from jax import lax
from jax.experimental import pallas as pl
from jax.experimental.pallas import tpu as pltpu
from jax.sharding import PartitionSpec as P

TILE_SIDE = 32
TILE_CELLS = 1024
SWEEPS = 6


LANES = 128
VMEM = pl.BlockSpec(memory_space=pltpu.VMEM)
SMEM = pl.BlockSpec(memory_space=pltpu.SMEM)
HBM = pl.BlockSpec(memory_space=pltpu.HBM)
PARAMS = pltpu.CompilerParams(vmem_limit_bytes=16 * 1024 * 1024)
EARLY = 4
SIDE = 4


def turned(core, index):
    return jnp.where(core == 0, index % SIDE * SIDE + index // SIDE, index)


def split_kernel(core_ref, x_ref, out_ref, held, made, in_sems, out_sems):
    kinds, own = held.shape[:2]
    width = held.shape[3]
    blocks = width // LANES
    parts, step = made.shape[1:3]
    per = blocks // parts
    loads = [
        pltpu.make_async_copy(x_ref.at[:, f], held.at[f], in_sems.at[f]) for f in range(kinds)
    ]
    stores = [
        pltpu.make_async_copy(
            made.at[f], out_ref.at[:, pl.ds(f * step, step)], out_sems.at[f]
        )
        for f in range(kinds)
    ]
    for load in loads:
        load.start()
    places = [turned(1 - core_ref[0], d) for d in range(parts)]
    for f in range(kinds):
        loads[f].wait()
        for c in range(blocks):
            for m in range(own):
                made[f, places[c // per], c % per * own + m] = held[
                    f, m, :, c * LANES : (c + 1) * LANES
                ]
        stores[f].start()
    for store in stores:
        store.wait()


def join_kernel(x_ref, out_ref, made, out_sems):
    kinds, own = made.shape[:2]
    width = made.shape[3]
    blocks = width // LANES
    per = blocks // x_ref.shape[0]
    stores = [
        pltpu.make_async_copy(made.at[f], out_ref.at[:, f], out_sems.at[f])
        for f in range(kinds)
    ]
    for f in range(kinds):
        for c in range(blocks):
            for m in range(own):
                made[f, m, :, c * LANES : (c + 1) * LANES] = x_ref[
                    c // per, (f * per + c % per) * own + m
                ]
        stores[f].start()
    for store in stores:
        store.wait()


def observe_kernel(x_ref, value_ref, precision_ref, cell_ref, count_ref, out_ref):
    own, fields, levels, cells = x_ref.shape
    slots = out_ref.shape[-1]
    tile = pl.program_id(0)
    cell = cell_ref[pl.ds(tile, 1), :]
    in_tile = cell % cells
    level_field = cell // cells
    wanted = (level_field % fields) * levels + level_field // fields
    onehot = lax.broadcasted_iota(jnp.int32, (cells, slots), 0) == in_tile
    rows = x_ref[...].reshape(own * fields * levels, cells)
    found = jnp.dot(rows, onehot.astype(rows.dtype), preferred_element_type=jnp.float32)
    found = found.reshape(own, fields * levels, slots)
    match = lax.broadcasted_iota(jnp.int32, (fields * levels, slots), 0) == wanted
    picked = jnp.sum(jnp.where(match[None], found, 0.0), axis=1)
    used = lax.broadcasted_iota(jnp.int32, (1, slots), 1) < count_ref[0, tile]
    active = jnp.where(used, precision_ref[pl.ds(tile, 1), :], 0.0)
    row_place = (in_tile // TILE_SIDE).astype(jnp.float32)
    col_place = (in_tile % TILE_SIDE).astype(jnp.float32)
    out_ref[0, 0:own, :] = picked
    out_ref[0, own : own + 1, :] = value_ref[pl.ds(tile, 1), :]
    out_ref[0, own + 1 : own + 2, :] = active
    out_ref[0, own + 2 : own + 3, :] = row_place
    out_ref[0, own + 3 : own + 4, :] = col_place


def pack_kernel(
    begin, core_ref, x_ref, inner_ref, own_ref, outer_ref, out_ref, above_ref, below_ref
):
    odd = core_ref[0] == 1
    places = [turned(1 - core_ref[0], d) for d in range(out_ref.shape[0])]
    inner, outer = inner_ref[...], outer_ref[...]
    above_ref[...] = jnp.where(odd, inner, outer)
    below_ref[...] = jnp.where(odd, outer, inner)
    parts, blocks, own, slots = out_ref.shape
    lane_blocks = x_ref.shape[3] // LANES
    per = lane_blocks // parts

    def copy_field(f, carry):
        for c in range(lane_blocks):
            for m in range(own):
                out_ref[places[c // per], ((f - begin) * per + c % per) * own + m] = x_ref[
                    m, f, :, c * LANES : (c + 1) * LANES
                ]
        return carry

    lax.fori_loop(begin, x_ref.shape[1], copy_field, 0)
    first = blocks - 9
    tiles = own_ref.shape[0]
    share = parts // tiles
    for a, rows_ref in enumerate((above_ref, own_ref, below_ref)):
        for t in range(tiles):
            rows = rows_ref[t, 0:own, :].astype(out_ref.dtype)
            for b in range(3):
                for h in range(share):
                    place = t + 1 - b
                    if 0 <= place < tiles:
                        out_ref[places[place * share + h], first + a * 3 + b] = rows
    blank = jnp.zeros((own, slots), out_ref.dtype)
    for h in range(share):
        for a in range(3):
            out_ref[places[h], first + a * 3] = blank
            out_ref[places[(tiles - 1) * share + h], first + a * 3 + 2] = blank


def two_terms(array):
    high = array.astype(jnp.bfloat16)
    return high, (array - high.astype(jnp.float32)).astype(jnp.bfloat16)


def gram(left, right):
    def product(a, b):
        return lax.dot_general(
            a, b, (((1,), (1,)), ((), ())), preferred_element_type=jnp.float32
        )

    return (
        product(left[0], right[0]) + product(left[0], right[1]) + product(left[1], right[0])
    )


def doubled_product(left, right):
    return jnp.dot(
        jnp.concatenate(left, axis=1),
        jnp.concatenate(right + right, axis=0),
        preferred_element_type=jnp.float32,
    )


def analyse_kernel(
    kinds, tile_ref, core_ref, radius_ref, x_ref, above_ref, own_ref, below_ref, out_ref, mix_ref
):
    tile = tile_ref[0]
    tiles = own_ref.shape[0]
    sources, _, levels, slots = x_ref.shape
    own = own_ref.shape[1] - 4
    first = x_ref.shape[1] - 9
    members = sources * own
    reach = radius_ref[0, tile].astype(jnp.float32)
    centre = 0.5 * TILE_SIDE - 0.5
    ensemble, values, weights = [], [], []
    for a, rows_ref in enumerate((above_ref, own_ref, below_ref)):
        for b in range(3):
            place = tile + b - 1
            inside = jnp.logical_and(place >= 0, place < tiles)
            held = jnp.clip(place, 0, tiles - 1)
            value, active, row, col = (
                rows_ref[held, own + i : own + i + 1, :] for i in range(4)
            )
            dist_row = row + ((a - 1) * TILE_SIDE - centre)
            dist_col = col + ((b - 1) * TILE_SIDE - centre)
            taper = jnp.maximum(
                1.0 - (dist_row * dist_row + dist_col * dist_col) / (reach * reach), 0.0
            )
            weights.append(jnp.where(inside, active, 0.0) * (taper * taper))
            values.append(value)
            ensemble.append(
                x_ref[:, first + a * 3 + b].astype(jnp.float32).reshape(members, slots)
            )
    ensemble = jnp.concatenate(ensemble, axis=1)
    values = jnp.concatenate(values, axis=1)
    weight = jnp.concatenate(weights, axis=1)
    mean_obs = jnp.mean(ensemble, axis=0, keepdims=True)
    anomaly = ensemble - mean_obs
    innovation = values - mean_obs
    scaled = anomaly * weight
    extended = jnp.concatenate(
        [anomaly, jnp.broadcast_to(innovation, (8, innovation.shape[1]))], axis=0
    )
    product = gram(two_terms(extended), two_terms(scaled))
    forcing = product[members : members + 1]
    row_id = lax.broadcasted_iota(jnp.int32, (members, 2 * members), 0)
    col_id = lax.broadcasted_iota(jnp.int32, (members, 2 * members), 1)
    identity = (row_id == col_id % members).astype(jnp.float32)
    system = (members - 1.0) * identity + jnp.concatenate([product[:members]] * 2, axis=1)
    scale = 0.5 * jnp.sum(
        jnp.sum(system * identity, axis=1, keepdims=True), axis=0, keepdims=True
    )
    root_part = system / scale
    factor = 1.5 * identity - 0.5 * root_part
    inverse = factor
    for sweep in range(1, SWEEPS):
        factor_terms = two_terms(factor)
        if sweep > 1:
            inverse = doubled_product(factor_terms, two_terms(inverse))
        root_part = doubled_product(two_terms(root_part), factor_terms)
        factor = 1.5 * identity - 0.5 * doubled_product(
            two_terms(inverse), two_terms(root_part)
        )
    inverse = doubled_product(two_terms(factor), two_terms(inverse))
    inv_sqrt = inverse[:, :members] / jnp.sqrt(scale)
    half = jnp.sum(inv_sqrt * forcing, axis=1, keepdims=True)
    mean_weight = jnp.sum(inv_sqrt * half, axis=0, keepdims=True)
    total = jnp.sqrt(jnp.float32(members - 1)) * inv_sqrt + mean_weight
    mixing = total - jnp.mean(total, axis=1, keepdims=True) + 1.0 / members
    mixing = mixing.astype(jnp.bfloat16)
    wide = members * levels
    spread = (
        lax.broadcasted_iota(jnp.int32, (wide, members), 0) // levels
        == lax.broadcasted_iota(jnp.int32, (wide, members), 1)
    ).astype(jnp.bfloat16)
    device = lax.broadcasted_iota(jnp.int32, (wide, members), 0) // (own * levels)
    row_member = turned(core_ref[0], device) * own + (
        lax.broadcasted_iota(jnp.int32, (wide, members), 0) // levels % own
    )
    chosen = (
        row_member == lax.broadcasted_iota(jnp.int32, (wide, members), 1)
    ).astype(jnp.bfloat16)
    tall = jnp.dot(chosen, mixing, preferred_element_type=jnp.float32).astype(jnp.bfloat16)
    full = lax.dot_general(
        tall, spread, (((1,), (1,)), ((), ())), preferred_element_type=jnp.float32
    )
    same = (
        lax.broadcasted_iota(jnp.int32, (wide, wide), 0) % levels
        == lax.broadcasted_iota(jnp.int32, (wide, wide), 1) % levels
    )
    mix_ref[...] = jnp.where(same, full, 0.0).astype(mix_ref.dtype)
    per = out_ref.shape[1] // (kinds * own)

    def body(f, carry):
        begin = f * per * own
        rows = jnp.concatenate(
            [x_ref[:, pl.ds(begin + c * own, own)].reshape(wide, LANES) for c in range(per)],
            axis=1,
        )
        mixed = jnp.dot(mix_ref[...], rows, preferred_element_type=jnp.float32)
        mixed = mixed.astype(out_ref.dtype)
        for c in range(per):
            out_ref[:, pl.ds(begin + c * own, own)] = mixed[
                :, c * LANES : (c + 1) * LANES
            ].reshape(sources, own, levels, LANES)
        return carry

    lax.fori_loop(0, kinds, body, 0)


def observe(fields, values, precision, cells, count):
    own, kinds, levels, width = fields.shape
    tiles, slots = cells.shape
    whole = pl.BlockSpec((tiles, slots), lambda t: (0, 0))
    return pl.pallas_call(
        observe_kernel,
        grid=(tiles,),
        in_specs=[
            pl.BlockSpec((own, kinds, levels, TILE_CELLS), lambda t: (0, 0, 0, t)),
            whole,
            whole,
            whole,
            pl.BlockSpec(memory_space=pltpu.SMEM),
        ],
        out_specs=pl.BlockSpec((1, own + 4, slots), lambda t: (t, 0, 0)),
        out_shape=jax.ShapeDtypeStruct((tiles, own + 4, slots), jnp.float32),
        compiler_params=PARAMS,
        name="observe",
    )(fields, values, precision, cells, count)


def split(core, fields, parts, end):
    own, kinds, levels, width = fields.shape
    step = own * (width // parts // LANES)
    return pl.pallas_call(
        split_kernel,
        in_specs=[SMEM, HBM],
        out_specs=HBM,
        out_shape=jax.ShapeDtypeStruct((parts, end * step, levels, LANES), fields.dtype),
        scratch_shapes=[
            pltpu.VMEM((end, own, levels, width), fields.dtype),
            pltpu.VMEM((end, parts, step, levels, LANES), fields.dtype),
            pltpu.SemaphoreType.DMA((end,)),
            pltpu.SemaphoreType.DMA((end,)),
        ],
        name="split",
    )(core, fields)


def join(pieces, shape):
    own, kinds, levels, width = shape
    return pl.pallas_call(
        join_kernel,
        in_specs=[VMEM],
        out_specs=HBM,
        out_shape=jax.ShapeDtypeStruct(shape, pieces.dtype),
        scratch_shapes=[
            pltpu.VMEM((kinds, own, levels, width), pieces.dtype),
            pltpu.SemaphoreType.DMA((kinds,)),
        ],
        compiler_params=PARAMS,
        name="join",
    )(pieces)


def pack(core, fields, parts, begin, inner, here, outer):
    own, kinds, levels, width = fields.shape
    blocks = own * (kinds - begin) * (width // parts // LANES) + 9
    small = jax.ShapeDtypeStruct(here.shape, here.dtype)
    return pl.pallas_call(
        functools.partial(pack_kernel, begin),
        in_specs=[SMEM] + [VMEM] * 4,
        out_specs=[VMEM] * 3,
        out_shape=[
            jax.ShapeDtypeStruct((parts, blocks, levels, LANES), fields.dtype),
            small,
            small,
        ],
        compiler_params=PARAMS,
        name="pack",
    )(core, fields, inner, here, outer)


def analyse(tile, core, radius, pieces, above, here, below, kinds):
    parts, blocks, levels, lanes = pieces.shape
    wide = parts * (here.shape[1] - 4) * levels
    return pl.pallas_call(
        functools.partial(analyse_kernel, kinds),
        in_specs=[SMEM] * 3 + [VMEM] * 4,
        out_specs=VMEM,
        out_shape=jax.ShapeDtypeStruct((parts, blocks - 9, levels, lanes), pieces.dtype),
        scratch_shapes=[pltpu.VMEM((wide, wide), jnp.bfloat16)],
        compiler_params=PARAMS,
        name="analyse",
    )(tile, core, radius, pieces, above, here, below)


def hop_groups(rows):
    def group(row, fixed, along_y):
        members = [
            i * SIDE + fixed if along_y else fixed * SIDE + i for i in range(SIDE)
        ]
        return [member * rows + row for member in members]

    return [
        [group(r, i, r % 2 == hop) for r in range(rows) for i in range(SIDE)]
        for hop in range(2)
    ]


def on_device(background, obs_values, obs_precision, obs_cell, obs_count, radius):
    own, levels, kinds, _, width = background.shape
    parts = lax.axis_size("member")
    rows = lax.axis_size("space")
    share = parts * TILE_CELLS // width
    pairs = [(i, i + 1) for i in range(rows - 1)]
    swap = [pairs[0::2], pairs[1::2]]
    swap = [one + [(j, i) for i, j in one] for one in swap]
    fields = background.transpose(0, 2, 3, 1, 4).reshape(own, kinds, levels, width)
    both = ("member", "space")
    groups = hop_groups(rows)
    core = (lax.axis_index("space") % 2).astype(jnp.int32).reshape(1)
    early = split(core, fields, parts, EARLY)
    early, fields = lax.optimization_barrier((early, fields))
    early = early.reshape((SIDE, SIDE) + early.shape[1:])
    early = lax.all_to_all(early, both, 0, 0, axis_index_groups=groups[0])
    here = observe(fields, obs_values[0], obs_precision[0], obs_cell[0], obs_count)
    inner = lax.ppermute(here, "space", swap[0])
    outer = lax.ppermute(here, "space", swap[1])
    late, above, below = pack(core, fields, parts, EARLY, inner, here, outer)
    late = late.reshape((SIDE, SIDE) + late.shape[1:])
    late, early = lax.optimization_barrier((late, early))
    late = lax.all_to_all(late, both, 0, 0, axis_index_groups=groups[0])
    pieces = jnp.concatenate([early, late], axis=2).swapaxes(0, 1)
    pieces = lax.all_to_all(pieces, both, 0, 0, axis_index_groups=groups[1])
    pieces = pieces.reshape((parts,) + pieces.shape[2:])
    tile = (lax.axis_index("member") // share).astype(jnp.int32).reshape(1)
    mixed = analyse(tile, core, radius, pieces, above, here, below, kinds)
    out = join(lax.all_to_all(mixed, "member", 0, 0), fields.shape)
    return out.reshape(own, kinds, 1, levels, width).transpose(0, 3, 1, 2, 4)


def solution(mesh):
    return jax.shard_map(
        on_device,
        mesh=mesh,
        in_specs=(
            P("member", None, None, "space", None),
            P("space", None, None),
            P("space", None, None),
            P("space", None, None),
            P("space", None),
            P("space", None),
        ),
        out_specs=P("member", None, None, "space", None),
        check_vma=False,
    )
```

```python
import functools

import jax
import jax.numpy as jnp
from jax import lax
from jax.experimental import pallas as pl
from jax.experimental.pallas import tpu as pltpu
from jax.sharding import PartitionSpec as P

TILE_SIDE = 32
TILE_CELLS = 1024
SWEEPS = 6


LANES = 128
VMEM = pl.BlockSpec(memory_space=pltpu.VMEM)
SMEM = pl.BlockSpec(memory_space=pltpu.SMEM)
HBM = pl.BlockSpec(memory_space=pltpu.HBM)
ANY = pl.BlockSpec(memory_space=pl.ANY)
PARAMS = pltpu.CompilerParams(vmem_limit_bytes=16 * 1024 * 1024)
EARLY = 4
SIDE = 4


def turned(core, index):
    return jnp.where(core == 0, index % SIDE * SIDE + index // SIDE, index)


def split_kernel(core_ref, x_ref, out_ref, held, made, in_sems, out_sems):
    kinds, own = held.shape[:2]
    width = held.shape[3]
    blocks = width // LANES
    parts, step = made.shape[1:3]
    per = blocks // parts
    loads = [
        pltpu.make_async_copy(x_ref.at[:, f], held.at[f], in_sems.at[f]) for f in range(kinds)
    ]
    stores = [
        pltpu.make_async_copy(
            made.at[f], out_ref.at[:, pl.ds(f * step, step)], out_sems.at[f]
        )
        for f in range(kinds)
    ]
    for load in loads:
        load.start()
    places = [turned(1 - core_ref[0], d) for d in range(parts)]
    for f in range(kinds):
        loads[f].wait()
        for c in range(blocks):
            for m in range(own):
                made[f, places[c // per], c % per * own + m] = held[
                    f, m, :, c * LANES : (c + 1) * LANES
                ]
        stores[f].start()
    for store in stores:
        store.wait()


def join_kernel(x_ref, out_ref, made, out_sems):
    kinds, own = made.shape[:2]
    width = made.shape[3]
    blocks = width // LANES
    per = blocks // x_ref.shape[0]
    stores = [
        pltpu.make_async_copy(made.at[f], out_ref.at[:, f], out_sems.at[f])
        for f in range(kinds)
    ]
    for f in range(kinds):
        for c in range(blocks):
            for m in range(own):
                made[f, m, :, c * LANES : (c + 1) * LANES] = x_ref[
                    c // per, (f * per + c % per) * own + m
                ]
        stores[f].start()
    for store in stores:
        store.wait()


def observe_kernel(x_ref, value_ref, precision_ref, cell_ref, count_ref, out_ref):
    own, fields, levels, cells = x_ref.shape
    slots = out_ref.shape[-1]
    tile = pl.program_id(0)
    cell = cell_ref[pl.ds(tile, 1), :]
    in_tile = cell % cells
    level_field = cell // cells
    wanted = (level_field % fields) * levels + level_field // fields
    onehot = lax.broadcasted_iota(jnp.int32, (cells, slots), 0) == in_tile
    rows = x_ref[...].reshape(own * fields * levels, cells)
    found = jnp.dot(rows, onehot.astype(rows.dtype), preferred_element_type=jnp.float32)
    found = found.reshape(own, fields * levels, slots)
    match = lax.broadcasted_iota(jnp.int32, (fields * levels, slots), 0) == wanted
    picked = jnp.sum(jnp.where(match[None], found, 0.0), axis=1)
    used = lax.broadcasted_iota(jnp.int32, (1, slots), 1) < count_ref[0, tile]
    active = jnp.where(used, precision_ref[pl.ds(tile, 1), :], 0.0)
    row_place = (in_tile // TILE_SIDE).astype(jnp.float32)
    col_place = (in_tile % TILE_SIDE).astype(jnp.float32)
    out_ref[0, 0:own, :] = picked
    out_ref[0, own : own + 1, :] = value_ref[pl.ds(tile, 1), :]
    out_ref[0, own + 1 : own + 2, :] = active
    out_ref[0, own + 2 : own + 3, :] = row_place
    out_ref[0, own + 3 : own + 4, :] = col_place


def pack_kernel(
    begin, core_ref, x_ref, inner_ref, own_ref, outer_ref, out_ref, above_ref, below_ref
):
    odd = core_ref[0] == 1
    places = [turned(1 - core_ref[0], d) for d in range(out_ref.shape[0])]
    inner, outer = inner_ref[...], outer_ref[...]
    above_ref[...] = jnp.where(odd, inner, outer)
    below_ref[...] = jnp.where(odd, outer, inner)
    parts, blocks, own, slots = out_ref.shape
    lane_blocks = x_ref.shape[3] // LANES
    per = lane_blocks // parts

    def copy_field(f, carry):
        for c in range(lane_blocks):
            for m in range(own):
                out_ref[places[c // per], ((f - begin) * per + c % per) * own + m] = x_ref[
                    m, f, :, c * LANES : (c + 1) * LANES
                ]
        return carry

    lax.fori_loop(begin, x_ref.shape[1], copy_field, 0)
    first = blocks - 9
    tiles = own_ref.shape[0]
    share = parts // tiles
    for a, rows_ref in enumerate((above_ref, own_ref, below_ref)):
        for t in range(tiles):
            rows = rows_ref[t, 0:own, :].astype(out_ref.dtype)
            for b in range(3):
                for h in range(share):
                    place = t + 1 - b
                    if 0 <= place < tiles:
                        out_ref[places[place * share + h], first + a * 3 + b] = rows
    blank = jnp.zeros((own, slots), out_ref.dtype)
    for h in range(share):
        for a in range(3):
            out_ref[places[h], first + a * 3] = blank
            out_ref[places[(tiles - 1) * share + h], first + a * 3 + 2] = blank


def two_terms(array):
    high = array.astype(jnp.bfloat16)
    return high, (array - high.astype(jnp.float32)).astype(jnp.bfloat16)


def gram(left, right):
    def product(a, b):
        return lax.dot_general(
            a, b, (((1,), (1,)), ((), ())), preferred_element_type=jnp.float32
        )

    return (
        product(left[0], right[0]) + product(left[0], right[1]) + product(left[1], right[0])
    )


def doubled_product(left, right):
    return jnp.dot(
        jnp.concatenate(left, axis=1),
        jnp.concatenate(right + right, axis=0),
        preferred_element_type=jnp.float32,
    )


def analyse_kernel(
    kinds, tile_ref, core_ref, radius_ref, x_ref, above_ref, own_ref, below_ref, out_ref, mix_ref
):
    tile = tile_ref[0]
    tiles = own_ref.shape[0]
    sources, _, levels, slots = x_ref.shape
    own = own_ref.shape[1] - 4
    first = x_ref.shape[1] - 9
    members = sources * own
    reach = radius_ref[0, tile].astype(jnp.float32)
    centre = 0.5 * TILE_SIDE - 0.5
    ensemble, values, weights = [], [], []
    for a, rows_ref in enumerate((above_ref, own_ref, below_ref)):
        for b in range(3):
            place = tile + b - 1
            inside = jnp.logical_and(place >= 0, place < tiles)
            held = jnp.clip(place, 0, tiles - 1)
            value, active, row, col = (
                rows_ref[held, own + i : own + i + 1, :] for i in range(4)
            )
            dist_row = row + ((a - 1) * TILE_SIDE - centre)
            dist_col = col + ((b - 1) * TILE_SIDE - centre)
            taper = jnp.maximum(
                1.0 - (dist_row * dist_row + dist_col * dist_col) / (reach * reach), 0.0
            )
            weights.append(jnp.where(inside, active, 0.0) * (taper * taper))
            values.append(value)
            ensemble.append(
                x_ref[:, first + a * 3 + b].astype(jnp.float32).reshape(members, slots)
            )
    ensemble = jnp.concatenate(ensemble, axis=1)
    values = jnp.concatenate(values, axis=1)
    weight = jnp.concatenate(weights, axis=1)
    mean_obs = jnp.mean(ensemble, axis=0, keepdims=True)
    anomaly = ensemble - mean_obs
    innovation = values - mean_obs
    scaled = anomaly * weight
    extended = jnp.concatenate(
        [anomaly, jnp.broadcast_to(innovation, (8, innovation.shape[1]))], axis=0
    )
    product = gram(two_terms(extended), two_terms(scaled))
    forcing = product[members : members + 1]
    row_id = lax.broadcasted_iota(jnp.int32, (members, 2 * members), 0)
    col_id = lax.broadcasted_iota(jnp.int32, (members, 2 * members), 1)
    identity = (row_id == col_id % members).astype(jnp.float32)
    system = (members - 1.0) * identity + jnp.concatenate([product[:members]] * 2, axis=1)
    scale = 0.5 * jnp.sum(
        jnp.sum(system * identity, axis=1, keepdims=True), axis=0, keepdims=True
    )
    root_part = system / scale
    factor = 1.5 * identity - 0.5 * root_part
    inverse = factor
    for sweep in range(1, SWEEPS):
        factor_terms = two_terms(factor)
        if sweep > 1:
            inverse = doubled_product(factor_terms, two_terms(inverse))
        root_part = doubled_product(two_terms(root_part), factor_terms)
        factor = 1.5 * identity - 0.5 * doubled_product(
            two_terms(inverse), two_terms(root_part)
        )
    inverse = doubled_product(two_terms(factor), two_terms(inverse))
    inv_sqrt = inverse[:, :members] / jnp.sqrt(scale)
    half = jnp.sum(inv_sqrt * forcing, axis=1, keepdims=True)
    mean_weight = jnp.sum(inv_sqrt * half, axis=0, keepdims=True)
    total = jnp.sqrt(jnp.float32(members - 1)) * inv_sqrt + mean_weight
    mixing = total - jnp.mean(total, axis=1, keepdims=True) + 1.0 / members
    mixing = mixing.astype(jnp.bfloat16)
    wide = members * levels
    spread = (
        lax.broadcasted_iota(jnp.int32, (wide, members), 0) // levels
        == lax.broadcasted_iota(jnp.int32, (wide, members), 1)
    ).astype(jnp.bfloat16)
    device = lax.broadcasted_iota(jnp.int32, (wide, members), 0) // (own * levels)
    row_member = turned(core_ref[0], device) * own + (
        lax.broadcasted_iota(jnp.int32, (wide, members), 0) // levels % own
    )
    chosen = (
        row_member == lax.broadcasted_iota(jnp.int32, (wide, members), 1)
    ).astype(jnp.bfloat16)
    tall = jnp.dot(chosen, mixing, preferred_element_type=jnp.float32).astype(jnp.bfloat16)
    full = lax.dot_general(
        tall, spread, (((1,), (1,)), ((), ())), preferred_element_type=jnp.float32
    )
    same = (
        lax.broadcasted_iota(jnp.int32, (wide, wide), 0) % levels
        == lax.broadcasted_iota(jnp.int32, (wide, wide), 1) % levels
    )
    mix_ref[...] = jnp.where(same, full, 0.0).astype(mix_ref.dtype)
    per = out_ref.shape[1] // (kinds * own)

    def body(f, carry):
        begin = f * per * own
        rows = jnp.concatenate(
            [x_ref[:, pl.ds(begin + c * own, own)].reshape(wide, LANES) for c in range(per)],
            axis=1,
        )
        mixed = jnp.dot(mix_ref[...], rows, preferred_element_type=jnp.float32)
        mixed = mixed.astype(out_ref.dtype)
        for c in range(per):
            out_ref[:, pl.ds(begin + c * own, own)] = mixed[
                :, c * LANES : (c + 1) * LANES
            ].reshape(sources, own, levels, LANES)
        return carry

    lax.fori_loop(0, kinds, body, 0)


def observe(fields, values, precision, cells, count):
    own, kinds, levels, width = fields.shape
    tiles, slots = cells.shape
    whole = pl.BlockSpec((tiles, slots), lambda t: (0, 0))
    return pl.pallas_call(
        observe_kernel,
        grid=(tiles,),
        in_specs=[
            pl.BlockSpec((own, kinds, levels, TILE_CELLS), lambda t: (0, 0, 0, t)),
            whole,
            whole,
            whole,
            pl.BlockSpec(memory_space=pltpu.SMEM),
        ],
        out_specs=pl.BlockSpec((1, own + 4, slots), lambda t: (t, 0, 0)),
        out_shape=jax.ShapeDtypeStruct((tiles, own + 4, slots), jnp.float32),
        compiler_params=PARAMS,
        name="observe",
    )(fields, values, precision, cells, count)


def split(core, fields, parts, end):
    own, kinds, levels, width = fields.shape
    step = own * (width // parts // LANES)
    return pl.pallas_call(
        split_kernel,
        in_specs=[SMEM, HBM],
        out_specs=HBM,
        out_shape=jax.ShapeDtypeStruct((parts, end * step, levels, LANES), fields.dtype),
        scratch_shapes=[
            pltpu.VMEM((end, own, levels, width), fields.dtype),
            pltpu.VMEM((end, parts, step, levels, LANES), fields.dtype),
            pltpu.SemaphoreType.DMA((end,)),
            pltpu.SemaphoreType.DMA((end,)),
        ],
        name="split",
    )(core, fields)


def join(pieces, shape):
    own, kinds, levels, width = shape
    return pl.pallas_call(
        join_kernel,
        in_specs=[VMEM],
        out_specs=HBM,
        out_shape=jax.ShapeDtypeStruct(shape, pieces.dtype),
        scratch_shapes=[
            pltpu.VMEM((kinds, own, levels, width), pieces.dtype),
            pltpu.SemaphoreType.DMA((kinds,)),
        ],
        compiler_params=PARAMS,
        name="join",
    )(pieces)


def pack(core, fields, parts, begin, inner, here, outer):
    own, kinds, levels, width = fields.shape
    blocks = own * (kinds - begin) * (width // parts // LANES) + 9
    small = jax.ShapeDtypeStruct(here.shape, here.dtype)
    return pl.pallas_call(
        functools.partial(pack_kernel, begin),
        in_specs=[SMEM] + [VMEM] * 4,
        out_specs=[VMEM] * 3,
        out_shape=[
            jax.ShapeDtypeStruct((parts, blocks, levels, LANES), fields.dtype),
            small,
            small,
        ],
        compiler_params=PARAMS,
        name="pack",
    )(core, fields, inner, here, outer)


def analyse(tile, core, radius, pieces, above, here, below, kinds):
    parts, blocks, levels, lanes = pieces.shape
    wide = parts * (here.shape[1] - 4) * levels
    return pl.pallas_call(
        functools.partial(analyse_kernel, kinds),
        in_specs=[SMEM] * 3 + [VMEM] * 4,
        out_specs=VMEM,
        out_shape=jax.ShapeDtypeStruct((parts, blocks - 9, levels, lanes), pieces.dtype),
        scratch_shapes=[pltpu.VMEM((wide, wide), jnp.bfloat16)],
        compiler_params=PARAMS,
        name="analyse",
    )(tile, core, radius, pieces, above, here, below)


def merge_kernel(early_ref, late_ref, out_ref, sems):
    ahead, rest = early_ref.shape[2], late_ref.shape[2]
    copies = []
    for i in range(SIDE):
        for j in range(SIDE):
            copies.append(
                pltpu.make_async_copy(
                    early_ref.at[i, j], out_ref.at[j, i, pl.ds(0, ahead)], sems.at[0, i, j]
                )
            )
            copies.append(
                pltpu.make_async_copy(
                    late_ref.at[i, j], out_ref.at[j, i, pl.ds(ahead, rest)], sems.at[1, i, j]
                )
            )
    for copy in copies:
        copy.start()
    for copy in copies:
        copy.wait()


def merge(early, late):
    shape = early.shape[:2] + (early.shape[2] + late.shape[2],) + early.shape[3:]
    return pl.pallas_call(
        merge_kernel,
        in_specs=[ANY, ANY],
        out_specs=ANY,
        out_shape=jax.ShapeDtypeStruct(shape, early.dtype),
        scratch_shapes=[pltpu.SemaphoreType.DMA((2, SIDE, SIDE))],
        compiler_params=PARAMS,
        name="merge",
    )(early, late)


def hop_groups(rows):
    def group(row, fixed, along_y):
        members = [
            i * SIDE + fixed if along_y else fixed * SIDE + i for i in range(SIDE)
        ]
        return [member * rows + row for member in members]

    return [
        [group(r, i, r % 2 == hop) for r in range(rows) for i in range(SIDE)]
        for hop in range(2)
    ]


def on_device(background, obs_values, obs_precision, obs_cell, obs_count, radius):
    own, levels, kinds, _, width = background.shape
    parts = lax.axis_size("member")
    rows = lax.axis_size("space")
    share = parts * TILE_CELLS // width
    pairs = [(i, i + 1) for i in range(rows - 1)]
    swap = [pairs[0::2], pairs[1::2]]
    swap = [one + [(j, i) for i, j in one] for one in swap]
    fields = background.transpose(0, 2, 3, 1, 4).reshape(own, kinds, levels, width)
    both = ("member", "space")
    groups = hop_groups(rows)
    core = (lax.axis_index("space") % 2).astype(jnp.int32).reshape(1)
    early = split(core, fields, parts, EARLY)
    early, fields = lax.optimization_barrier((early, fields))
    early = early.reshape((SIDE, SIDE) + early.shape[1:])
    early = lax.all_to_all(early, both, 0, 0, axis_index_groups=groups[0])
    here = observe(fields, obs_values[0], obs_precision[0], obs_cell[0], obs_count)
    inner = lax.ppermute(here, "space", swap[0])
    outer = lax.ppermute(here, "space", swap[1])
    late, above, below = pack(core, fields, parts, EARLY, inner, here, outer)
    late = late.reshape((SIDE, SIDE) + late.shape[1:])
    late, early = lax.optimization_barrier((late, early))
    late = lax.all_to_all(late, both, 0, 0, axis_index_groups=groups[0])
    pieces = merge(early, late)
    pieces = lax.all_to_all(pieces, both, 0, 0, axis_index_groups=groups[1])
    pieces = pieces.reshape((parts,) + pieces.shape[2:])
    tile = (lax.axis_index("member") // share).astype(jnp.int32).reshape(1)
    mixed = analyse(tile, core, radius, pieces, above, here, below, kinds)
    out = join(lax.all_to_all(mixed, "member", 0, 0), fields.shape)
    return out.reshape(own, kinds, 1, levels, width).transpose(0, 3, 1, 2, 4)


def solution(mesh):
    return jax.shard_map(
        on_device,
        mesh=mesh,
        in_specs=(
            P("member", None, None, "space", None),
            P("space", None, None),
            P("space", None, None),
            P("space", None, None),
            P("space", None),
            P("space", None),
        ),
        out_specs=P("member", None, None, "space", None),
        check_vma=False,
    )
```

```python
import functools

import jax
import jax.numpy as jnp
from jax import lax
from jax.experimental import pallas as pl
from jax.experimental.pallas import tpu as pltpu
from jax.sharding import PartitionSpec as P

TILE_SIDE = 32
TILE_CELLS = 1024
SWEEPS = 6


LANES = 128
VMEM = pl.BlockSpec(memory_space=pltpu.VMEM)
SMEM = pl.BlockSpec(memory_space=pltpu.SMEM)
HBM = pl.BlockSpec(memory_space=pltpu.HBM)
ANY = pl.BlockSpec(memory_space=pl.ANY)
PARAMS = pltpu.CompilerParams(vmem_limit_bytes=16 * 1024 * 1024)
EARLY = 3
SIDE = 4


def turned(core, index):
    return jnp.where(core == 0, index % SIDE * SIDE + index // SIDE, index)


def split_kernel(core_ref, x_ref, out_ref, held, made, in_sems, out_sems):
    kinds, own = held.shape[:2]
    width = held.shape[3]
    blocks = width // LANES
    parts, step = made.shape[1:3]
    per = blocks // parts
    loads = [
        pltpu.make_async_copy(x_ref.at[:, f], held.at[f], in_sems.at[f]) for f in range(kinds)
    ]
    stores = [
        pltpu.make_async_copy(
            made.at[f], out_ref.at[:, pl.ds(f * step, step)], out_sems.at[f]
        )
        for f in range(kinds)
    ]
    for load in loads:
        load.start()
    places = [turned(1 - core_ref[0], d) for d in range(parts)]
    for f in range(kinds):
        loads[f].wait()
        for c in range(blocks):
            for m in range(own):
                made[f, places[c // per], c % per * own + m] = held[
                    f, m, :, c * LANES : (c + 1) * LANES
                ]
        stores[f].start()
    for store in stores:
        store.wait()


def join_kernel(x_ref, out_ref, made, out_sems):
    kinds, own = made.shape[:2]
    width = made.shape[3]
    blocks = width // LANES
    per = blocks // x_ref.shape[0]
    stores = [
        pltpu.make_async_copy(made.at[f], out_ref.at[:, f], out_sems.at[f])
        for f in range(kinds)
    ]
    for f in range(kinds):
        for c in range(blocks):
            for m in range(own):
                made[f, m, :, c * LANES : (c + 1) * LANES] = x_ref[
                    c // per, (f * per + c % per) * own + m
                ]
        stores[f].start()
    for store in stores:
        store.wait()


def observe_kernel(x_ref, value_ref, precision_ref, cell_ref, count_ref, out_ref):
    own, kinds, levels, width = x_ref.shape
    tiles, slots = cell_ref.shape
    cells = width // tiles
    cell = cell_ref[...]
    in_tile = cell % cells
    level_field = cell // cells
    wanted = (level_field % kinds) * levels + level_field // kinds
    row_place = (in_tile // TILE_SIDE).astype(jnp.float32)
    col_place = (in_tile % TILE_SIDE).astype(jnp.float32)
    place_id = lax.broadcasted_iota(jnp.int32, (cells, slots), 0)
    field_id = lax.broadcasted_iota(jnp.int32, (kinds * levels, slots), 0)
    slot_id = lax.broadcasted_iota(jnp.int32, (1, slots), 1)
    for tile in range(tiles):
        at = slice(tile, tile + 1)
        onehot = (place_id == in_tile[at]).astype(x_ref.dtype)
        rows = x_ref[:, :, :, tile * cells : (tile + 1) * cells].reshape(-1, cells)
        found = jnp.dot(rows, onehot, preferred_element_type=jnp.float32)
        found = found.reshape(own, kinds * levels, slots)
        match = field_id == wanted[at]
        out_ref[tile, 0:own, :] = jnp.sum(jnp.where(match[None], found, 0.0), axis=1)
        out_ref[tile, own : own + 1, :] = value_ref[at, :]
        out_ref[tile, own + 1 : own + 2, :] = jnp.where(
            slot_id < count_ref[0, tile], precision_ref[at, :], 0.0
        )
        out_ref[tile, own + 2 : own + 3, :] = row_place[at]
        out_ref[tile, own + 3 : own + 4, :] = col_place[at]


def pack_kernel(
    begin, core_ref, x_ref, inner_ref, own_ref, outer_ref, out_ref, above_ref, below_ref
):
    odd = core_ref[0] == 1
    places = [turned(1 - core_ref[0], d) for d in range(out_ref.shape[0])]
    inner, outer = inner_ref[...], outer_ref[...]
    above_ref[...] = jnp.where(odd, inner, outer)
    below_ref[...] = jnp.where(odd, outer, inner)
    parts, blocks, own, slots = out_ref.shape
    lane_blocks = x_ref.shape[3] // LANES
    per = lane_blocks // parts

    def copy_field(f, carry):
        for c in range(lane_blocks):
            for m in range(own):
                out_ref[places[c // per], ((f - begin) * per + c % per) * own + m] = x_ref[
                    m, f, :, c * LANES : (c + 1) * LANES
                ]
        return carry

    lax.fori_loop(begin, x_ref.shape[1], copy_field, 0)
    first = blocks - 9
    tiles = own_ref.shape[0]
    share = parts // tiles
    for a, rows_ref in enumerate((above_ref, own_ref, below_ref)):
        for t in range(tiles):
            rows = rows_ref[t, 0:own, :].astype(out_ref.dtype)
            for b in range(3):
                for h in range(share):
                    place = t + 1 - b
                    if 0 <= place < tiles:
                        out_ref[places[place * share + h], first + a * 3 + b] = rows
    blank = jnp.zeros((own, slots), out_ref.dtype)
    for h in range(share):
        for a in range(3):
            out_ref[places[h], first + a * 3] = blank
            out_ref[places[(tiles - 1) * share + h], first + a * 3 + 2] = blank


def two_terms(array):
    high = array.astype(jnp.bfloat16)
    return high, (array - high.astype(jnp.float32)).astype(jnp.bfloat16)


def gram(left, right):
    def product(a, b):
        return lax.dot_general(
            a, b, (((1,), (1,)), ((), ())), preferred_element_type=jnp.float32
        )

    return (
        product(left[0], right[0]) + product(left[0], right[1]) + product(left[1], right[0])
    )


def doubled_product(left, right):
    return jnp.dot(
        jnp.concatenate(left, axis=1),
        jnp.concatenate(right + right, axis=0),
        preferred_element_type=jnp.float32,
    )


def analyse_kernel(
    kinds, tile_ref, core_ref, radius_ref, x_ref, above_ref, own_ref, below_ref, out_ref, mix_ref
):
    tile = tile_ref[0]
    tiles = own_ref.shape[0]
    sources, _, levels, slots = x_ref.shape
    own = own_ref.shape[1] - 4
    first = x_ref.shape[1] - 9
    members = sources * own
    reach = radius_ref[0, tile].astype(jnp.float32)
    centre = 0.5 * TILE_SIDE - 0.5
    ensemble, values, weights = [], [], []
    for a, rows_ref in enumerate((above_ref, own_ref, below_ref)):
        for b in range(3):
            place = tile + b - 1
            inside = jnp.logical_and(place >= 0, place < tiles)
            held = jnp.clip(place, 0, tiles - 1)
            value, active, row, col = (
                rows_ref[held, own + i : own + i + 1, :] for i in range(4)
            )
            dist_row = row + ((a - 1) * TILE_SIDE - centre)
            dist_col = col + ((b - 1) * TILE_SIDE - centre)
            taper = jnp.maximum(
                1.0 - (dist_row * dist_row + dist_col * dist_col) / (reach * reach), 0.0
            )
            weights.append(jnp.where(inside, active, 0.0) * (taper * taper))
            values.append(value)
            ensemble.append(
                x_ref[:, first + a * 3 + b].astype(jnp.float32).reshape(members, slots)
            )
    ensemble = jnp.concatenate(ensemble, axis=1)
    values = jnp.concatenate(values, axis=1)
    weight = jnp.concatenate(weights, axis=1)
    mean_obs = jnp.mean(ensemble, axis=0, keepdims=True)
    anomaly = ensemble - mean_obs
    innovation = values - mean_obs
    scaled = anomaly * weight
    extended = jnp.concatenate(
        [anomaly, jnp.broadcast_to(innovation, (8, innovation.shape[1]))], axis=0
    )
    product = gram(two_terms(extended), two_terms(scaled))
    forcing = product[members : members + 1]
    row_id = lax.broadcasted_iota(jnp.int32, (members, 2 * members), 0)
    col_id = lax.broadcasted_iota(jnp.int32, (members, 2 * members), 1)
    identity = (row_id == col_id % members).astype(jnp.float32)
    system = (members - 1.0) * identity + jnp.concatenate([product[:members]] * 2, axis=1)
    scale = 0.5 * jnp.sum(
        jnp.sum(system * identity, axis=1, keepdims=True), axis=0, keepdims=True
    )
    root_part = system / scale
    factor = 1.5 * identity - 0.5 * root_part
    inverse = factor
    for sweep in range(1, SWEEPS):
        factor_terms = two_terms(factor)
        if sweep > 1:
            inverse = doubled_product(factor_terms, two_terms(inverse))
        root_part = doubled_product(two_terms(root_part), factor_terms)
        factor = 1.5 * identity - 0.5 * doubled_product(
            two_terms(inverse), two_terms(root_part)
        )
    inverse = doubled_product(two_terms(factor), two_terms(inverse))
    inv_sqrt = inverse[:, :members] / jnp.sqrt(scale)
    half = jnp.sum(inv_sqrt * forcing, axis=1, keepdims=True)
    mean_weight = jnp.sum(inv_sqrt * half, axis=0, keepdims=True)
    total = jnp.sqrt(jnp.float32(members - 1)) * inv_sqrt + mean_weight
    mixing = total - jnp.mean(total, axis=1, keepdims=True) + 1.0 / members
    mixing = mixing.astype(jnp.bfloat16)
    wide = members * levels
    spread = (
        lax.broadcasted_iota(jnp.int32, (wide, members), 0) // levels
        == lax.broadcasted_iota(jnp.int32, (wide, members), 1)
    ).astype(jnp.bfloat16)
    device = lax.broadcasted_iota(jnp.int32, (wide, members), 0) // (own * levels)
    row_member = turned(core_ref[0], device) * own + (
        lax.broadcasted_iota(jnp.int32, (wide, members), 0) // levels % own
    )
    chosen = (
        row_member == lax.broadcasted_iota(jnp.int32, (wide, members), 1)
    ).astype(jnp.bfloat16)
    tall = jnp.dot(chosen, mixing, preferred_element_type=jnp.float32).astype(jnp.bfloat16)
    full = lax.dot_general(
        tall, spread, (((1,), (1,)), ((), ())), preferred_element_type=jnp.float32
    )
    same = (
        lax.broadcasted_iota(jnp.int32, (wide, wide), 0) % levels
        == lax.broadcasted_iota(jnp.int32, (wide, wide), 1) % levels
    )
    mix_ref[...] = jnp.where(same, full, 0.0).astype(mix_ref.dtype)
    per = out_ref.shape[1] // (kinds * own)

    def body(f, carry):
        begin = f * per * own
        rows = jnp.concatenate(
            [x_ref[:, pl.ds(begin + c * own, own)].reshape(wide, LANES) for c in range(per)],
            axis=1,
        )
        mixed = jnp.dot(mix_ref[...], rows, preferred_element_type=jnp.float32)
        mixed = mixed.astype(out_ref.dtype)
        for c in range(per):
            out_ref[:, pl.ds(begin + c * own, own)] = mixed[
                :, c * LANES : (c + 1) * LANES
            ].reshape(sources, own, levels, LANES)
        return carry

    lax.fori_loop(0, kinds, body, 0)


def observe(fields, values, precision, cells, count):
    own = fields.shape[0]
    tiles, slots = cells.shape
    return pl.pallas_call(
        observe_kernel,
        in_specs=[VMEM] * 4 + [SMEM],
        out_specs=VMEM,
        out_shape=jax.ShapeDtypeStruct((tiles, own + 4, slots), jnp.float32),
        compiler_params=PARAMS,
        name="observe",
    )(fields, values, precision, cells, count)


def split(core, fields, parts, end):
    own, kinds, levels, width = fields.shape
    step = own * (width // parts // LANES)
    return pl.pallas_call(
        split_kernel,
        in_specs=[SMEM, HBM],
        out_specs=HBM,
        out_shape=jax.ShapeDtypeStruct((parts, end * step, levels, LANES), fields.dtype),
        scratch_shapes=[
            pltpu.VMEM((end, own, levels, width), fields.dtype),
            pltpu.VMEM((end, parts, step, levels, LANES), fields.dtype),
            pltpu.SemaphoreType.DMA((end,)),
            pltpu.SemaphoreType.DMA((end,)),
        ],
        name="split",
    )(core, fields)


def join(pieces, shape):
    own, kinds, levels, width = shape
    return pl.pallas_call(
        join_kernel,
        in_specs=[VMEM],
        out_specs=HBM,
        out_shape=jax.ShapeDtypeStruct(shape, pieces.dtype),
        scratch_shapes=[
            pltpu.VMEM((kinds, own, levels, width), pieces.dtype),
            pltpu.SemaphoreType.DMA((kinds,)),
        ],
        compiler_params=PARAMS,
        name="join",
    )(pieces)


def pack(core, fields, parts, begin, inner, here, outer):
    own, kinds, levels, width = fields.shape
    blocks = own * (kinds - begin) * (width // parts // LANES) + 9
    small = jax.ShapeDtypeStruct(here.shape, here.dtype)
    return pl.pallas_call(
        functools.partial(pack_kernel, begin),
        in_specs=[SMEM] + [VMEM] * 4,
        out_specs=[VMEM] * 3,
        out_shape=[
            jax.ShapeDtypeStruct((parts, blocks, levels, LANES), fields.dtype),
            small,
            small,
        ],
        compiler_params=PARAMS,
        name="pack",
    )(core, fields, inner, here, outer)


def analyse(tile, core, radius, pieces, above, here, below, kinds):
    parts, blocks, levels, lanes = pieces.shape
    wide = parts * (here.shape[1] - 4) * levels
    return pl.pallas_call(
        functools.partial(analyse_kernel, kinds),
        in_specs=[SMEM] * 3 + [VMEM] * 4,
        out_specs=VMEM,
        out_shape=jax.ShapeDtypeStruct((parts, blocks - 9, levels, lanes), pieces.dtype),
        scratch_shapes=[pltpu.VMEM((wide, wide), jnp.bfloat16)],
        compiler_params=PARAMS,
        name="analyse",
    )(tile, core, radius, pieces, above, here, below)


def merge_kernel(early_ref, late_ref, out_ref, sems):
    ahead, rest = early_ref.shape[2], late_ref.shape[2]
    copies = []
    for i in range(SIDE):
        for j in range(SIDE):
            copies.append(
                pltpu.make_async_copy(
                    early_ref.at[i, j], out_ref.at[j, i, pl.ds(0, ahead)], sems.at[0, i, j]
                )
            )
            copies.append(
                pltpu.make_async_copy(
                    late_ref.at[i, j], out_ref.at[j, i, pl.ds(ahead, rest)], sems.at[1, i, j]
                )
            )
    for copy in copies:
        copy.start()
    for copy in copies:
        copy.wait()


def merge(early, late):
    shape = early.shape[:2] + (early.shape[2] + late.shape[2],) + early.shape[3:]
    return pl.pallas_call(
        merge_kernel,
        in_specs=[ANY, ANY],
        out_specs=ANY,
        out_shape=jax.ShapeDtypeStruct(shape, early.dtype),
        scratch_shapes=[pltpu.SemaphoreType.DMA((2, SIDE, SIDE))],
        compiler_params=PARAMS,
        name="merge",
    )(early, late)


def hop_groups(rows):
    def group(row, fixed, along_y):
        members = [
            i * SIDE + fixed if along_y else fixed * SIDE + i for i in range(SIDE)
        ]
        return [member * rows + row for member in members]

    return [
        [group(r, i, r % 2 == hop) for r in range(rows) for i in range(SIDE)]
        for hop in range(2)
    ]


def on_device(background, obs_values, obs_precision, obs_cell, obs_count, radius):
    own, levels, kinds, _, width = background.shape
    parts = lax.axis_size("member")
    rows = lax.axis_size("space")
    share = parts * TILE_CELLS // width
    pairs = [(i, i + 1) for i in range(rows - 1)]
    swap = [pairs[0::2], pairs[1::2]]
    swap = [one + [(j, i) for i, j in one] for one in swap]
    fields = background.transpose(0, 2, 3, 1, 4).reshape(own, kinds, levels, width)
    both = ("member", "space")
    groups = hop_groups(rows)
    core = (lax.axis_index("space") % 2).astype(jnp.int32).reshape(1)
    early = split(core, fields, parts, EARLY)
    early, fields = lax.optimization_barrier((early, fields))
    early = early.reshape((SIDE, SIDE) + early.shape[1:])
    early = lax.all_to_all(early, both, 0, 0, axis_index_groups=groups[0])
    here = observe(fields, obs_values[0], obs_precision[0], obs_cell[0], obs_count)
    inner = lax.ppermute(here, "space", swap[0])
    outer = lax.ppermute(here, "space", swap[1])
    late, above, below = pack(core, fields, parts, EARLY, inner, here, outer)
    late = late.reshape((SIDE, SIDE) + late.shape[1:])
    late, early = lax.optimization_barrier((late, early))
    late = lax.all_to_all(late, both, 0, 0, axis_index_groups=groups[0])
    pieces = merge(early, late)
    pieces = lax.all_to_all(pieces, both, 0, 0, axis_index_groups=groups[1])
    pieces = pieces.reshape((parts,) + pieces.shape[2:])
    tile = (lax.axis_index("member") // share).astype(jnp.int32).reshape(1)
    mixed = analyse(tile, core, radius, pieces, above, here, below, kinds)
    out = join(lax.all_to_all(mixed, "member", 0, 0), fields.shape)
    return out.reshape(own, kinds, 1, levels, width).transpose(0, 3, 1, 2, 4)


def solution(mesh):
    return jax.shard_map(
        on_device,
        mesh=mesh,
        in_specs=(
            P("member", None, None, "space", None),
            P("space", None, None),
            P("space", None, None),
            P("space", None, None),
            P("space", None),
            P("space", None),
        ),
        out_specs=P("member", None, None, "space", None),
        check_vma=False,
    )
```

```python
import functools

import jax
import jax.numpy as jnp
from jax import lax
from jax.experimental import pallas as pl
from jax.experimental.pallas import tpu as pltpu
from jax.sharding import PartitionSpec as P

TILE_SIDE = 32
TILE_CELLS = 1024
SWEEPS = 6


LANES = 128
VMEM = pl.BlockSpec(memory_space=pltpu.VMEM)
SMEM = pl.BlockSpec(memory_space=pltpu.SMEM)
HBM = pl.BlockSpec(memory_space=pltpu.HBM)
ANY = pl.BlockSpec(memory_space=pl.ANY)
PARAMS = pltpu.CompilerParams(vmem_limit_bytes=16 * 1024 * 1024)
EARLY = 3
SIDE = 4


def turned(core, index):
    return jnp.where(core == 0, index % SIDE * SIDE + index // SIDE, index)


def split_kernel(core_ref, x_ref, out_ref, held, made, in_sems, out_sems):
    kinds, own = held.shape[:2]
    width = held.shape[3]
    blocks = width // LANES
    parts, step = made.shape[1:3]
    per = blocks // parts
    loads = [
        pltpu.make_async_copy(x_ref.at[:, f], held.at[f], in_sems.at[f]) for f in range(kinds)
    ]
    stores = [
        pltpu.make_async_copy(
            made.at[f], out_ref.at[:, pl.ds(f * step, step)], out_sems.at[f]
        )
        for f in range(kinds)
    ]
    for load in loads:
        load.start()
    places = [turned(1 - core_ref[0], d) for d in range(parts)]
    for f in range(kinds):
        loads[f].wait()
        for c in range(blocks):
            for m in range(own):
                made[f, places[c // per], c % per * own + m] = held[
                    f, m, :, c * LANES : (c + 1) * LANES
                ]
        stores[f].start()
    for store in stores:
        store.wait()


def join_kernel(x_ref, out_ref, made, out_sems):
    kinds, own = made.shape[:2]
    width = made.shape[3]
    blocks = width // LANES
    per = blocks // x_ref.shape[0]
    stores = [
        pltpu.make_async_copy(made.at[f], out_ref.at[:, f], out_sems.at[f])
        for f in range(kinds)
    ]
    for f in range(kinds):
        for c in range(blocks):
            for m in range(own):
                made[f, m, :, c * LANES : (c + 1) * LANES] = x_ref[
                    c // per, (f * per + c % per) * own + m
                ]
        stores[f].start()
    for store in stores:
        store.wait()


def observe_kernel(x_ref, value_ref, precision_ref, cell_ref, count_ref, out_ref):
    own, kinds, levels, width = x_ref.shape
    tiles, slots = cell_ref.shape
    cells = width // tiles
    cell = cell_ref[...]
    in_tile = cell % cells
    level_field = cell // cells
    wanted = (level_field % kinds) * levels + level_field // kinds
    row_place = (in_tile // TILE_SIDE).astype(jnp.float32)
    col_place = (in_tile % TILE_SIDE).astype(jnp.float32)
    place_id = lax.broadcasted_iota(jnp.int32, (cells, slots), 0)
    field_id = lax.broadcasted_iota(jnp.int32, (kinds * levels, slots), 0)
    slot_id = lax.broadcasted_iota(jnp.int32, (1, slots), 1)
    for tile in range(tiles):
        at = slice(tile, tile + 1)
        onehot = (place_id == in_tile[at]).astype(x_ref.dtype)
        rows = x_ref[:, :, :, tile * cells : (tile + 1) * cells].reshape(-1, cells)
        found = jnp.dot(rows, onehot, preferred_element_type=jnp.float32)
        found = found.reshape(own, kinds * levels, slots)
        match = field_id == wanted[at]
        out_ref[tile, 0:own, :] = jnp.sum(jnp.where(match[None], found, 0.0), axis=1)
        out_ref[tile, own : own + 1, :] = value_ref[at, :]
        out_ref[tile, own + 1 : own + 2, :] = jnp.where(
            slot_id < count_ref[0, tile], precision_ref[at, :], 0.0
        )
        out_ref[tile, own + 2 : own + 3, :] = row_place[at]
        out_ref[tile, own + 3 : own + 4, :] = col_place[at]


def pack_kernel(
    begin, core_ref, x_ref, inner_ref, own_ref, outer_ref, out_ref, above_ref, below_ref
):
    odd = core_ref[0] == 1
    places = [turned(1 - core_ref[0], d) for d in range(out_ref.shape[0])]
    inner, outer = inner_ref[...], outer_ref[...]
    above_ref[...] = jnp.where(odd, inner, outer)
    below_ref[...] = jnp.where(odd, outer, inner)
    parts, blocks, own, slots = out_ref.shape
    lane_blocks = x_ref.shape[3] // LANES
    per = lane_blocks // parts

    def copy_field(f, carry):
        for c in range(lane_blocks):
            for m in range(own):
                out_ref[places[c // per], ((f - begin) * per + c % per) * own + m] = x_ref[
                    m, f, :, c * LANES : (c + 1) * LANES
                ]
        return carry

    lax.fori_loop(begin, x_ref.shape[1], copy_field, 0)
    first = blocks - 9
    tiles = own_ref.shape[0]
    share = parts // tiles
    for a, rows_ref in enumerate((above_ref, own_ref, below_ref)):
        for t in range(tiles):
            rows = rows_ref[t, 0:own, :].astype(out_ref.dtype)
            for b in range(3):
                for h in range(share):
                    place = t + 1 - b
                    if 0 <= place < tiles:
                        out_ref[places[place * share + h], first + a * 3 + b] = rows
    blank = jnp.zeros((own, slots), out_ref.dtype)
    for h in range(share):
        for a in range(3):
            out_ref[places[h], first + a * 3] = blank
            out_ref[places[(tiles - 1) * share + h], first + a * 3 + 2] = blank


def two_terms(array):
    high = array.astype(jnp.bfloat16)
    return high, (array - high.astype(jnp.float32)).astype(jnp.bfloat16)


def gram(left, right):
    def product(a, b):
        return lax.dot_general(
            a, b, (((1,), (1,)), ((), ())), preferred_element_type=jnp.float32
        )

    return (
        product(left[0], right[0]) + product(left[0], right[1]) + product(left[1], right[0])
    )


def doubled_product(left, right):
    return jnp.dot(
        jnp.concatenate(left, axis=1),
        jnp.concatenate(right + right, axis=0),
        preferred_element_type=jnp.float32,
    )


def analyse_kernel(
    kinds, tile_ref, core_ref, radius_ref, x_ref, above_ref, own_ref, below_ref, out_ref, mix_ref
):
    tile = tile_ref[0]
    tiles = own_ref.shape[0]
    sources, _, levels, slots = x_ref.shape
    own = own_ref.shape[1] - 4
    first = x_ref.shape[1] - 9
    members = sources * own
    reach = radius_ref[0, tile].astype(jnp.float32)
    centre = 0.5 * TILE_SIDE - 0.5
    ensemble, values, weights = [], [], []
    for a, rows_ref in enumerate((above_ref, own_ref, below_ref)):
        for b in range(3):
            place = tile + b - 1
            inside = jnp.logical_and(place >= 0, place < tiles)
            held = jnp.clip(place, 0, tiles - 1)
            value, active, row, col = (
                rows_ref[held, own + i : own + i + 1, :] for i in range(4)
            )
            dist_row = row + ((a - 1) * TILE_SIDE - centre)
            dist_col = col + ((b - 1) * TILE_SIDE - centre)
            taper = jnp.maximum(
                1.0 - (dist_row * dist_row + dist_col * dist_col) / (reach * reach), 0.0
            )
            weights.append(jnp.where(inside, active, 0.0) * (taper * taper))
            values.append(value)
            ensemble.append(
                x_ref[:, first + a * 3 + b].astype(jnp.float32).reshape(members, slots)
            )
    ensemble = jnp.concatenate(ensemble, axis=1)
    values = jnp.concatenate(values, axis=1)
    weight = jnp.concatenate(weights, axis=1)
    mean_obs = jnp.mean(ensemble, axis=0, keepdims=True)
    anomaly = ensemble - mean_obs
    innovation = values - mean_obs
    scaled = anomaly * weight
    extended = jnp.concatenate(
        [anomaly, jnp.broadcast_to(innovation, (8, innovation.shape[1]))], axis=0
    )
    product = gram(two_terms(extended), two_terms(scaled))
    forcing = product[members : members + 1]
    row_id = lax.broadcasted_iota(jnp.int32, (members, 2 * members), 0)
    col_id = lax.broadcasted_iota(jnp.int32, (members, 2 * members), 1)
    identity = (row_id == col_id % members).astype(jnp.float32)
    system = (members - 1.0) * identity + jnp.concatenate([product[:members]] * 2, axis=1)
    scale = 0.5 * jnp.sum(
        jnp.sum(system * identity, axis=1, keepdims=True), axis=0, keepdims=True
    )
    root_part = system / scale
    factor = 1.5 * identity - 0.5 * root_part
    inverse = factor
    for sweep in range(1, SWEEPS):
        factor_terms = two_terms(factor)
        if sweep > 1:
            inverse = doubled_product(factor_terms, two_terms(inverse))
        root_part = doubled_product(two_terms(root_part), factor_terms)
        factor = 1.5 * identity - 0.5 * doubled_product(
            two_terms(inverse), two_terms(root_part)
        )
    inverse = doubled_product(two_terms(factor), two_terms(inverse))
    inv_sqrt = inverse[:, :members] / jnp.sqrt(scale)
    half = jnp.sum(inv_sqrt * forcing, axis=1, keepdims=True)
    mean_weight = jnp.sum(inv_sqrt * half, axis=0, keepdims=True)
    total = jnp.sqrt(jnp.float32(members - 1)) * inv_sqrt + mean_weight
    mixing = total - jnp.mean(total, axis=1, keepdims=True) + 1.0 / members
    mixing = mixing.astype(jnp.bfloat16)
    wide = members * levels
    spread = (
        lax.broadcasted_iota(jnp.int32, (wide, members), 0) // levels
        == lax.broadcasted_iota(jnp.int32, (wide, members), 1)
    ).astype(jnp.bfloat16)
    device = lax.broadcasted_iota(jnp.int32, (wide, members), 0) // (own * levels)
    row_member = turned(core_ref[0], device) * own + (
        lax.broadcasted_iota(jnp.int32, (wide, members), 0) // levels % own
    )
    chosen = (
        row_member == lax.broadcasted_iota(jnp.int32, (wide, members), 1)
    ).astype(jnp.bfloat16)
    tall = jnp.dot(chosen, mixing, preferred_element_type=jnp.float32).astype(jnp.bfloat16)
    full = lax.dot_general(
        tall, spread, (((1,), (1,)), ((), ())), preferred_element_type=jnp.float32
    )
    same = (
        lax.broadcasted_iota(jnp.int32, (wide, wide), 0) % levels
        == lax.broadcasted_iota(jnp.int32, (wide, wide), 1) % levels
    )
    mix_ref[...] = jnp.where(same, full, 0.0).astype(mix_ref.dtype)
    per = out_ref.shape[1] // (kinds * own)

    def body(f, carry):
        begin = f * per * own
        rows = jnp.concatenate(
            [x_ref[:, pl.ds(begin + c * own, own)].reshape(wide, LANES) for c in range(per)],
            axis=1,
        )
        mixed = jnp.dot(mix_ref[...], rows, preferred_element_type=jnp.float32)
        mixed = mixed.astype(out_ref.dtype)
        for c in range(per):
            out_ref[:, pl.ds(begin + c * own, own)] = mixed[
                :, c * LANES : (c + 1) * LANES
            ].reshape(sources, own, levels, LANES)
        return carry

    lax.fori_loop(0, kinds, body, 0, unroll=True)


def observe(fields, values, precision, cells, count):
    own = fields.shape[0]
    tiles, slots = cells.shape
    return pl.pallas_call(
        observe_kernel,
        in_specs=[VMEM] * 4 + [SMEM],
        out_specs=VMEM,
        out_shape=jax.ShapeDtypeStruct((tiles, own + 4, slots), jnp.float32),
        compiler_params=PARAMS,
        name="observe",
    )(fields, values, precision, cells, count)


def split(core, fields, parts, end):
    own, kinds, levels, width = fields.shape
    step = own * (width // parts // LANES)
    return pl.pallas_call(
        split_kernel,
        in_specs=[SMEM, HBM],
        out_specs=HBM,
        out_shape=jax.ShapeDtypeStruct((parts, end * step, levels, LANES), fields.dtype),
        scratch_shapes=[
            pltpu.VMEM((end, own, levels, width), fields.dtype),
            pltpu.VMEM((end, parts, step, levels, LANES), fields.dtype),
            pltpu.SemaphoreType.DMA((end,)),
            pltpu.SemaphoreType.DMA((end,)),
        ],
        name="split",
    )(core, fields)


def join(pieces, shape):
    own, kinds, levels, width = shape
    return pl.pallas_call(
        join_kernel,
        in_specs=[VMEM],
        out_specs=HBM,
        out_shape=jax.ShapeDtypeStruct(shape, pieces.dtype),
        scratch_shapes=[
            pltpu.VMEM((kinds, own, levels, width), pieces.dtype),
            pltpu.SemaphoreType.DMA((kinds,)),
        ],
        compiler_params=PARAMS,
        name="join",
    )(pieces)


def pack(core, fields, parts, begin, inner, here, outer):
    own, kinds, levels, width = fields.shape
    blocks = own * (kinds - begin) * (width // parts // LANES) + 9
    small = jax.ShapeDtypeStruct(here.shape, here.dtype)
    return pl.pallas_call(
        functools.partial(pack_kernel, begin),
        in_specs=[SMEM] + [VMEM] * 4,
        out_specs=[VMEM] * 3,
        out_shape=[
            jax.ShapeDtypeStruct((parts, blocks, levels, LANES), fields.dtype),
            small,
            small,
        ],
        compiler_params=PARAMS,
        name="pack",
    )(core, fields, inner, here, outer)


def analyse(tile, core, radius, pieces, above, here, below, kinds):
    parts, blocks, levels, lanes = pieces.shape
    wide = parts * (here.shape[1] - 4) * levels
    return pl.pallas_call(
        functools.partial(analyse_kernel, kinds),
        in_specs=[SMEM] * 3 + [VMEM] * 4,
        out_specs=VMEM,
        out_shape=jax.ShapeDtypeStruct((parts, blocks - 9, levels, lanes), pieces.dtype),
        scratch_shapes=[pltpu.VMEM((wide, wide), jnp.bfloat16)],
        compiler_params=PARAMS,
        name="analyse",
    )(tile, core, radius, pieces, above, here, below)


def merge_kernel(early_ref, late_ref, out_ref, sems):
    ahead, rest = early_ref.shape[2], late_ref.shape[2]
    copies = []
    for j in range(SIDE):
        copies.append(
            pltpu.make_async_copy(
                early_ref.at[:, j], out_ref.at[j, :, pl.ds(0, ahead)], sems.at[0, j]
            )
        )
        copies.append(
            pltpu.make_async_copy(
                late_ref.at[:, j], out_ref.at[j, :, pl.ds(ahead, rest)], sems.at[1, j]
            )
        )
    for copy in copies:
        copy.start()
    for copy in copies:
        copy.wait()


def merge(early, late):
    shape = early.shape[:2] + (early.shape[2] + late.shape[2],) + early.shape[3:]
    return pl.pallas_call(
        merge_kernel,
        in_specs=[ANY, ANY],
        out_specs=ANY,
        out_shape=jax.ShapeDtypeStruct(shape, early.dtype),
        scratch_shapes=[pltpu.SemaphoreType.DMA((2, SIDE))],
        compiler_params=PARAMS,
        name="merge",
    )(early, late)


def hop_groups(rows):
    def group(row, fixed, along_y):
        members = [
            i * SIDE + fixed if along_y else fixed * SIDE + i for i in range(SIDE)
        ]
        return [member * rows + row for member in members]

    return [
        [group(r, i, r % 2 == hop) for r in range(rows) for i in range(SIDE)]
        for hop in range(2)
    ]


def on_device(background, obs_values, obs_precision, obs_cell, obs_count, radius):
    own, levels, kinds, _, width = background.shape
    parts = lax.axis_size("member")
    rows = lax.axis_size("space")
    share = parts * TILE_CELLS // width
    pairs = [(i, i + 1) for i in range(rows - 1)]
    swap = [pairs[0::2], pairs[1::2]]
    swap = [one + [(j, i) for i, j in one] for one in swap]
    fields = background.transpose(0, 2, 3, 1, 4).reshape(own, kinds, levels, width)
    both = ("member", "space")
    groups = hop_groups(rows)
    core = (lax.axis_index("space") % 2).astype(jnp.int32).reshape(1)
    early = split(core, fields, parts, EARLY)
    early, fields = lax.optimization_barrier((early, fields))
    early = early.reshape((SIDE, SIDE) + early.shape[1:])
    early = lax.all_to_all(early, both, 0, 0, axis_index_groups=groups[0])
    here = observe(fields, obs_values[0], obs_precision[0], obs_cell[0], obs_count)
    inner = lax.ppermute(here, "space", swap[0])
    outer = lax.ppermute(here, "space", swap[1])
    late, above, below = pack(core, fields, parts, EARLY, inner, here, outer)
    late = late.reshape((SIDE, SIDE) + late.shape[1:])
    late, early = lax.optimization_barrier((late, early))
    late = lax.all_to_all(late, both, 0, 0, axis_index_groups=groups[0])
    pieces = merge(early, late)
    pieces = lax.all_to_all(pieces, both, 0, 0, axis_index_groups=groups[1])
    pieces = pieces.reshape((parts,) + pieces.shape[2:])
    tile = (lax.axis_index("member") // share).astype(jnp.int32).reshape(1)
    mixed = analyse(tile, core, radius, pieces, above, here, below, kinds)
    out = join(lax.all_to_all(mixed, "member", 0, 0), fields.shape)
    return out.reshape(own, kinds, 1, levels, width).transpose(0, 3, 1, 2, 4)


def solution(mesh):
    return jax.shard_map(
        on_device,
        mesh=mesh,
        in_specs=(
            P("member", None, None, "space", None),
            P("space", None, None),
            P("space", None, None),
            P("space", None, None),
            P("space", None),
            P("space", None),
        ),
        out_specs=P("member", None, None, "space", None),
        check_vma=False,
    )
```

```python
import functools

import jax
import jax.numpy as jnp
from jax import lax
from jax.experimental import pallas as pl
from jax.experimental.pallas import tpu as pltpu
from jax.sharding import PartitionSpec as P

TILE_SIDE = 32
TILE_CELLS = 1024
SWEEPS = 6


LANES = 128
VMEM = pl.BlockSpec(memory_space=pltpu.VMEM)
SMEM = pl.BlockSpec(memory_space=pltpu.SMEM)
HBM = pl.BlockSpec(memory_space=pltpu.HBM)
ANY = pl.BlockSpec(memory_space=pl.ANY)
PARAMS = pltpu.CompilerParams(vmem_limit_bytes=16 * 1024 * 1024)
EARLY = 3
SIDE = 4


def turned(core, index):
    return jnp.where(core == 0, index % SIDE * SIDE + index // SIDE, index)


def split_kernel(core_ref, x_ref, out_ref, held, made, in_sems, out_sems):
    kinds, own = held.shape[:2]
    width = held.shape[3]
    blocks = width // LANES
    parts, step = made.shape[1:3]
    per = blocks // parts
    loads = [
        pltpu.make_async_copy(x_ref.at[:, f], held.at[f], in_sems.at[f]) for f in range(kinds)
    ]
    stores = [
        pltpu.make_async_copy(
            made.at[f], out_ref.at[:, pl.ds(f * step, step)], out_sems.at[f]
        )
        for f in range(kinds)
    ]
    for load in loads:
        load.start()
    places = [turned(1 - core_ref[0], d) for d in range(parts)]
    for f in range(kinds):
        loads[f].wait()
        for c in range(blocks):
            for m in range(own):
                made[f, places[c // per], c % per * own + m] = held[
                    f, m, :, c * LANES : (c + 1) * LANES
                ]
        stores[f].start()
    for store in stores:
        store.wait()


def join_kernel(x_ref, out_ref, made, out_sems):
    kinds, own = made.shape[:2]
    width = made.shape[3]
    blocks = width // LANES
    per = blocks // x_ref.shape[0]
    stores = [
        pltpu.make_async_copy(made.at[f], out_ref.at[:, f], out_sems.at[f])
        for f in range(kinds)
    ]
    for f in range(kinds):
        for c in range(blocks):
            for m in range(own):
                made[f, m, :, c * LANES : (c + 1) * LANES] = x_ref[
                    c // per, (f * per + c % per) * own + m
                ]
        stores[f].start()
    for store in stores:
        store.wait()


def observe_kernel(x_ref, value_ref, precision_ref, cell_ref, count_ref, out_ref):
    own, kinds, levels, width = x_ref.shape
    tiles, slots = cell_ref.shape
    cells = width // tiles
    cell = cell_ref[...]
    in_tile = cell % cells
    level_field = cell // cells
    wanted = (level_field % kinds) * levels + level_field // kinds
    row_place = (in_tile // TILE_SIDE).astype(jnp.float32)
    col_place = (in_tile % TILE_SIDE).astype(jnp.float32)
    place_id = lax.broadcasted_iota(jnp.int32, (cells, slots), 0)
    field_id = lax.broadcasted_iota(jnp.int32, (kinds * levels, slots), 0)
    slot_id = lax.broadcasted_iota(jnp.int32, (1, slots), 1)
    for tile in range(tiles):
        at = slice(tile, tile + 1)
        onehot = (place_id == in_tile[at]).astype(x_ref.dtype)
        rows = x_ref[:, :, :, tile * cells : (tile + 1) * cells].reshape(-1, cells)
        found = jnp.dot(rows, onehot, preferred_element_type=jnp.float32)
        found = found.reshape(own, kinds * levels, slots)
        match = field_id == wanted[at]
        out_ref[tile, 0:own, :] = jnp.sum(jnp.where(match[None], found, 0.0), axis=1)
        out_ref[tile, own : own + 1, :] = value_ref[at, :]
        out_ref[tile, own + 1 : own + 2, :] = jnp.where(
            slot_id < count_ref[0, tile], precision_ref[at, :], 0.0
        )
        out_ref[tile, own + 2 : own + 3, :] = row_place[at]
        out_ref[tile, own + 3 : own + 4, :] = col_place[at]


def pack_kernel(
    begin,
    core_ref,
    tile_ref,
    radius_ref,
    x_ref,
    inner_ref,
    own_ref,
    outer_ref,
    out_ref,
    above_ref,
    below_ref,
    reach_ref,
):
    reach_ref[...] = jnp.full(reach_ref.shape, radius_ref[0, tile_ref[0]], jnp.float32)
    odd = core_ref[0] == 1
    places = [turned(1 - core_ref[0], d) for d in range(out_ref.shape[0])]
    inner, outer = inner_ref[...], outer_ref[...]
    above_ref[...] = jnp.where(odd, inner, outer)
    below_ref[...] = jnp.where(odd, outer, inner)
    parts, blocks, own, slots = out_ref.shape
    lane_blocks = x_ref.shape[3] // LANES
    per = lane_blocks // parts

    def copy_field(f, carry):
        for c in range(lane_blocks):
            for m in range(own):
                out_ref[places[c // per], ((f - begin) * per + c % per) * own + m] = x_ref[
                    m, f, :, c * LANES : (c + 1) * LANES
                ]
        return carry

    lax.fori_loop(begin, x_ref.shape[1], copy_field, 0, unroll=True)
    first = blocks - 9
    tiles = own_ref.shape[0]
    share = parts // tiles
    for a, rows_ref in enumerate((above_ref, own_ref, below_ref)):
        for t in range(tiles):
            rows = rows_ref[t, 0:own, :].astype(out_ref.dtype)
            for b in range(3):
                for h in range(share):
                    place = t + 1 - b
                    if 0 <= place < tiles:
                        out_ref[places[place * share + h], first + a * 3 + b] = rows
    blank = jnp.zeros((own, slots), out_ref.dtype)
    for h in range(share):
        for a in range(3):
            out_ref[places[h], first + a * 3] = blank
            out_ref[places[(tiles - 1) * share + h], first + a * 3 + 2] = blank


def two_terms(array):
    high = array.astype(jnp.bfloat16)
    return high, (array - high.astype(jnp.float32)).astype(jnp.bfloat16)


def gram(left, right):
    def product(a, b):
        return lax.dot_general(
            a, b, (((1,), (1,)), ((), ())), preferred_element_type=jnp.float32
        )

    count = left[0].shape[0]
    both = product(jnp.concatenate(left, axis=0), right[0])
    return both[:count] + both[count:] + product(left[0], right[1])


def doubled_product(left, right):
    return jnp.dot(
        jnp.concatenate(left, axis=1),
        jnp.concatenate(right + right, axis=0),
        preferred_element_type=jnp.float32,
    )


def analyse_kernel(
    kinds, tile_ref, core_ref, reach_ref, x_ref, above_ref, own_ref, below_ref, out_ref, mix_ref
):
    tile = tile_ref[0]
    tiles = own_ref.shape[0]
    sources, _, levels, slots = x_ref.shape
    own = own_ref.shape[1] - 4
    first = x_ref.shape[1] - 9
    members = sources * own
    reach = reach_ref[0:1, :]
    centre = 0.5 * TILE_SIDE - 0.5
    ensemble, values, weights = [], [], []
    for a, rows_ref in enumerate((above_ref, own_ref, below_ref)):
        for b in range(3):
            place = tile + b - 1
            inside = jnp.logical_and(place >= 0, place < tiles)
            held = jnp.clip(place, 0, tiles - 1)
            value, active, row, col = (
                rows_ref[held, own + i : own + i + 1, :] for i in range(4)
            )
            dist_row = row + ((a - 1) * TILE_SIDE - centre)
            dist_col = col + ((b - 1) * TILE_SIDE - centre)
            taper = jnp.maximum(
                1.0 - (dist_row * dist_row + dist_col * dist_col) / (reach * reach), 0.0
            )
            weights.append(jnp.where(inside, active, 0.0) * (taper * taper))
            values.append(value)
            ensemble.append(
                x_ref[:, first + a * 3 + b].astype(jnp.float32).reshape(members, slots)
            )
    ensemble = jnp.concatenate(ensemble, axis=1)
    values = jnp.concatenate(values, axis=1)
    weight = jnp.concatenate(weights, axis=1)
    mean_obs = jnp.mean(ensemble, axis=0, keepdims=True)
    anomaly = ensemble - mean_obs
    innovation = values - mean_obs
    scaled = anomaly * weight
    extended = jnp.concatenate(
        [anomaly, jnp.broadcast_to(innovation, (8, innovation.shape[1]))], axis=0
    )
    product = gram(two_terms(extended), two_terms(scaled))
    forcing = product[members : members + 1]
    row_id = lax.broadcasted_iota(jnp.int32, (members, 2 * members), 0)
    col_id = lax.broadcasted_iota(jnp.int32, (members, 2 * members), 1)
    identity = (row_id == col_id % members).astype(jnp.float32)
    system = (members - 1.0) * identity + jnp.concatenate([product[:members]] * 2, axis=1)
    scale = 0.5 * jnp.sum(
        jnp.sum(system * identity, axis=1, keepdims=True), axis=0, keepdims=True
    )
    root_part = system / scale
    factor = 1.5 * identity - 0.5 * root_part
    inverse = factor
    for sweep in range(1, SWEEPS):
        factor_terms = two_terms(factor)
        if sweep > 1:
            inverse = doubled_product(factor_terms, two_terms(inverse))
        root_part = doubled_product(two_terms(root_part), factor_terms)
        factor = 1.5 * identity - 0.5 * doubled_product(
            two_terms(inverse), two_terms(root_part)
        )
    inverse = doubled_product(two_terms(factor), two_terms(inverse))
    inv_sqrt = inverse[:, :members] / jnp.sqrt(scale)
    half = jnp.sum(inv_sqrt * forcing, axis=1, keepdims=True)
    mean_weight = jnp.sum(inv_sqrt * half, axis=0, keepdims=True)
    total = jnp.sqrt(jnp.float32(members - 1)) * inv_sqrt + mean_weight
    mixing = total - jnp.mean(total, axis=1, keepdims=True) + 1.0 / members
    mixing = mixing.astype(jnp.bfloat16)
    wide = members * levels
    spread = (
        lax.broadcasted_iota(jnp.int32, (wide, members), 0) // levels
        == lax.broadcasted_iota(jnp.int32, (wide, members), 1)
    ).astype(jnp.bfloat16)
    device = lax.broadcasted_iota(jnp.int32, (wide, members), 0) // (own * levels)
    row_member = turned(core_ref[0], device) * own + (
        lax.broadcasted_iota(jnp.int32, (wide, members), 0) // levels % own
    )
    chosen = (
        row_member == lax.broadcasted_iota(jnp.int32, (wide, members), 1)
    ).astype(jnp.bfloat16)
    tall = jnp.dot(chosen, mixing, preferred_element_type=jnp.float32).astype(jnp.bfloat16)
    full = lax.dot_general(
        tall, spread, (((1,), (1,)), ((), ())), preferred_element_type=jnp.float32
    )
    same = (
        lax.broadcasted_iota(jnp.int32, (wide, wide), 0) % levels
        == lax.broadcasted_iota(jnp.int32, (wide, wide), 1) % levels
    )
    mix_ref[...] = jnp.where(same, full, 0.0).astype(mix_ref.dtype)
    per = out_ref.shape[1] // (kinds * own)

    def body(f, carry):
        begin = f * per * own
        rows = jnp.concatenate(
            [x_ref[:, pl.ds(begin + c * own, own)].reshape(wide, LANES) for c in range(per)],
            axis=1,
        )
        mixed = jnp.dot(mix_ref[...], rows, preferred_element_type=jnp.float32)
        mixed = mixed.astype(out_ref.dtype)
        for c in range(per):
            out_ref[:, pl.ds(begin + c * own, own)] = mixed[
                :, c * LANES : (c + 1) * LANES
            ].reshape(sources, own, levels, LANES)
        return carry

    lax.fori_loop(0, kinds, body, 0, unroll=True)


def observe(fields, values, precision, cells, count):
    own = fields.shape[0]
    tiles, slots = cells.shape
    return pl.pallas_call(
        observe_kernel,
        in_specs=[VMEM] * 4 + [SMEM],
        out_specs=VMEM,
        out_shape=jax.ShapeDtypeStruct((tiles, own + 4, slots), jnp.float32),
        compiler_params=PARAMS,
        name="observe",
    )(fields, values, precision, cells, count)


def split(core, fields, parts, end):
    own, kinds, levels, width = fields.shape
    step = own * (width // parts // LANES)
    return pl.pallas_call(
        split_kernel,
        in_specs=[SMEM, HBM],
        out_specs=HBM,
        out_shape=jax.ShapeDtypeStruct((parts, end * step, levels, LANES), fields.dtype),
        scratch_shapes=[
            pltpu.VMEM((end, own, levels, width), fields.dtype),
            pltpu.VMEM((end, parts, step, levels, LANES), fields.dtype),
            pltpu.SemaphoreType.DMA((end,)),
            pltpu.SemaphoreType.DMA((end,)),
        ],
        name="split",
    )(core, fields)


def join(pieces, shape):
    own, kinds, levels, width = shape
    return pl.pallas_call(
        join_kernel,
        in_specs=[VMEM],
        out_specs=HBM,
        out_shape=jax.ShapeDtypeStruct(shape, pieces.dtype),
        scratch_shapes=[
            pltpu.VMEM((kinds, own, levels, width), pieces.dtype),
            pltpu.SemaphoreType.DMA((kinds,)),
        ],
        compiler_params=PARAMS,
        name="join",
    )(pieces)


def pack(core, tile, radius, fields, parts, begin, inner, here, outer):
    own, kinds, levels, width = fields.shape
    blocks = own * (kinds - begin) * (width // parts // LANES) + 9
    small = jax.ShapeDtypeStruct(here.shape, here.dtype)
    return pl.pallas_call(
        functools.partial(pack_kernel, begin),
        in_specs=[SMEM] * 3 + [VMEM] * 4,
        out_specs=[VMEM] * 4,
        out_shape=[
            jax.ShapeDtypeStruct((parts, blocks, levels, LANES), fields.dtype),
            small,
            small,
            jax.ShapeDtypeStruct((8, LANES), jnp.float32),
        ],
        compiler_params=PARAMS,
        name="pack",
    )(core, tile, radius, fields, inner, here, outer)


def analyse(tile, core, reach, pieces, above, here, below, kinds):
    parts, blocks, levels, lanes = pieces.shape
    wide = parts * (here.shape[1] - 4) * levels
    return pl.pallas_call(
        functools.partial(analyse_kernel, kinds),
        in_specs=[SMEM] * 2 + [VMEM] * 5,
        out_specs=VMEM,
        out_shape=jax.ShapeDtypeStruct((parts, blocks - 9, levels, lanes), pieces.dtype),
        scratch_shapes=[pltpu.VMEM((wide, wide), jnp.bfloat16)],
        compiler_params=PARAMS,
        name="analyse",
    )(tile, core, reach, pieces, above, here, below)


def merge_kernel(early_ref, late_ref, out_ref, sems):
    ahead, rest = early_ref.shape[2], late_ref.shape[2]
    copies = []
    for j in range(SIDE):
        copies.append(
            pltpu.make_async_copy(
                early_ref.at[:, j], out_ref.at[j, :, pl.ds(0, ahead)], sems.at[0, j]
            )
        )
        copies.append(
            pltpu.make_async_copy(
                late_ref.at[:, j], out_ref.at[j, :, pl.ds(ahead, rest)], sems.at[1, j]
            )
        )
    for copy in copies:
        copy.start()
    for copy in copies:
        copy.wait()


def merge(early, late):
    shape = early.shape[:2] + (early.shape[2] + late.shape[2],) + early.shape[3:]
    return pl.pallas_call(
        merge_kernel,
        in_specs=[ANY, ANY],
        out_specs=ANY,
        out_shape=jax.ShapeDtypeStruct(shape, early.dtype),
        scratch_shapes=[pltpu.SemaphoreType.DMA((2, SIDE))],
        compiler_params=PARAMS,
        name="merge",
    )(early, late)


def hop_groups(rows):
    def group(row, fixed, along_y):
        members = [
            i * SIDE + fixed if along_y else fixed * SIDE + i for i in range(SIDE)
        ]
        return [member * rows + row for member in members]

    return [
        [group(r, i, r % 2 == hop) for r in range(rows) for i in range(SIDE)]
        for hop in range(2)
    ]


def on_device(background, obs_values, obs_precision, obs_cell, obs_count, radius):
    own, levels, kinds, _, width = background.shape
    parts = lax.axis_size("member")
    rows = lax.axis_size("space")
    share = parts * TILE_CELLS // width
    pairs = [(i, i + 1) for i in range(rows - 1)]
    swap = [pairs[0::2], pairs[1::2]]
    swap = [one + [(j, i) for i, j in one] for one in swap]
    fields = background.transpose(0, 2, 3, 1, 4).reshape(own, kinds, levels, width)
    both = ("member", "space")
    groups = hop_groups(rows)
    core = (lax.axis_index("space") % 2).astype(jnp.int32).reshape(1)
    tile = (lax.axis_index("member") // share).astype(jnp.int32).reshape(1)
    early = split(core, fields, parts, EARLY)
    early, fields = lax.optimization_barrier((early, fields))
    early = early.reshape((SIDE, SIDE) + early.shape[1:])
    early = lax.all_to_all(early, both, 0, 0, axis_index_groups=groups[0])
    here = observe(fields, obs_values[0], obs_precision[0], obs_cell[0], obs_count)
    inner = lax.ppermute(here, "space", swap[0])
    outer = lax.ppermute(here, "space", swap[1])
    late, above, below, reach = pack(core, tile, radius, fields, parts, EARLY, inner, here, outer)
    late = late.reshape((SIDE, SIDE) + late.shape[1:])
    late, early = lax.optimization_barrier((late, early))
    late = lax.all_to_all(late, both, 0, 0, axis_index_groups=groups[0])
    pieces = merge(early, late)
    pieces = lax.all_to_all(pieces, both, 0, 0, axis_index_groups=groups[1])
    pieces = pieces.reshape((parts,) + pieces.shape[2:])
    mixed = analyse(tile, core, reach, pieces, above, here, below, kinds)
    out = join(lax.all_to_all(mixed, "member", 0, 0), fields.shape)
    return out.reshape(own, kinds, 1, levels, width).transpose(0, 3, 1, 2, 4)


def solution(mesh):
    return jax.shard_map(
        on_device,
        mesh=mesh,
        in_specs=(
            P("member", None, None, "space", None),
            P("space", None, None),
            P("space", None, None),
            P("space", None, None),
            P("space", None),
            P("space", None),
        ),
        out_specs=P("member", None, None, "space", None),
        check_vma=False,
    )
```

```python
import functools

import jax
import jax.numpy as jnp
from jax import lax
from jax.experimental import pallas as pl
from jax.experimental.pallas import tpu as pltpu
from jax.sharding import PartitionSpec as P

TILE_SIDE = 32
TILE_CELLS = 1024
SWEEPS = 6


LANES = 128
VMEM = pl.BlockSpec(memory_space=pltpu.VMEM)
SMEM = pl.BlockSpec(memory_space=pltpu.SMEM)
HBM = pl.BlockSpec(memory_space=pltpu.HBM)
ANY = pl.BlockSpec(memory_space=pl.ANY)
PARAMS = pltpu.CompilerParams(vmem_limit_bytes=16 * 1024 * 1024)
EARLY = 3
SIDE = 4


def turned(core, index):
    return jnp.where(core == 0, index % SIDE * SIDE + index // SIDE, index)


def split_kernel(core_ref, x_ref, out_ref, held, made, in_sems, out_sems):
    kinds, own = held.shape[:2]
    width = held.shape[3]
    blocks = width // LANES
    parts, step = made.shape[1:3]
    per = blocks // parts
    loads = [
        pltpu.make_async_copy(x_ref.at[:, f], held.at[f], in_sems.at[f]) for f in range(kinds)
    ]
    stores = [
        pltpu.make_async_copy(
            made.at[f], out_ref.at[:, pl.ds(f * step, step)], out_sems.at[f]
        )
        for f in range(kinds)
    ]
    for load in loads:
        load.start()
    places = [turned(1 - core_ref[0], d) for d in range(parts)]
    for f in range(kinds):
        loads[f].wait()
        for c in range(blocks):
            for m in range(own):
                made[f, places[c // per], c % per * own + m] = held[
                    f, m, :, c * LANES : (c + 1) * LANES
                ]
        stores[f].start()
    for store in stores:
        store.wait()


def join_kernel(x_ref, out_ref, made, out_sems):
    kinds, own = made.shape[:2]
    width = made.shape[3]
    blocks = width // LANES
    per = blocks // x_ref.shape[0]
    stores = [
        pltpu.make_async_copy(made.at[f], out_ref.at[:, f], out_sems.at[f])
        for f in range(kinds)
    ]
    for f in range(kinds):
        for c in range(blocks):
            for m in range(own):
                made[f, m, :, c * LANES : (c + 1) * LANES] = x_ref[
                    c // per, (f * per + c % per) * own + m
                ]
        stores[f].start()
    for store in stores:
        store.wait()


def observe_kernel(
    x_ref,
    value_ref,
    precision_ref,
    cell_ref,
    count_ref,
    tile_ref,
    radius_ref,
    out_ref,
    reach_ref,
):
    reach_ref[...] = jnp.full(reach_ref.shape, radius_ref[0, tile_ref[0]], jnp.float32)
    own, kinds, levels, width = x_ref.shape
    tiles, slots = cell_ref.shape
    cells = width // tiles
    cell = cell_ref[...]
    in_tile = cell % cells
    level_field = cell // cells
    wanted = (level_field % kinds) * levels + level_field // kinds
    row_place = (in_tile // TILE_SIDE).astype(jnp.float32)
    col_place = (in_tile % TILE_SIDE).astype(jnp.float32)
    place_id = lax.broadcasted_iota(jnp.int32, (cells, slots), 0)
    field_id = lax.broadcasted_iota(jnp.int32, (kinds * levels, slots), 0)
    slot_id = lax.broadcasted_iota(jnp.int32, (1, slots), 1)
    for tile in range(tiles):
        at = slice(tile, tile + 1)
        onehot = (place_id == in_tile[at]).astype(x_ref.dtype)
        rows = x_ref[:, :, :, tile * cells : (tile + 1) * cells].reshape(-1, cells)
        found = jnp.dot(rows, onehot, preferred_element_type=jnp.float32)
        found = found.reshape(own, kinds * levels, slots)
        match = field_id == wanted[at]
        out_ref[tile, 0:own, :] = jnp.sum(jnp.where(match[None], found, 0.0), axis=1)
        out_ref[tile, own : own + 1, :] = value_ref[at, :]
        out_ref[tile, own + 1 : own + 2, :] = jnp.where(
            slot_id < count_ref[0, tile], precision_ref[at, :], 0.0
        )
        out_ref[tile, own + 2 : own + 3, :] = row_place[at]
        out_ref[tile, own + 3 : own + 4, :] = col_place[at]


def pack_kernel(
    begin,
    core_ref,
    x_ref,
    inner_ref,
    own_ref,
    outer_ref,
    out_ref,
    above_ref,
    below_ref,
):
    odd = core_ref[0] == 1
    places = [turned(1 - core_ref[0], d) for d in range(out_ref.shape[0])]
    inner, outer = inner_ref[...], outer_ref[...]
    above_ref[...] = jnp.where(odd, inner, outer)
    below_ref[...] = jnp.where(odd, outer, inner)
    parts, blocks, own, slots = out_ref.shape
    lane_blocks = x_ref.shape[3] // LANES
    per = lane_blocks // parts

    def copy_field(f, carry):
        for c in range(lane_blocks):
            for m in range(own):
                out_ref[places[c // per], ((f - begin) * per + c % per) * own + m] = x_ref[
                    m, f, :, c * LANES : (c + 1) * LANES
                ]
        return carry

    lax.fori_loop(begin, x_ref.shape[1], copy_field, 0, unroll=True)
    first = blocks - 9
    tiles = own_ref.shape[0]
    share = parts // tiles
    for a, rows_ref in enumerate((above_ref, own_ref, below_ref)):
        for t in range(tiles):
            rows = rows_ref[t, 0:own, :].astype(out_ref.dtype)
            for b in range(3):
                for h in range(share):
                    place = t + 1 - b
                    if 0 <= place < tiles:
                        out_ref[places[place * share + h], first + a * 3 + b] = rows
    blank = jnp.zeros((own, slots), out_ref.dtype)
    for h in range(share):
        for a in range(3):
            out_ref[places[h], first + a * 3] = blank
            out_ref[places[(tiles - 1) * share + h], first + a * 3 + 2] = blank


def two_terms(array):
    high = array.astype(jnp.bfloat16)
    return high, (array - high.astype(jnp.float32)).astype(jnp.bfloat16)


def gram(left, right):
    def product(a, b):
        return lax.dot_general(
            a, b, (((1,), (1,)), ((), ())), preferred_element_type=jnp.float32
        )

    count = left[0].shape[0]
    both = product(jnp.concatenate(left, axis=0), right[0])
    return both[:count] + both[count:] + product(left[0], right[1])


def doubled_product(left, right):
    return jnp.dot(
        jnp.concatenate(left, axis=1),
        jnp.concatenate(right + right, axis=0),
        preferred_element_type=jnp.float32,
    )


def analyse_kernel(
    kinds, tile_ref, core_ref, reach_ref, x_ref, above_ref, own_ref, below_ref, out_ref, mix_ref
):
    tile = tile_ref[0]
    tiles = own_ref.shape[0]
    sources, _, levels, slots = x_ref.shape
    own = own_ref.shape[1] - 4
    first = x_ref.shape[1] - 9
    members = sources * own
    reach = reach_ref[0:1, :]
    centre = 0.5 * TILE_SIDE - 0.5
    ensemble, values, weights = [], [], []
    for a, rows_ref in enumerate((above_ref, own_ref, below_ref)):
        for b in range(3):
            place = tile + b - 1
            inside = jnp.logical_and(place >= 0, place < tiles)
            held = jnp.clip(place, 0, tiles - 1)
            value, active, row, col = (
                rows_ref[held, own + i : own + i + 1, :] for i in range(4)
            )
            dist_row = row + ((a - 1) * TILE_SIDE - centre)
            dist_col = col + ((b - 1) * TILE_SIDE - centre)
            taper = jnp.maximum(
                1.0 - (dist_row * dist_row + dist_col * dist_col) / (reach * reach), 0.0
            )
            weights.append(jnp.where(inside, active, 0.0) * (taper * taper))
            values.append(value)
            ensemble.append(
                x_ref[:, first + a * 3 + b].astype(jnp.float32).reshape(members, slots)
            )
    ensemble = jnp.concatenate(ensemble, axis=1)
    values = jnp.concatenate(values, axis=1)
    weight = jnp.concatenate(weights, axis=1)
    mean_obs = jnp.mean(ensemble, axis=0, keepdims=True)
    anomaly = ensemble - mean_obs
    innovation = values - mean_obs
    scaled = anomaly * weight
    extended = jnp.concatenate(
        [anomaly, jnp.broadcast_to(innovation, (8, innovation.shape[1]))], axis=0
    )
    product = gram(two_terms(extended), two_terms(scaled))
    forcing = product[members : members + 1]
    row_id = lax.broadcasted_iota(jnp.int32, (members, 2 * members), 0)
    col_id = lax.broadcasted_iota(jnp.int32, (members, 2 * members), 1)
    identity = (row_id == col_id % members).astype(jnp.float32)
    system = (members - 1.0) * identity + jnp.concatenate([product[:members]] * 2, axis=1)
    scale = 0.5 * jnp.sum(
        jnp.sum(system * identity, axis=1, keepdims=True), axis=0, keepdims=True
    )
    root_part = system / scale
    factor = 1.5 * identity - 0.5 * root_part
    inverse = factor
    for sweep in range(1, SWEEPS):
        factor_terms = two_terms(factor)
        if sweep > 1:
            inverse = doubled_product(factor_terms, two_terms(inverse))
        root_part = doubled_product(two_terms(root_part), factor_terms)
        factor = 1.5 * identity - 0.5 * doubled_product(
            two_terms(inverse), two_terms(root_part)
        )
    inverse = doubled_product(two_terms(factor), two_terms(inverse))
    inv_sqrt = inverse[:, :members] / jnp.sqrt(scale)
    half = jnp.sum(inv_sqrt * forcing, axis=1, keepdims=True)
    mean_weight = jnp.sum(inv_sqrt * half, axis=0, keepdims=True)
    total = jnp.sqrt(jnp.float32(members - 1)) * inv_sqrt + mean_weight
    mixing = total - jnp.mean(total, axis=1, keepdims=True) + 1.0 / members
    mixing = mixing.astype(jnp.bfloat16)
    wide = members * levels
    spread = (
        lax.broadcasted_iota(jnp.int32, (wide, members), 0) // levels
        == lax.broadcasted_iota(jnp.int32, (wide, members), 1)
    ).astype(jnp.bfloat16)
    device = lax.broadcasted_iota(jnp.int32, (wide, members), 0) // (own * levels)
    row_member = turned(core_ref[0], device) * own + (
        lax.broadcasted_iota(jnp.int32, (wide, members), 0) // levels % own
    )
    chosen = (
        row_member == lax.broadcasted_iota(jnp.int32, (wide, members), 1)
    ).astype(jnp.bfloat16)
    tall = jnp.dot(chosen, mixing, preferred_element_type=jnp.float32).astype(jnp.bfloat16)
    full = lax.dot_general(
        tall, spread, (((1,), (1,)), ((), ())), preferred_element_type=jnp.float32
    )
    same = (
        lax.broadcasted_iota(jnp.int32, (wide, wide), 0) % levels
        == lax.broadcasted_iota(jnp.int32, (wide, wide), 1) % levels
    )
    mix_ref[...] = jnp.where(same, full, 0.0).astype(mix_ref.dtype)
    per = out_ref.shape[1] // (kinds * own)

    def body(f, carry):
        begin = f * per * own
        rows = jnp.concatenate(
            [x_ref[:, pl.ds(begin + c * own, own)].reshape(wide, LANES) for c in range(per)],
            axis=1,
        )
        mixed = jnp.dot(mix_ref[...], rows, preferred_element_type=jnp.float32)
        mixed = mixed.astype(out_ref.dtype)
        for c in range(per):
            out_ref[:, pl.ds(begin + c * own, own)] = mixed[
                :, c * LANES : (c + 1) * LANES
            ].reshape(sources, own, levels, LANES)
        return carry

    lax.fori_loop(0, kinds, body, 0, unroll=True)


def observe(fields, values, precision, cells, count, tile, radius):
    own = fields.shape[0]
    tiles, slots = cells.shape
    return pl.pallas_call(
        observe_kernel,
        in_specs=[VMEM] * 4 + [SMEM] * 3,
        out_specs=[VMEM] * 2,
        out_shape=[
            jax.ShapeDtypeStruct((tiles, own + 4, slots), jnp.float32),
            jax.ShapeDtypeStruct((8, LANES), jnp.float32),
        ],
        compiler_params=PARAMS,
        name="observe",
    )(fields, values, precision, cells, count, tile, radius)


def split(core, fields, parts, end):
    own, kinds, levels, width = fields.shape
    step = own * (width // parts // LANES)
    return pl.pallas_call(
        split_kernel,
        in_specs=[SMEM, HBM],
        out_specs=HBM,
        out_shape=jax.ShapeDtypeStruct((parts, end * step, levels, LANES), fields.dtype),
        scratch_shapes=[
            pltpu.VMEM((end, own, levels, width), fields.dtype),
            pltpu.VMEM((end, parts, step, levels, LANES), fields.dtype),
            pltpu.SemaphoreType.DMA((end,)),
            pltpu.SemaphoreType.DMA((end,)),
        ],
        name="split",
    )(core, fields)


def join(pieces, shape):
    own, kinds, levels, width = shape
    return pl.pallas_call(
        join_kernel,
        in_specs=[VMEM],
        out_specs=HBM,
        out_shape=jax.ShapeDtypeStruct(shape, pieces.dtype),
        scratch_shapes=[
            pltpu.VMEM((kinds, own, levels, width), pieces.dtype),
            pltpu.SemaphoreType.DMA((kinds,)),
        ],
        compiler_params=PARAMS,
        name="join",
    )(pieces)


def pack(core, fields, parts, begin, inner, here, outer):
    own, kinds, levels, width = fields.shape
    blocks = own * (kinds - begin) * (width // parts // LANES) + 9
    small = jax.ShapeDtypeStruct(here.shape, here.dtype)
    return pl.pallas_call(
        functools.partial(pack_kernel, begin),
        in_specs=[SMEM] + [VMEM] * 4,
        out_specs=[VMEM] * 3,
        out_shape=[
            jax.ShapeDtypeStruct((parts, blocks, levels, LANES), fields.dtype),
            small,
            small,
        ],
        compiler_params=PARAMS,
        name="pack",
    )(core, fields, inner, here, outer)


def analyse(tile, core, reach, pieces, above, here, below, kinds):
    parts, blocks, levels, lanes = pieces.shape
    wide = parts * (here.shape[1] - 4) * levels
    return pl.pallas_call(
        functools.partial(analyse_kernel, kinds),
        in_specs=[SMEM] * 2 + [VMEM] * 5,
        out_specs=VMEM,
        out_shape=jax.ShapeDtypeStruct((parts, blocks - 9, levels, lanes), pieces.dtype),
        scratch_shapes=[pltpu.VMEM((wide, wide), jnp.bfloat16)],
        compiler_params=PARAMS,
        name="analyse",
    )(tile, core, reach, pieces, above, here, below)


def merge_kernel(early_ref, late_ref, out_ref, sems):
    ahead, rest = early_ref.shape[2], late_ref.shape[2]
    copies = []
    for j in range(SIDE):
        copies.append(
            pltpu.make_async_copy(
                early_ref.at[:, j], out_ref.at[j, :, pl.ds(0, ahead)], sems.at[0, j]
            )
        )
        copies.append(
            pltpu.make_async_copy(
                late_ref.at[:, j], out_ref.at[j, :, pl.ds(ahead, rest)], sems.at[1, j]
            )
        )
    for copy in copies:
        copy.start()
    for copy in copies:
        copy.wait()


def merge(early, late):
    shape = early.shape[:2] + (early.shape[2] + late.shape[2],) + early.shape[3:]
    return pl.pallas_call(
        merge_kernel,
        in_specs=[ANY, ANY],
        out_specs=ANY,
        out_shape=jax.ShapeDtypeStruct(shape, early.dtype),
        scratch_shapes=[pltpu.SemaphoreType.DMA((2, SIDE))],
        compiler_params=PARAMS,
        name="merge",
    )(early, late)


def hop_groups(rows):
    def group(row, fixed, along_y):
        members = [
            i * SIDE + fixed if along_y else fixed * SIDE + i for i in range(SIDE)
        ]
        return [member * rows + row for member in members]

    return [
        [group(r, i, r % 2 == hop) for r in range(rows) for i in range(SIDE)]
        for hop in range(2)
    ]


def on_device(background, obs_values, obs_precision, obs_cell, obs_count, radius):
    own, levels, kinds, _, width = background.shape
    parts = lax.axis_size("member")
    rows = lax.axis_size("space")
    share = parts * TILE_CELLS // width
    pairs = [(i, i + 1) for i in range(rows - 1)]
    swap = [pairs[0::2], pairs[1::2]]
    swap = [one + [(j, i) for i, j in one] for one in swap]
    fields = background.transpose(0, 2, 3, 1, 4).reshape(own, kinds, levels, width)
    both = ("member", "space")
    groups = hop_groups(rows)
    core = (lax.axis_index("space") % 2).astype(jnp.int32).reshape(1)
    tile = (lax.axis_index("member") // share).astype(jnp.int32).reshape(1)
    early = split(core, fields, parts, EARLY)
    early, fields = lax.optimization_barrier((early, fields))
    early = early.reshape((SIDE, SIDE) + early.shape[1:])
    early = lax.all_to_all(early, both, 0, 0, axis_index_groups=groups[0])
    here, reach = observe(
        fields, obs_values[0], obs_precision[0], obs_cell[0], obs_count, tile, radius
    )
    inner = lax.ppermute(here, "space", swap[0])
    outer = lax.ppermute(here, "space", swap[1])
    late, above, below = pack(core, fields, parts, EARLY, inner, here, outer)
    late = late.reshape((SIDE, SIDE) + late.shape[1:])
    late, early = lax.optimization_barrier((late, early))
    late = lax.all_to_all(late, both, 0, 0, axis_index_groups=groups[0])
    pieces = merge(early, late)
    pieces = lax.all_to_all(pieces, both, 0, 0, axis_index_groups=groups[1])
    pieces = pieces.reshape((parts,) + pieces.shape[2:])
    mixed = analyse(tile, core, reach, pieces, above, here, below, kinds)
    out = join(lax.all_to_all(mixed, "member", 0, 0), fields.shape)
    return out.reshape(own, kinds, 1, levels, width).transpose(0, 3, 1, 2, 4)


def solution(mesh):
    return jax.shard_map(
        on_device,
        mesh=mesh,
        in_specs=(
            P("member", None, None, "space", None),
            P("space", None, None),
            P("space", None, None),
            P("space", None, None),
            P("space", None),
            P("space", None),
        ),
        out_specs=P("member", None, None, "space", None),
        check_vma=False,
    )
```

```python
import functools

import jax
import jax.numpy as jnp
from jax import lax
from jax.experimental import pallas as pl
from jax.experimental.pallas import tpu as pltpu
from jax.sharding import PartitionSpec as P

TILE_SIDE = 32
TILE_CELLS = 1024
SWEEPS = 6


LANES = 128
VMEM = pl.BlockSpec(memory_space=pltpu.VMEM)
SMEM = pl.BlockSpec(memory_space=pltpu.SMEM)
HBM = pl.BlockSpec(memory_space=pltpu.HBM)
ANY = pl.BlockSpec(memory_space=pl.ANY)
PARAMS = pltpu.CompilerParams(vmem_limit_bytes=16 * 1024 * 1024)
EARLY = 3
SIDE = 4


def turned(core, index):
    return jnp.where(core == 0, index % SIDE * SIDE + index // SIDE, index)


def split_kernel(core_ref, x_ref, out_ref, held, made, in_sems, out_sems):
    kinds, own = held.shape[:2]
    width = held.shape[3]
    blocks = width // LANES
    parts, step = made.shape[1:3]
    per = blocks // parts
    loads = [
        pltpu.make_async_copy(x_ref.at[:, f], held.at[f], in_sems.at[f]) for f in range(kinds)
    ]
    stores = [
        pltpu.make_async_copy(
            made.at[f], out_ref.at[:, pl.ds(f * step, step)], out_sems.at[f]
        )
        for f in range(kinds)
    ]
    for load in loads:
        load.start()
    places = [turned(1 - core_ref[0], d) for d in range(parts)]
    for f in range(kinds):
        loads[f].wait()
        for c in range(blocks):
            for m in range(own):
                made[f, places[c // per], c % per * own + m] = held[
                    f, m, :, c * LANES : (c + 1) * LANES
                ]
        stores[f].start()
    for store in stores:
        store.wait()


def join_kernel(x_ref, out_ref, made, out_sems):
    kinds, own = made.shape[:2]
    width = made.shape[3]
    blocks = width // LANES
    per = blocks // x_ref.shape[0]
    stores = [
        pltpu.make_async_copy(made.at[f], out_ref.at[:, f], out_sems.at[f])
        for f in range(kinds)
    ]
    for f in range(kinds):
        for c in range(blocks):
            for m in range(own):
                made[f, m, :, c * LANES : (c + 1) * LANES] = x_ref[
                    c // per, (f * per + c % per) * own + m
                ]
        stores[f].start()
    for store in stores:
        store.wait()


def observe_kernel(
    x_ref,
    value_ref,
    precision_ref,
    cell_ref,
    count_ref,
    tile_ref,
    radius_ref,
    out_ref,
    reach_ref,
):
    reach_ref[...] = jnp.full(reach_ref.shape, radius_ref[0, tile_ref[0]], jnp.float32)
    own, kinds, levels, width = x_ref.shape
    tiles, slots = cell_ref.shape
    cells = width // tiles
    cell = cell_ref[...]
    in_tile = cell % cells
    level_field = cell // cells
    wanted = (level_field % kinds) * levels + level_field // kinds
    row_place = (in_tile // TILE_SIDE).astype(jnp.float32)
    col_place = (in_tile % TILE_SIDE).astype(jnp.float32)
    place_id = lax.broadcasted_iota(jnp.int32, (cells, slots), 0)
    field_id = lax.broadcasted_iota(jnp.int32, (kinds * levels, slots), 0)
    slot_id = lax.broadcasted_iota(jnp.int32, (1, slots), 1)
    for tile in range(tiles):
        at = slice(tile, tile + 1)
        onehot = (place_id == in_tile[at]).astype(x_ref.dtype)
        rows = x_ref[:, :, :, tile * cells : (tile + 1) * cells].reshape(-1, cells)
        found = jnp.dot(rows, onehot, preferred_element_type=jnp.float32)
        found = found.reshape(own, kinds * levels, slots)
        match = field_id == wanted[at]
        out_ref[tile, 0:own, :] = jnp.sum(jnp.where(match[None], found, 0.0), axis=1)
        out_ref[tile, own : own + 1, :] = value_ref[at, :]
        out_ref[tile, own + 1 : own + 2, :] = jnp.where(
            slot_id < count_ref[0, tile], precision_ref[at, :], 0.0
        )
        out_ref[tile, own + 2 : own + 3, :] = row_place[at]
        out_ref[tile, own + 3 : own + 4, :] = col_place[at]


def pack_kernel(
    begin,
    core_ref,
    x_ref,
    inner_ref,
    own_ref,
    outer_ref,
    out_ref,
    above_ref,
    below_ref,
):
    odd = core_ref[0] == 1
    places = [turned(1 - core_ref[0], d) for d in range(out_ref.shape[0])]
    inner, outer = inner_ref[...], outer_ref[...]
    above_ref[...] = jnp.where(odd, inner, outer)
    below_ref[...] = jnp.where(odd, outer, inner)
    parts, blocks, own, slots = out_ref.shape
    lane_blocks = x_ref.shape[3] // LANES
    per = lane_blocks // parts

    def copy_field(f, carry):
        for c in range(lane_blocks):
            for m in range(own):
                out_ref[places[c // per], ((f - begin) * per + c % per) * own + m] = x_ref[
                    m, f, :, c * LANES : (c + 1) * LANES
                ]
        return carry

    lax.fori_loop(begin, x_ref.shape[1], copy_field, 0, unroll=True)
    first = blocks - 9
    tiles = own_ref.shape[0]
    share = parts // tiles
    for a, rows_ref in enumerate((above_ref, own_ref, below_ref)):
        for t in range(tiles):
            rows = rows_ref[t, 0:own, :].astype(out_ref.dtype)
            for b in range(3):
                for h in range(share):
                    place = t + 1 - b
                    if 0 <= place < tiles:
                        out_ref[places[place * share + h], first + a * 3 + b] = rows
    blank = jnp.zeros((own, slots), out_ref.dtype)
    for h in range(share):
        for a in range(3):
            out_ref[places[h], first + a * 3] = blank
            out_ref[places[(tiles - 1) * share + h], first + a * 3 + 2] = blank


def two_terms(array):
    high = array.astype(jnp.bfloat16)
    return high, (array - high.astype(jnp.float32)).astype(jnp.bfloat16)


def gram(left, right):
    def product(a, b):
        return lax.dot_general(
            a, b, (((1,), (1,)), ((), ())), preferred_element_type=jnp.float32
        )

    count = left[0].shape[0]
    both = product(jnp.concatenate(left, axis=0), right[0])
    return both[:count] + both[count:] + product(left[0], right[1])


def doubled_product(left, right):
    return jnp.dot(
        jnp.concatenate(left, axis=1),
        jnp.concatenate(right + right, axis=0),
        preferred_element_type=jnp.float32,
    )


def analyse_kernel(
    kinds, where_ref, reach_ref, x_ref, above_ref, own_ref, below_ref, out_ref, mix_ref
):
    tile, core = where_ref[0] // 2, where_ref[0] % 2
    tiles = own_ref.shape[0]
    sources, _, levels, slots = x_ref.shape
    own = own_ref.shape[1] - 4
    first = x_ref.shape[1] - 9
    members = sources * own
    reach = reach_ref[0:1, :]
    centre = 0.5 * TILE_SIDE - 0.5
    ensemble, values, weights = [], [], []
    for a, rows_ref in enumerate((above_ref, own_ref, below_ref)):
        for b in range(3):
            place = tile + b - 1
            inside = jnp.logical_and(place >= 0, place < tiles)
            held = jnp.clip(place, 0, tiles - 1)
            value, active, row, col = (
                rows_ref[held, own + i : own + i + 1, :] for i in range(4)
            )
            dist_row = row + ((a - 1) * TILE_SIDE - centre)
            dist_col = col + ((b - 1) * TILE_SIDE - centre)
            taper = jnp.maximum(
                1.0 - (dist_row * dist_row + dist_col * dist_col) / (reach * reach), 0.0
            )
            weights.append(jnp.where(inside, active, 0.0) * (taper * taper))
            values.append(value)
            ensemble.append(
                x_ref[:, first + a * 3 + b].astype(jnp.float32).reshape(members, slots)
            )
    ensemble = jnp.concatenate(ensemble, axis=1)
    values = jnp.concatenate(values, axis=1)
    weight = jnp.concatenate(weights, axis=1)
    mean_obs = jnp.mean(ensemble, axis=0, keepdims=True)
    anomaly = ensemble - mean_obs
    innovation = values - mean_obs
    scaled = anomaly * weight
    extended = jnp.concatenate(
        [anomaly, jnp.broadcast_to(innovation, (8, innovation.shape[1]))], axis=0
    )
    product = gram(two_terms(extended), two_terms(scaled))
    forcing = product[members : members + 1]
    row_id = lax.broadcasted_iota(jnp.int32, (members, 2 * members), 0)
    col_id = lax.broadcasted_iota(jnp.int32, (members, 2 * members), 1)
    identity = (row_id == col_id % members).astype(jnp.float32)
    system = (members - 1.0) * identity + jnp.concatenate([product[:members]] * 2, axis=1)
    scale = 0.5 * jnp.sum(
        jnp.sum(system * identity, axis=1, keepdims=True), axis=0, keepdims=True
    )
    root_part = system / scale
    factor = 1.5 * identity - 0.5 * root_part
    inverse = factor
    for sweep in range(1, SWEEPS):
        factor_terms = two_terms(factor)
        if sweep > 1:
            inverse = doubled_product(factor_terms, two_terms(inverse))
        root_part = doubled_product(two_terms(root_part), factor_terms)
        factor = 1.5 * identity - 0.5 * doubled_product(
            two_terms(inverse), two_terms(root_part)
        )
    inverse = doubled_product(two_terms(factor), two_terms(inverse))
    inv_sqrt = inverse[:, :members] / jnp.sqrt(scale)
    half = jnp.sum(inv_sqrt * forcing, axis=1, keepdims=True)
    mean_weight = jnp.sum(inv_sqrt * half, axis=0, keepdims=True)
    total = jnp.sqrt(jnp.float32(members - 1)) * inv_sqrt + mean_weight
    mixing = total - jnp.mean(total, axis=1, keepdims=True) + 1.0 / members
    mixing = mixing.astype(jnp.bfloat16)
    wide = members * levels
    spread = (
        lax.broadcasted_iota(jnp.int32, (wide, members), 0) // levels
        == lax.broadcasted_iota(jnp.int32, (wide, members), 1)
    ).astype(jnp.bfloat16)
    device = lax.broadcasted_iota(jnp.int32, (wide, members), 0) // (own * levels)
    row_member = turned(core, device) * own + (
        lax.broadcasted_iota(jnp.int32, (wide, members), 0) // levels % own
    )
    chosen = (
        row_member == lax.broadcasted_iota(jnp.int32, (wide, members), 1)
    ).astype(jnp.bfloat16)
    tall = jnp.dot(chosen, mixing, preferred_element_type=jnp.float32).astype(jnp.bfloat16)
    full = lax.dot_general(
        tall, spread, (((1,), (1,)), ((), ())), preferred_element_type=jnp.float32
    )
    same = (
        lax.broadcasted_iota(jnp.int32, (wide, wide), 0) % levels
        == lax.broadcasted_iota(jnp.int32, (wide, wide), 1) % levels
    )
    mix_ref[...] = jnp.where(same, full, 0.0).astype(mix_ref.dtype)
    per = out_ref.shape[1] // (kinds * own)

    def body(f, carry):
        begin = f * per * own
        rows = jnp.concatenate(
            [x_ref[:, pl.ds(begin + c * own, own)].reshape(wide, LANES) for c in range(per)],
            axis=1,
        )
        mixed = jnp.dot(mix_ref[...], rows, preferred_element_type=jnp.float32)
        mixed = mixed.astype(out_ref.dtype)
        for c in range(per):
            out_ref[:, pl.ds(begin + c * own, own)] = mixed[
                :, c * LANES : (c + 1) * LANES
            ].reshape(sources, own, levels, LANES)
        return carry

    lax.fori_loop(0, kinds, body, 0, unroll=True)


def observe(fields, values, precision, cells, count, tile, radius):
    own = fields.shape[0]
    tiles, slots = cells.shape
    return pl.pallas_call(
        observe_kernel,
        in_specs=[VMEM] * 4 + [SMEM] * 3,
        out_specs=[VMEM] * 2,
        out_shape=[
            jax.ShapeDtypeStruct((tiles, own + 4, slots), jnp.float32),
            jax.ShapeDtypeStruct((8, LANES), jnp.float32),
        ],
        compiler_params=PARAMS,
        name="observe",
    )(fields, values, precision, cells, count, tile, radius)


def split(core, fields, parts, end):
    own, kinds, levels, width = fields.shape
    step = own * (width // parts // LANES)
    return pl.pallas_call(
        split_kernel,
        in_specs=[SMEM, HBM],
        out_specs=HBM,
        out_shape=jax.ShapeDtypeStruct((parts, end * step, levels, LANES), fields.dtype),
        scratch_shapes=[
            pltpu.VMEM((end, own, levels, width), fields.dtype),
            pltpu.VMEM((end, parts, step, levels, LANES), fields.dtype),
            pltpu.SemaphoreType.DMA((end,)),
            pltpu.SemaphoreType.DMA((end,)),
        ],
        name="split",
    )(core, fields)


def join(pieces, shape):
    own, kinds, levels, width = shape
    return pl.pallas_call(
        join_kernel,
        in_specs=[VMEM],
        out_specs=HBM,
        out_shape=jax.ShapeDtypeStruct(shape, pieces.dtype),
        scratch_shapes=[
            pltpu.VMEM((kinds, own, levels, width), pieces.dtype),
            pltpu.SemaphoreType.DMA((kinds,)),
        ],
        compiler_params=PARAMS,
        name="join",
    )(pieces)


def pack(core, fields, parts, begin, inner, here, outer):
    own, kinds, levels, width = fields.shape
    blocks = own * (kinds - begin) * (width // parts // LANES) + 9
    small = jax.ShapeDtypeStruct(here.shape, here.dtype)
    return pl.pallas_call(
        functools.partial(pack_kernel, begin),
        in_specs=[SMEM] + [VMEM] * 4,
        out_specs=[VMEM] * 3,
        out_shape=[
            jax.ShapeDtypeStruct((parts, blocks, levels, LANES), fields.dtype),
            small,
            small,
        ],
        compiler_params=PARAMS,
        name="pack",
    )(core, fields, inner, here, outer)


def analyse(where, reach, pieces, above, here, below, kinds):
    parts, blocks, levels, lanes = pieces.shape
    wide = parts * (here.shape[1] - 4) * levels
    return pl.pallas_call(
        functools.partial(analyse_kernel, kinds),
        in_specs=[SMEM] + [VMEM] * 5,
        out_specs=VMEM,
        out_shape=jax.ShapeDtypeStruct((parts, blocks - 9, levels, lanes), pieces.dtype),
        scratch_shapes=[pltpu.VMEM((wide, wide), jnp.bfloat16)],
        compiler_params=PARAMS,
        name="analyse",
    )(where, reach, pieces, above, here, below)


def merge_kernel(early_ref, late_ref, out_ref, sems):
    ahead, rest = early_ref.shape[2], late_ref.shape[2]
    copies = []
    for j in range(SIDE):
        copies.append(
            pltpu.make_async_copy(
                early_ref.at[:, j], out_ref.at[j, :, pl.ds(0, ahead)], sems.at[0, j]
            )
        )
        copies.append(
            pltpu.make_async_copy(
                late_ref.at[:, j], out_ref.at[j, :, pl.ds(ahead, rest)], sems.at[1, j]
            )
        )
    for copy in copies:
        copy.start()
    for copy in copies:
        copy.wait()


def merge(early, late):
    shape = early.shape[:2] + (early.shape[2] + late.shape[2],) + early.shape[3:]
    return pl.pallas_call(
        merge_kernel,
        in_specs=[ANY, ANY],
        out_specs=ANY,
        out_shape=jax.ShapeDtypeStruct(shape, early.dtype),
        scratch_shapes=[pltpu.SemaphoreType.DMA((2, SIDE))],
        compiler_params=PARAMS,
        name="merge",
    )(early, late)


def hop_groups(rows):
    def group(row, fixed, along_y):
        members = [
            i * SIDE + fixed if along_y else fixed * SIDE + i for i in range(SIDE)
        ]
        return [member * rows + row for member in members]

    return [
        [group(r, i, r % 2 == hop) for r in range(rows) for i in range(SIDE)]
        for hop in range(2)
    ]


def on_device(background, obs_values, obs_precision, obs_cell, obs_count, radius):
    own, levels, kinds, _, width = background.shape
    parts = lax.axis_size("member")
    rows = lax.axis_size("space")
    share = parts * TILE_CELLS // width
    pairs = [(i, i + 1) for i in range(rows - 1)]
    swap = [pairs[0::2], pairs[1::2]]
    swap = [one + [(j, i) for i, j in one] for one in swap]
    fields = background.transpose(0, 2, 3, 1, 4).reshape(own, kinds, levels, width)
    both = ("member", "space")
    groups = hop_groups(rows)
    core = (lax.axis_index("space") % 2).astype(jnp.int32).reshape(1)
    tile = (lax.axis_index("member") // share).astype(jnp.int32).reshape(1)
    early = split(core, fields, parts, EARLY)
    early, fields = lax.optimization_barrier((early, fields))
    early = early.reshape((SIDE, SIDE) + early.shape[1:])
    early = lax.all_to_all(early, both, 0, 0, axis_index_groups=groups[0])
    here, reach = observe(
        fields, obs_values[0], obs_precision[0], obs_cell[0], obs_count, tile, radius
    )
    inner = lax.ppermute(here, "space", swap[0])
    outer = lax.ppermute(here, "space", swap[1])
    late, above, below = pack(core, fields, parts, EARLY, inner, here, outer)
    late = late.reshape((SIDE, SIDE) + late.shape[1:])
    late, early = lax.optimization_barrier((late, early))
    late = lax.all_to_all(late, both, 0, 0, axis_index_groups=groups[0])
    pieces = merge(early, late)
    pieces = lax.all_to_all(pieces, both, 0, 0, axis_index_groups=groups[1])
    pieces = pieces.reshape((parts,) + pieces.shape[2:])
    mixed = analyse(tile * 2 + core, reach, pieces, above, here, below, kinds)
    out = join(lax.all_to_all(mixed, "member", 0, 0), fields.shape)
    return out.reshape(own, kinds, 1, levels, width).transpose(0, 3, 1, 2, 4)


def solution(mesh):
    return jax.shard_map(
        on_device,
        mesh=mesh,
        in_specs=(
            P("member", None, None, "space", None),
            P("space", None, None),
            P("space", None, None),
            P("space", None, None),
            P("space", None),
            P("space", None),
        ),
        out_specs=P("member", None, None, "space", None),
        check_vma=False,
    )
```
